32 devices in a mesh: dp: 4 (over z), fsdp: 8 (over y, x, core).
Axes of the slice: x: 2, y: 2, z: 4, core: 2. Of those that a mesh axis runs over, the one named last changes fastest.
Arguments:
- tokens: bfloat16 [32768, 768], P(('dp', 'fsdp')), may hold values from -6 to 6
- block_bucket: int32 [512], P(('dp', 'fsdp')), may hold values from 64 to 512, as said below
- lengths: int32 [512], P(('dp', 'fsdp')), may hold values from 0 to 512, as said below
- query_weight: bfloat16 [768, 768], P(('dp', 'fsdp')), may hold values from -0.3125 to 0.3125
- query_bias: bfloat16 [768], P(('dp', 'fsdp')), may hold values from -1 to 1
- key_weight: bfloat16 [768, 768], P(('dp', 'fsdp')), may hold values from -0.3125 to 0.3125
- value_weight: bfloat16 [768, 768], P(('dp', 'fsdp')), may hold values from -0.21875 to 0.21875
- value_bias: bfloat16 [768], P(('dp', 'fsdp')), may hold values from -1 to 1
- out_weight: bfloat16 [768, 768], P(('dp', 'fsdp')), may hold values from -0.875 to 0.875
- out_bias: bfloat16 [768], P(('dp', 'fsdp')), may hold values from -1 to 1
- first_gain: bfloat16 [768], P(('dp', 'fsdp')), may hold values from 0.5 to 1.5
- first_shift: bfloat16 [768], P(('dp', 'fsdp')), may hold values from -1 to 1
- up_weight: bfloat16 [768, 3072], P(('dp', 'fsdp')), may hold values from -0.21875 to 0.21875
- up_bias: bfloat16 [3072], P(('dp', 'fsdp')), may hold values from -1 to 1
- down_weight: bfloat16 [3072, 768], P(('dp', 'fsdp')), may hold values from -0.109375 to 0.109375
- down_bias: bfloat16 [768], P(('dp', 'fsdp')), may hold values from -1 to 1
- second_gain: bfloat16 [768], P(('dp', 'fsdp')), may hold values from 0.5 to 1.5
- second_shift: bfloat16 [768], P(('dp', 'fsdp')), may hold values from -1 to 1
- out_grad: bfloat16 [32768, 768], P(('dp', 'fsdp')), may hold values from -6 to 6
- pool_grad: float32 [512, 1728], P(('dp', 'fsdp')), may hold values from -6 to 6
Outputs:
- layer_out: bfloat16 [32768, 768], P(('dp', 'fsdp'))
- pools: float32 [512, 1728], P(('dp', 'fsdp'))
- token_grad: float32 [32768, 768], P(('dp', 'fsdp'))
- grad_query_weight: float32 [768, 768], P(('dp', 'fsdp'))
- grad_query_bias: float32 [768], P(('dp', 'fsdp'))
- grad_key_weight: float32 [768, 768], P(('dp', 'fsdp'))
- grad_value_weight: float32 [768, 768], P(('dp', 'fsdp'))
- grad_value_bias: float32 [768], P(('dp', 'fsdp'))
- grad_out_weight: float32 [768, 768], P(('dp', 'fsdp'))
- grad_out_bias: float32 [768], P(('dp', 'fsdp'))
- grad_first_gain: float32 [768], P(('dp', 'fsdp'))
- grad_first_shift: float32 [768], P(('dp', 'fsdp'))
- grad_up_weight: float32 [768, 3072], P(('dp', 'fsdp'))
- grad_up_bias: float32 [3072], P(('dp', 'fsdp'))
- grad_down_weight: float32 [3072, 768], P(('dp', 'fsdp'))
- grad_down_bias: float32 [768], P(('dp', 'fsdp'))
- grad_second_gain: float32 [768], P(('dp', 'fsdp'))
- grad_second_shift: float32 [768], P(('dp', 'fsdp'))
The draws below stay inside these ranges and needn't reach their ends.
Inputs may be any that keep to these rules, and one draw needn't show every extreme that they name: `block_bucket`: each row of 512 tokens is cut into buckets of 64 times a power of two tokens, each aligned to its size; every block gives the size of its bucket. `lengths`: at the first block of a bucket the length of its sentence, from 8 to the bucket's size and over half of it in buckets larger than 64; 0 at the other blocks; the first sentence has 512 tokens.
All inputs are finite; a program needn't handle non-finite values.
Results may differ from the reference program's by a relative error of at most 0.014.
The reference program's roundings to bfloat16 on the way count: a program that leaves them out, or rounds other values in their place, can miss the bound.
Values may be sent and summed in bfloat16 or wider, within the bound.
A program may use at most 192 MiB of HBM per device.

```python
import jax
import jax.numpy as jnp
from jax import lax

D = 768
HEADS = 12
HD = 64
FF = 3072
ROW = 512
BLOCK = 64
TOKENS = 32768
NBLOCKS = 512
POOLW = 1728


def bucket_layout(key):
    row_total = TOKENS // ROW
    per_row = ROW // BLOCK
    row_index = jnp.arange(row_total, dtype=jnp.int32)
    bucket = jnp.full((row_total, per_row), ROW, jnp.int32)
    breadth = ROW
    depth_level = 0
    while breadth > BLOCK:
        node_count = ROW // breadth
        splits = jax.random.randint(jax.random.fold_in(key, 10 + depth_level), (row_total, node_count), 0, 5) < 3
        if depth_level == 0:
            splits = splits & (row_index != 0)[:, None]
        splits = jnp.repeat(splits, breadth // BLOCK, axis=1)
        bucket = jnp.where((bucket == breadth) & splits, breadth // 2, bucket)
        breadth = breadth // 2
        depth_level = depth_level + 1
    position = jnp.arange(per_row, dtype=jnp.int32)[None, :]
    opening = position * BLOCK % bucket == 0
    lowest = jnp.where(bucket == BLOCK, 8, bucket // 2 + 1)
    drawn_len = jax.random.randint(jax.random.fold_in(key, 20), (row_total, per_row), lowest, bucket + 1)
    first_cell = (row_index[:, None] == 0) & (position == 0)
    drawn_len = jnp.where(first_cell, ROW, drawn_len)
    return (bucket.reshape(-1), jnp.where(opening, drawn_len, 0).reshape(-1).astype(jnp.int32))


def draw_block_bucket(key, part):
    return bucket_layout(key)[0]


def draw_lengths(key, part):
    return bucket_layout(key)[1]


def steps_of(stream_key, dims, cuts, smallest, high):
    def one(dim, blocks):
        heights = jax.random.uniform(jax.random.fold_in(jax.random.fold_in(stream_key, 6), dim), (blocks,), jnp.float32, smallest / len(cuts), high / len(cuts))
        return jnp.repeat(jnp.exp(heights), dims[dim] // blocks).reshape((-1,) + (1,) * (len(dims) - dim - 1))

    level = one(*cuts[0])
    for cut in cuts[1:]:
        level = level * one(*cut)
    return level


def gaussian(rng, shape, scale, most, shards=(), held_as=jnp.bfloat16):
    values = scale * jax.random.normal(rng, shape, jnp.float32)
    if shards:
        values = values * steps_of(rng, shape, shards, -0.22, 0.18)
    return jnp.clip(values, -most, most).astype(held_as)


def setup_inputs(seed: int = 0) -> dict:
    key_of = jax.random.split(jax.random.key(seed), 21)
    return {
        "tokens": gaussian(key_of[0], (TOKENS, D), 1.0, 6.0, ((0, 32),)),
        "block_bucket": draw_block_bucket(jax.random.fold_in(key_of[20], 71), 0),
        "lengths": draw_lengths(jax.random.fold_in(key_of[20], 71), 0),
        "query_weight": gaussian(key_of[3], (D, D), (D // 2) ** -0.5, 0.3125, ((0, 32),)),
        "query_bias": gaussian(key_of[4], (D,), 0.2, 1.0, ((0, 32),)),
        "key_weight": gaussian(key_of[5], (D, D), (D // 2) ** -0.5, 0.3125, ((0, 32),)),
        "value_weight": gaussian(key_of[6], (D, D), D ** -0.5, 0.21875, ((0, 32),)),
        "value_bias": gaussian(key_of[7], (D,), 0.2, 1.0, ((0, 32),)),
        "out_weight": gaussian(key_of[8], (D, D), (D // 16) ** -0.5, 0.875, ((0, 32),)),
        "out_bias": gaussian(key_of[9], (D,), 0.2, 1.0, ((0, 32),)),
        "first_gain": jnp.clip(1.0 + 0.1 * jax.random.normal(key_of[10], (D,), jnp.float32), 0.5, 1.5).astype(jnp.bfloat16),
        "first_shift": gaussian(key_of[11], (D,), 0.2, 1.0, ((0, 32),)),
        "up_weight": gaussian(key_of[12], (D, FF), D ** -0.5, 0.21875, ((0, 32),)),
        "up_bias": gaussian(key_of[13], (FF,), 0.2, 1.0, ((0, 32),)),
        "down_weight": gaussian(key_of[14], (FF, D), FF ** -0.5, 0.109375, ((0, 32),)),
        "down_bias": gaussian(key_of[15], (D,), 0.2, 1.0, ((0, 32),)),
        "second_gain": jnp.clip(1.0 + 0.1 * jax.random.normal(key_of[16], (D,), jnp.float32), 0.5, 1.5).astype(jnp.bfloat16),
        "second_shift": gaussian(key_of[17], (D,), 0.2, 1.0, ((0, 32),)),
        "out_grad": gaussian(key_of[18], (TOKENS, D), 1.0, 6.0, ((0, 32),)),
        "pool_grad": gaussian(key_of[19], (NBLOCKS, POOLW), 1.0, 6.0, ((0, 32),), jnp.float32),
    }


@jax.custom_vjp
def low(v):
    return lax.optimization_barrier(v.astype(jnp.bfloat16)).astype(jnp.float32)

@jax.custom_vjp
def low_back(v):
    return v

def low_keep(v):
    return (low(v), None)

def low_pass(kept, grad):
    return (grad,)

def back_keep(v):
    return (v, None)

def back_low(kept, grad):
    return (low(grad),)
low.defvjp(low_keep, low_pass)
low_back.defvjp(back_keep, back_low)

def product(left, right):
    return jnp.dot(left, right, precision=lax.Precision.HIGHEST, preferred_element_type=jnp.float32)

def layer_norm(values, scales, offset):
    center = values - lax.optimization_barrier(jnp.mean(values, axis=-1, keepdims=True))
    spread = lax.optimization_barrier(jnp.mean(center * center, axis=-1, keepdims=True))
    return center * lax.rsqrt(spread + 1e-05) * scales + offset

def pool_breadths(model_width):
    return [model_width, 2 * model_width // 3, model_width // 3, model_width // 6, model_width // 12]

def matryoshka(averages, model_width):
    pieces = []
    for breadth in pool_breadths(model_width):
        leading = averages[:, :breadth]
        pieces.append(leading * lax.rsqrt(lax.optimization_barrier(jnp.mean(leading * leading, axis=-1, keepdims=True)) + 1e-06))
    return jnp.concatenate(pieces, axis=-1)

def sentence_layout(block_bucket, lengths, block_size):
    block_count = block_bucket.shape[0]
    blocks = jnp.arange(block_count, dtype=jnp.int32)
    stride = (block_bucket // block_size).astype(jnp.int32)
    start_block = (blocks // stride * stride).astype(jnp.int32)
    block_len = lax.optimization_barrier(jnp.sum(jnp.where(start_block[:, None] == blocks[None, :], lengths[None, :], 0), axis=1)).astype(jnp.int32)
    token_start = jnp.repeat(start_block * block_size, block_size).astype(jnp.int32)
    token_len = jnp.repeat(block_len, block_size).astype(jnp.int32)
    positions = jnp.arange(block_count * block_size, dtype=jnp.int32)
    valid = positions - token_start < token_len
    member = (token_start[None, :] == (start_block * block_size)[:, None]) & valid[None, :]
    pool_matrix = jnp.where(member, 1.0, 0.0).astype(jnp.float32) / block_len.astype(jnp.float32)[:, None]
    return (token_start, valid, pool_matrix)

def row_attention(items):
    query_rows, key_rows, value_rows, token_start, valid = items
    scores = low_back(jnp.einsum('qhd,khd->hqk', query_rows, key_rows, precision=lax.Precision.HIGHEST) * 0.125)
    allowed = (token_start[:, None] == token_start[None, :]) & valid[None, :]
    scores = jnp.where(allowed[None], scores, -1e+30)
    row_peak = lax.optimization_barrier(jnp.max(scores, axis=-1, keepdims=True))
    exponent = jnp.exp(scores - row_peak)
    softmax_out = low(exponent / lax.optimization_barrier(jnp.sum(exponent, axis=-1, keepdims=True)))
    return jnp.einsum('hqk,khd->qhd', softmax_out, value_rows, precision=lax.Precision.HIGHEST)

def encode_group(params, items):
    query_weight, query_bias, key_weight, value_weight, value_bias, out_weight, out_bias, first_gain, first_shift, up_weight, up_bias, down_weight, down_bias, second_gain, second_shift = params
    tokens_group, bucket_group, length_group = items
    group_rows = bucket_group.shape[0]
    queries = low_back(low(product(tokens_group, query_weight) + query_bias))
    keys_all = low_back(low(product(tokens_group, key_weight)))
    values_all = low_back(low(product(tokens_group, value_weight) + value_bias))
    token_start, valid, pool_matrix = jax.vmap(lambda bucket_row, length_row: sentence_layout(bucket_row, length_row, BLOCK))(bucket_group, length_group)

    def split_heads(array):
        return array.reshape(group_rows, ROW, HEADS, HD)
    context = lax.map(jax.checkpoint(row_attention), (split_heads(queries), split_heads(keys_all), split_heads(values_all), token_start, valid))
    context = low_back(low(context.reshape(group_rows * ROW, D)))
    attended = low_back(product(context, out_weight) + out_bias)
    hidden = low(layer_norm(tokens_group + attended, first_gain, first_shift))
    pre_gelu = low_back(product(hidden, up_weight) + up_bias)
    activated = low(jax.nn.gelu(pre_gelu, approximate=False))
    branch_out = low_back(product(activated, down_weight) + down_bias)
    outputs = layer_norm(hidden + branch_out, second_gain, second_shift)
    averages = jnp.einsum('gbt,gtd->gbd', pool_matrix, outputs.reshape(group_rows, ROW, D), precision=lax.Precision.HIGHEST)
    pools = matryoshka(averages.reshape(-1, D), D)
    return (outputs, pools)

def reference(tokens, block_bucket, lengths, query_weight, query_bias, key_weight, value_weight, value_bias, out_weight, out_bias, first_gain, first_shift, up_weight, up_bias, down_weight, down_bias, second_gain, second_shift, out_grad, pool_grad):
    group_rows = 8
    per_row = ROW // BLOCK
    bucket_groups = block_bucket.reshape(-1, group_rows, per_row)
    length_groups = lengths.reshape(-1, group_rows, per_row)

    def forward(token_values, *params):
        token_groups = token_values.reshape(-1, group_rows * ROW, D)
        outputs, pools = lax.map(jax.checkpoint(lambda items: encode_group(params, items)), (token_groups, bucket_groups, length_groups))
        return (outputs.reshape(-1, D), pools.reshape(-1, POOLW))
    floats = [a.astype(jnp.float32) for a in (tokens, query_weight, query_bias, key_weight, value_weight, value_bias, out_weight, out_bias, first_gain, first_shift, up_weight, up_bias, down_weight, down_bias, second_gain, second_shift)]
    (outputs, pools), pullback = jax.vjp(forward, *floats)
    grads = pullback((out_grad.astype(jnp.float32), pool_grad.astype(jnp.float32)))
    return (outputs.astype(jnp.bfloat16), pools, grads[0], grads[1], grads[2], grads[3], grads[4], grads[5], grads[6], grads[7], grads[8], grads[9], grads[10], grads[11], grads[12], grads[13], grads[14], grads[15])
```

```python
import functools
import math

import jax
import jax.numpy as jnp
from jax import lax
from jax.experimental import pallas as pl
from jax.experimental.pallas import tpu as pltpu
from jax.sharding import PartitionSpec as P

MESH = pl.DeviceIdType.MESH
D = 768
F32 = jnp.float32
BF16 = jnp.bfloat16


class Grid:
    def __init__(self, nz, nf):
        self.nz = nz
        self.side = math.isqrt(nf // 2)
        assert 2 * self.side * self.side == nf
        self.chips = nz * self.side * self.side
        self.rows = D // self.chips
        self.dev_rows = self.rows // 2
        self.pad = -(-self.rows // 16) * 16

    def place(self):
        s = self.side
        self.z = lax.axis_index("dp")
        f = lax.axis_index("fsdp")
        self.core = lax.rem(f, 2)
        self.lo = lax.rem(f // 2, s)
        self.hi = f // (2 * s)

    def dev(self, z, hi, lo, core):
        return (z, (hi * self.side + lo) * 2 + core)

    def sib(self):
        return self.dev(self.z, self.hi, self.lo, 1 - self.core)

    def zs(self, d):
        return lax.rem(self.z + d, self.nz)

    def los(self, d):
        return lax.rem(self.lo + d, self.side)

    def his(self, d):
        return lax.rem(self.hi + d, self.side)

    def z_peer(self, d):
        return self.dev(self.zs(d), self.hi, self.lo, self.core)

    def lo_peer(self, d):
        return self.dev(self.z, self.hi, self.los(d), self.core)

    def hi_peer(self, d):
        return self.dev(self.z, self.his(d), self.lo, self.core)

    def chip(self, z, hi, lo):
        return (z * self.side + hi) * self.side + lo

    def peers(self):
        out = [self.sib()]
        out += [self.z_peer(d) for d in range(1, self.nz)]
        out += [self.lo_peer(d) for d in range(1, self.side)]
        out += [self.hi_peer(d) for d in range(1, self.side)]
        return out

    def barrier(self):
        sem = pltpu.get_barrier_semaphore()
        peers = self.peers()
        for peer in peers:
            pl.semaphore_signal(sem, inc=1, device_id=peer, device_id_type=MESH)
        pl.semaphore_wait(sem, len(peers))


class Sender:
    def __init__(self, sems):
        self.sems = sems
        self.started = []

    def start(self, src, dst, recv_sem, device):
        copy = pltpu.make_async_remote_copy(
            src_ref=src,
            dst_ref=dst,
            send_sem=self.sems.at[len(self.started)],
            recv_sem=recv_sem,
            device_id=device,
            device_id_type=MESH,
        )
        copy.start()
        self.started.append(copy)
        return copy

    def arrived(self, dst, recv_sem, grid):
        pltpu.make_async_remote_copy(
            src_ref=dst,
            dst_ref=dst,
            send_sem=self.sems.at[0],
            recv_sem=recv_sem,
            device_id=grid.sib(),
            device_id_type=MESH,
        ).wait_recv()

    def finish(self):
        for copy in self.started:
            copy.wait_send()


class Gather:
    def __init__(self, grid, sender, at, sem, per_core=2):
        self.grid, self.sender, self.at, self.sem = grid, sender, at, sem
        self.per_core = per_core

    def mine(self, jj):
        return self.grid.core * self.per_core + jj

    def send(self, j, p, device):
        self.sender.start(self.at(j, p), self.at(j, p), self.sem(j, p), device)

    def wait(self, j, p):
        self.sender.arrived(self.at(j, p), self.sem(j, p), self.grid)

    def own(self):
        g = self.grid
        for jj in range(self.per_core):
            j, p = self.mine(jj), g.chip(g.z, g.hi, g.lo)
            for d in range(1, g.nz):
                self.send(j, p, g.z_peer(d))
            self.spread(j, p)

    def spread(self, j, p):
        g = self.grid
        for d in range(1, g.side):
            self.send(j, p, g.lo_peer(d))
        for d in range(1, g.side):
            self.send(j, p, g.hi_peer(d))
        self.send(j, p, g.sib())

    def along_z(self, d):
        g = self.grid
        for jj in range(self.per_core):
            j, p = self.mine(jj), g.chip(g.zs(d), g.hi, g.lo)
            self.wait(j, p)
            self.spread(j, p)

    def second(self, d):
        g = self.grid
        for jj in range(self.per_core):
            j = self.mine(jj)
            for e in range(1, g.side):
                if jj % 2 == 0:
                    p = g.chip(g.zs(d), g.hi, g.los(e))
                else:
                    p = g.chip(g.zs(d), g.his(e), g.lo)
                self.wait(j, p)
                for k in range(1, g.side):
                    self.send(j, p, g.hi_peer(k) if jj % 2 == 0 else g.lo_peer(k))
                self.send(j, p, g.sib())

    def third(self, d):
        g = self.grid
        for jj in range(self.per_core):
            j = self.mine(jj)
            for e in range(1, g.side):
                for k in range(g.side):
                    if jj % 2 == 0:
                        p = g.chip(g.zs(d), g.his(e), g.los(k))
                    else:
                        p = g.chip(g.zs(d), g.his(k), g.los(e))
                    self.wait(j, p)
                    self.send(j, p, g.sib())

    def sibling(self):
        g = self.grid
        for jj in range(self.per_core):
            j = (1 - g.core) * self.per_core + jj
            for d in range(g.nz):
                for e in range(g.side):
                    for k in range(g.side):
                        self.wait(j, g.chip(g.zs(d), g.his(e), g.los(k)))

    @staticmethod
    def sends(grid, per_core):
        n, s = grid.nz, grid.side
        return per_core * (n - 1 + n * (s - 1) + n * s * (s - 1) + grid.chips)


def join_rows(grid, low, high):
    parts = [low.astype(F32), high.astype(F32)]
    if grid.pad != grid.rows:
        parts.append(jnp.zeros((grid.pad - grid.rows, low.shape[1]), F32))
    return jnp.concatenate(parts, axis=0).astype(BF16)


def gather_kernel(grid, attn_ref, up_ref, down_ref, vec_ref, w_attn, w_up, w_down, w_vec,
                  pre_ref, pre_vec, stage, stage_vec, rsem, vsem, ssem, psem, lsem):
    grid.place()
    grid.barrier()
    sender = Sender(ssem)
    c = grid.core
    me = grid.chip(grid.z, grid.hi, grid.lo)
    raws = (attn_ref, up_ref)
    for g, raw in enumerate(raws):
        for jj in range(2):
            sender.start(raw.at[(1 - c) * 2 + jj], pre_ref.at[g, jj], psem.at[g, jj], grid.sib())
    sender.start(vec_ref.at[1 - c], pre_vec, psem.at[2, 0], grid.sib())

    groups = [
        Gather(grid, sender, lambda j, p: w_attn.at[j, p], lambda j, p: rsem.at[0, j, p]),
        Gather(grid, sender, lambda j, p: w_up.at[j, p], lambda j, p: rsem.at[1, j, p]),
        Gather(grid, sender, lambda j, p: w_down.at[p, j], lambda j, p: rsem.at[2, j, p]),
    ]
    vec = Gather(grid, sender, lambda j, p: w_vec.at[j, p], lambda j, p: vsem.at[j, p], per_core=1)

    def put(src, dst, k):
        copy = pltpu.make_async_copy(src, dst, lsem.at[k])
        copy.start()
        copy.wait()

    def assemble(g):
        for jj in range(2):
            if g < 2:
                sender.arrived(pre_ref.at[g, jj], psem.at[g, jj], grid)
                own, other = raws[g][c * 2 + jj], pre_ref[g, jj]
                first = jnp.where(c == 0, own.astype(F32), other.astype(F32))
                last = jnp.where(c == 0, other.astype(F32), own.astype(F32))
            else:
                first, last = down_ref[2 * jj], down_ref[2 * jj + 1]
            stage[jj] = join_rows(grid, first, last)
            put(stage.at[jj], groups[g].at(c * 2 + jj, me), 0)

    assemble(0)
    groups[0].own()
    sender.arrived(pre_vec, psem.at[2, 0], grid)
    stage_vec[...] = (vec_ref[c].astype(F32) + pre_vec[...].astype(F32)).astype(BF16)
    put(stage_vec, w_vec.at[c, me], 0)
    vec.own()
    def z_steps(g):
        for d in range(grid.nz - 1, 0, -1):
            g.along_z(d)

    def second_steps(g):
        for d in range(grid.nz, 0, -1):
            g.second(d)

    def third_steps(g):
        for d in range(grid.nz, 0, -1):
            g.third(d)

    z_steps(vec)
    z_steps(groups[0])
    assemble(1)
    groups[1].own()
    second_steps(vec)
    second_steps(groups[0])
    z_steps(groups[1])
    assemble(2)
    groups[2].own()
    third_steps(vec)
    third_steps(groups[0])
    second_steps(groups[1])
    z_steps(groups[2])
    third_steps(groups[1])
    second_steps(groups[2])
    third_steps(groups[2])
    for g in [vec] + groups:
        g.sibling()
    sender.finish()


def gather_all(grid, raw_attn, raw_up, raw_down, raw_vec):
    n, pad, dr = grid.chips, grid.pad, grid.dev_rows
    nsend = 5 + 3 * Gather.sends(grid, 2) + Gather.sends(grid, 1)
    any_spec = pl.BlockSpec(memory_space=pl.ANY)
    vmem = pl.BlockSpec(memory_space=pltpu.VMEM)
    return pl.pallas_call(
        functools.partial(gather_kernel, grid),
        out_shape=[
            jax.ShapeDtypeStruct((4, n, pad, D), BF16),
            jax.ShapeDtypeStruct((4, n, pad, D), BF16),
            jax.ShapeDtypeStruct((n, 4, pad, D), BF16),
            jax.ShapeDtypeStruct((2, n, 16, D), BF16),
        ],
        in_specs=[vmem] * 4,
        out_specs=[any_spec] * 4,
        scratch_shapes=[
            pltpu.VMEM((2, 2, dr, D), BF16),
            pltpu.VMEM((16, D), BF16),
            pltpu.VMEM((2, pad, D), BF16),
            pltpu.VMEM((16, D), BF16),
            pltpu.SemaphoreType.DMA((3, 4, n)),
            pltpu.SemaphoreType.DMA((2, n)),
            pltpu.SemaphoreType.DMA((nsend,)),
            pltpu.SemaphoreType.DMA((3, 2)),
            pltpu.SemaphoreType.DMA((1,)),
        ],
        compiler_params=pltpu.CompilerParams(collective_id=0, has_side_effects=True, vmem_limit_bytes=32 * 2**20),
    )(raw_attn, raw_up, raw_down, raw_vec)


class Reduce:
    def __init__(self, grid, sender, part, held, second, third, last, sems):
        self.grid, self.sender, self.part = grid, sender, part
        self.held, self.from_second, self.from_third, self.from_z = held, second, third, last
        self.sem_sib, self.sem_second, self.sem_third, self.sem_z = sems

    def to_sibling(self, d):
        g = self.grid
        z = g.zs(d)
        for jj in range(2):
            j = (1 - g.core) * 2 + jj
            self.sender.start(self.part(j, z), self.held.at[jj, z], self.sem_sib.at[jj, z], g.sib())

    def add_sibling(self, d):
        g, s = self.grid, self.grid.side
        z = g.zs(d)
        for jj in range(2):
            held = self.held.at[jj, z]
            self.sender.arrived(held, self.sem_sib.at[jj, z], g)
            own = self.part(g.core * 2 + jj, z)
            for h in range(s):
                def add(l, carry, h=h):
                    held[h, l] = (held[h, l].astype(F32) + own[h, l].astype(F32)).astype(BF16)
                    return carry
                lax.fori_loop(0, s, add, 0)
            for k in range(1, s):
                if jj % 2 == 0:
                    src, peer = held.at[g.his(k)], g.hi_peer(k)
                else:
                    src, peer = held.at[:, g.los(k)], g.lo_peer(k)
                self.sender.start(src, self.from_second.at[jj, s - k - 1, z], self.sem_second.at[jj, s - k - 1, z], peer)

    def add_second(self, d):
        g, s = self.grid, self.grid.side
        z = g.zs(d)
        for jj in range(2):
            for k in range(s - 1):
                self.sender.arrived(self.from_second.at[jj, k, z], self.sem_second.at[jj, k, z], g)
            for e in range(s):
                at = self.held.at[jj, z, g.hi, e] if jj % 2 == 0 else self.held.at[jj, z, e, g.lo]
                total = at[...].astype(F32)
                for k in range(s - 1):
                    total = total + self.from_second[jj, k, z, e].astype(F32)
                at[...] = total.astype(BF16)
            for k in range(1, s):
                if jj % 2 == 0:
                    src, peer = self.held.at[jj, z, g.hi, g.los(k)], g.lo_peer(k)
                else:
                    src, peer = self.held.at[jj, z, g.his(k), g.lo], g.hi_peer(k)
                self.sender.start(src, self.from_third.at[jj, s - k - 1, z], self.sem_third.at[jj, s - k - 1, z], peer)

    def own(self, jj, z):
        g, s = self.grid, self.grid.side
        for k in range(s - 1):
            self.sender.arrived(self.from_third.at[jj, k, z], self.sem_third.at[jj, k, z], g)
        total = self.held[jj, z, g.hi, g.lo].astype(F32)
        for k in range(s - 1):
            total = total + self.from_third[jj, k, z].astype(F32)
        return total

    def add_third(self, d):
        g = self.grid
        z = g.zs(d)
        for jj in range(2):
            at = self.held.at[jj, z, g.hi, g.lo]
            at[...] = self.own(jj, z).astype(BF16)
            self.sender.start(at, self.from_z.at[jj, g.nz - d - 1], self.sem_z.at[jj, g.nz - d - 1], g.z_peer(d))

    def result(self, jj):
        g = self.grid
        total = self.own(jj, g.z)
        for k in range(g.nz - 1):
            self.sender.arrived(self.from_z.at[jj, k], self.sem_z.at[jj, k], g)
            total = total + self.from_z[jj, k].astype(F32)
        return total

    @staticmethod
    def sends(grid):
        n, s = grid.nz, grid.side
        return 2 * (n + n * (s - 1) * 2 + n - 1)

    @staticmethod
    def scratch(grid, groups):
        n, s, pad = grid.nz, grid.side, grid.pad
        return [
            pltpu.VMEM((groups, 2, n, s, s, pad, D), BF16),
            pltpu.VMEM((groups, 2, s - 1, n, s, pad, D), BF16),
            pltpu.VMEM((groups, 2, s - 1, n, pad, D), BF16),
            pltpu.VMEM((groups, 2, n - 1, pad, D), BF16),
            pltpu.SemaphoreType.DMA((groups, 2, n)),
            pltpu.SemaphoreType.DMA((groups, 2, s - 1, n)),
            pltpu.SemaphoreType.DMA((groups, 2, s - 1, n)),
            pltpu.SemaphoreType.DMA((groups, 2, n - 1)),
        ]


def sum_everywhere(grid, sender, own, landing, sem):
    steps = [[grid.sib()],
             [grid.lo_peer(d) for d in range(1, grid.side)],
             [grid.hi_peer(d) for d in range(1, grid.side)],
             [grid.z_peer(d) for d in range(1, grid.nz)]]
    slot = 0
    for n, peers in enumerate(steps):
        for k, peer in enumerate(peers):
            sender.start(own.at[n], landing.at[slot + len(peers) - 1 - k], sem.at[slot + len(peers) - 1 - k], peer)
        total = own[n]
        for k in range(len(peers)):
            sender.arrived(landing.at[slot + k], sem.at[slot + k], grid)
            total = total + landing[slot + k]
        slot += len(peers)
        own[n + 1] = total


def peer_count(grid):
    return 1 + 2 * (grid.side - 1) + grid.nz - 1


def reduce_kernel(grid, g_attn, g_up, g_down, g_vec, o_attn, o_up, o_down, o_vec,
                  held, second, third, last, s1, s2, s3, s4, swap_out, swap_in, wsem, vec, vec_in, vsem, ssem):
    grid.place()
    grid.barrier()
    sender = Sender(ssem)
    c = grid.core
    parts = [lambda j, z: g_attn.at[j, z], lambda j, z: g_up.at[j, z], lambda j, z: g_down.at[z, :, :, j]]
    groups = [
        Reduce(grid, sender, parts[g], held.at[g], second.at[g], third.at[g], last.at[g],
               (s1.at[g], s2.at[g], s3.at[g], s4.at[g]))
        for g in range(3)
    ]
    order = [groups[2], groups[1], groups[0]]
    n = grid.nz
    for g in order:
        for d in range(n, 0, -1):
            g.to_sibling(d)
    vec[0] = g_vec[...]
    for g in order:
        for d in range(n, 0, -1):
            g.add_sibling(d)
    for g in order:
        for d in range(n, 0, -1):
            g.add_second(d)
    for g in order:
        for d in range(n - 1, 0, -1):
            g.add_third(d)
    sum_everywhere(grid, sender, vec, vec_in, vsem)
    o_vec[...] = vec[4]
    r, dr = grid.rows, grid.dev_rows
    for i, (g, out) in enumerate(((groups[1], o_up), (groups[0], o_attn))):
        for jj in range(2):
            total = g.result(jj)
            top, bottom = total[:dr], total[dr:r]
            out[c * 2 + jj] = jnp.where(c == 0, top, bottom)
            swap_out[i, jj] = jnp.where(c == 0, bottom, top)
            sender.start(swap_out.at[i, jj], swap_in.at[i, jj], wsem.at[i, jj], grid.sib())
    for jj in range(2):
        o_down[jj] = groups[2].result(jj)[:r]
    for i, out in enumerate((o_up, o_attn)):
        for jj in range(2):
            sender.arrived(swap_in.at[i, jj], wsem.at[i, jj], grid)
            out[(1 - c) * 2 + jj] = swap_in[i, jj]
    sender.finish()


def reduce_all(grid, g_attn, g_up, g_down, g_vec):
    n, s, pad, dr = grid.nz, grid.side, grid.pad, grid.dev_rows
    nsend = 3 * Reduce.sends(grid) + 4 + peer_count(grid)
    vmem = pl.BlockSpec(memory_space=pltpu.VMEM)
    return pl.pallas_call(
        functools.partial(reduce_kernel, grid),
        out_shape=[
            jax.ShapeDtypeStruct((4, dr, D), F32),
            jax.ShapeDtypeStruct((4, dr, D), F32),
            jax.ShapeDtypeStruct((2, grid.rows, D), F32),
            jax.ShapeDtypeStruct((16, D), F32),
        ],
        in_specs=[vmem] * 4,
        out_specs=[vmem] * 4,
        scratch_shapes=Reduce.scratch(grid, 3) + [
            pltpu.VMEM((2, 2, dr, D), F32),
            pltpu.VMEM((2, 2, dr, D), F32),
            pltpu.SemaphoreType.DMA((2, 2)),
            pltpu.VMEM((5, 16, D), F32),
            pltpu.VMEM((peer_count(grid), 16, D), F32),
            pltpu.SemaphoreType.DMA((peer_count(grid),)),
            pltpu.SemaphoreType.DMA((nsend,)),
        ],
        compiler_params=pltpu.CompilerParams(collective_id=1, has_side_effects=True, vmem_limit_bytes=56 * 2**20),
    )(g_attn, g_up, g_down, g_vec)


HEADS = 12
HD = 64
ROW = 512
BLOCK = 64


def dense(left, right):
    return jnp.dot(left, right, preferred_element_type=jnp.float32)


def product(left, right):
    return jnp.dot(left, right, precision=lax.Precision.HIGHEST, preferred_element_type=jnp.float32)


def layer_norm(values, scales, offset):
    center = values - jnp.mean(values, axis=-1, keepdims=True)
    spread = jnp.mean(center * center, axis=-1, keepdims=True)
    return center * lax.rsqrt(spread + 1e-05) * scales + offset


def pool_breadths(model_width):
    return [
        model_width,
        2 * model_width // 3,
        model_width // 3,
        model_width // 6,
        model_width // 12,
    ]


def matryoshka(averages, model_width):
    pieces = []
    for breadth in pool_breadths(model_width):
        leading = averages[:, :breadth]
        pieces.append(
            leading * lax.rsqrt(jnp.mean(leading * leading, axis=-1, keepdims=True) + 1e-06)
        )
    return jnp.concatenate(pieces, axis=-1)


def gelu_exact(values):
    return jax.nn.gelu(values, approximate=False)


def sentence_layout(block_bucket, lengths, block_size):
    block_count = block_bucket.shape[0]
    blocks = jnp.arange(block_count, dtype=jnp.int32)
    stride = block_bucket // block_size
    start_block = blocks // stride * stride
    block_len = jnp.sum(
        jnp.where(start_block[:, None] == blocks[None, :], lengths[None, :], 0), axis=1
    )
    token_start = jnp.repeat(start_block * block_size, block_size)
    token_len = jnp.repeat(block_len, block_size)
    positions = jnp.arange(block_count * block_size, dtype=jnp.int32)
    valid = positions - token_start < token_len
    member = (token_start[None, :] == (start_block * block_size)[:, None]) & valid[None, :]
    pool_matrix = (
        jnp.where(member, 1.0, 0.0).astype(jnp.float32) / block_len.astype(jnp.float32)[:, None]
    )
    return (token_start, valid, pool_matrix)


def masked_scores(query_rows, key_rows, start_rows, valid_rows):
    allowed = (start_rows[:, None] == start_rows[None, :]) & valid_rows[None, :]
    scores = (
        jnp.einsum("qhd,khd->hqk", query_rows, key_rows, preferred_element_type=jnp.float32) * 0.125
    )
    return jnp.where(allowed[None], scores, -1e30)


def attend_forward(items):
    query_rows, key_rows, value_rows, start_rows, valid_rows = items
    scores = masked_scores(query_rows, key_rows, start_rows, valid_rows)
    row_peak = jnp.max(scores, axis=-1, keepdims=True)
    exponent = jnp.exp(scores - row_peak)
    row_total = jnp.sum(exponent, axis=-1, keepdims=True)
    softmax_out = (exponent / row_total).astype(jnp.bfloat16)
    context = jnp.einsum(
        "hqk,khd->qhd", softmax_out, value_rows, preferred_element_type=jnp.float32
    )
    return (context.astype(jnp.bfloat16), row_peak + jnp.log(row_total))


def attend_backward(items):
    query_rows, key_rows, value_rows, grad_rows, log_total, start_rows, valid_rows = items
    scores = masked_scores(query_rows, key_rows, start_rows, valid_rows)
    softmax_out = jnp.exp(scores - log_total)
    grad_value_rows = jnp.einsum(
        "hqk,qhd->khd",
        softmax_out.astype(jnp.bfloat16),
        grad_rows,
        preferred_element_type=jnp.float32,
    )
    grad_probs = jnp.einsum(
        "qhd,khd->hqk", grad_rows, value_rows, preferred_element_type=jnp.float32
    )
    row_delta = jnp.sum(softmax_out * grad_probs, axis=-1, keepdims=True)
    grad_scores = (softmax_out * (grad_probs - row_delta)).astype(jnp.bfloat16)
    grad_query_rows = (
        jnp.einsum("hqk,khd->qhd", grad_scores, key_rows, preferred_element_type=jnp.float32)
        * 0.125
    )
    grad_key_rows = (
        jnp.einsum("hqk,qhd->khd", grad_scores, query_rows, preferred_element_type=jnp.float32)
        * 0.125
    )
    return (
        grad_query_rows.astype(jnp.bfloat16),
        grad_key_rows.astype(jnp.bfloat16),
        grad_value_rows.astype(jnp.bfloat16),
    )


def body(
    grid,
    tokens,
    block_bucket,
    lengths,
    query_weight,
    query_bias,
    key_weight,
    value_weight,
    value_bias,
    out_weight,
    out_bias,
    first_gain,
    first_shift,
    up_weight,
    up_bias,
    down_weight,
    down_bias,
    second_gain,
    second_shift,
    out_grad,
    pool_grad,
):
    rank = lax.axis_index("dp") * lax.axis_size("fsdp") + lax.axis_index("fsdp")
    dr = grid.dev_rows
    raw_attn = jnp.stack([query_weight, key_weight, value_weight, out_weight])
    raw_up = up_weight.reshape(dr, 4, D).transpose(1, 0, 2)
    raw_down = down_weight.reshape(4, dr, D)
    small = jnp.stack([query_bias, value_bias, out_bias, first_gain, first_shift, down_bias, second_gain, second_shift])
    small = lax.dynamic_update_slice(jnp.zeros((16, D), BF16), small, (0, rank * dr))
    wide = lax.dynamic_update_slice(jnp.zeros((16 * D,), BF16), up_bias, (rank * 4 * dr,)).reshape(16, D)
    w_attn, w_up, w_down, w_vec = gather_all(grid, raw_attn, raw_up, raw_down, jnp.stack([small, wide]))
    r = grid.rows
    w_attn = w_attn[:, :, :r].reshape(4, D, D)
    full_query, full_key, full_value, full_out = w_attn[0], w_attn[1], w_attn[2], w_attn[3]
    full_up = w_up[:, :, :r].reshape(4, D, D).transpose(1, 0, 2).reshape(D, 4 * D)
    full_down = w_down[:, :, :r].reshape(4 * D, D)
    vec = jnp.sum(w_vec.astype(F32), axis=1)
    bias_query, bias_value, bias_out, gain_first, shift_first, bias_down, gain_second, shift_second = [vec[0, i] for i in range(8)]
    bias_up = vec[1, :4].reshape(4 * D)
    up_back, down_back = full_up, full_down
    query_back, key_back, value_back, out_back = full_query, full_key, full_value, full_out
    token_start, valid, pool_matrix = sentence_layout(block_bucket, lengths, BLOCK)
    row_count = tokens.shape[0] // ROW

    def by_rows(array):
        return array.reshape((row_count, ROW) + array.shape[1:])

    def split_heads(array):
        return array.reshape(row_count, ROW, HEADS, HD)

    queries = (dense(tokens, full_query) + bias_query).astype(jnp.bfloat16)
    keys_all = dense(tokens, full_key).astype(jnp.bfloat16)
    values_all = (dense(tokens, full_value) + bias_value).astype(jnp.bfloat16)
    context, log_total = lax.map(
        attend_forward,
        (
            split_heads(queries),
            split_heads(keys_all),
            split_heads(values_all),
            by_rows(token_start),
            by_rows(valid),
        ),
    )
    context_low = context.reshape(-1, D)
    first_sum = tokens.astype(jnp.float32) + dense(context_low, full_out) + bias_out
    hidden_f, first_back = jax.vjp(layer_norm, first_sum, gain_first, shift_first)
    hidden_low = hidden_f.astype(jnp.bfloat16)
    pre_gelu = dense(hidden_low, full_up) + bias_up
    activated = gelu_exact(pre_gelu).astype(jnp.bfloat16)
    second_sum = hidden_low.astype(jnp.float32) + dense(activated, full_down) + bias_down
    outputs, second_back = jax.vjp(layer_norm, second_sum, gain_second, shift_second)
    pools, pool_back = jax.vjp(
        lambda rows_in: matryoshka(product(pool_matrix, rows_in), D), outputs
    )
    out_total = out_grad.astype(jnp.float32) + pool_back(pool_grad)[0]
    grad_second_sum, grad_gain_second, grad_shift_second = second_back(out_total)
    grad_branch = grad_second_sum.astype(jnp.bfloat16)
    grad_bias_down = jnp.sum(grad_branch.astype(jnp.float32), axis=0)
    grad_down = jnp.einsum("tf,td->fd", activated, grad_branch, preferred_element_type=jnp.float32)
    grad_activated = jnp.einsum(
        "td,fd->tf", grad_branch, down_back, preferred_element_type=jnp.float32
    )
    grad_pre = jax.vjp(gelu_exact, pre_gelu)[1](grad_activated)[0].astype(jnp.bfloat16)
    grad_bias_up = jnp.sum(grad_pre.astype(jnp.float32), axis=0)
    grad_up = jnp.einsum("td,tf->df", hidden_low, grad_pre, preferred_element_type=jnp.float32)
    grad_hidden = grad_second_sum + jnp.einsum(
        "tf,df->td", grad_pre, up_back, preferred_element_type=jnp.float32
    )
    grad_first_sum, grad_gain_first, grad_shift_first = first_back(grad_hidden)
    grad_attended = grad_first_sum.astype(jnp.bfloat16)
    grad_bias_out = jnp.sum(grad_attended.astype(jnp.float32), axis=0)
    grad_out = jnp.einsum(
        "td,te->de", context_low, grad_attended, preferred_element_type=jnp.float32
    )
    grad_context = jnp.einsum(
        "te,de->td", grad_attended, out_back, preferred_element_type=jnp.float32
    ).astype(jnp.bfloat16)
    grad_queries, grad_keys, grad_values = lax.map(
        attend_backward,
        (
            split_heads(queries),
            split_heads(keys_all),
            split_heads(values_all),
            split_heads(grad_context),
            log_total,
            by_rows(token_start),
            by_rows(valid),
        ),
    )
    grad_queries = grad_queries.reshape(-1, D)
    grad_keys = grad_keys.reshape(-1, D)
    grad_values = grad_values.reshape(-1, D)
    grad_query = jnp.einsum("td,te->de", tokens, grad_queries, preferred_element_type=jnp.float32)
    grad_key = jnp.einsum("td,te->de", tokens, grad_keys, preferred_element_type=jnp.float32)
    grad_value = jnp.einsum("td,te->de", tokens, grad_values, preferred_element_type=jnp.float32)
    grad_bias_query = jnp.sum(grad_queries.astype(jnp.float32), axis=0)
    grad_bias_value = jnp.sum(grad_values.astype(jnp.float32), axis=0)
    token_grad = grad_first_sum + jnp.einsum(
        "te,de->td", grad_queries, query_back, preferred_element_type=jnp.float32
    )
    token_grad = token_grad + jnp.einsum(
        "te,de->td", grad_keys, key_back, preferred_element_type=jnp.float32
    )
    token_grad = token_grad + jnp.einsum(
        "te,de->td", grad_values, value_back, preferred_element_type=jnp.float32
    )
    def blocks(grad):
        low = grad.astype(BF16).reshape(-1, grid.rows, D)
        return jnp.pad(low, ((0, 0), (0, grid.pad - grid.rows), (0, 0)))

    n, s, pad = grid.nz, grid.side, grid.pad
    g_attn = jnp.stack([blocks(grad_query), blocks(grad_key), blocks(grad_value), blocks(grad_out)]).reshape(4, n, s, s, pad, D)
    g_up = jnp.stack([blocks(grad_up[:, j * D : (j + 1) * D]) for j in range(4)]).reshape(4, n, s, s, pad, D)
    g_down = blocks(grad_down).reshape(n, s, s, 4, pad, D)
    g_vec = jnp.concatenate([
        jnp.stack([grad_bias_query, grad_bias_value, grad_bias_out, grad_gain_first, grad_shift_first, grad_bias_down, grad_gain_second, grad_shift_second]),
        grad_bias_up.reshape(4, D), jnp.zeros((4, D), F32)])
    o_attn, o_up, o_down, o_vec = reduce_all(grid, g_attn, g_up, g_down, g_vec)
    small = lax.dynamic_slice(o_vec, (0, rank * dr), (8, dr))
    wide = lax.dynamic_slice(o_vec[8:12].reshape(4 * D), (rank * 4 * dr,), (4 * dr,))
    return (
        outputs.astype(jnp.bfloat16),
        pools,
        token_grad,
        o_attn[0],
        small[0],
        o_attn[1],
        o_attn[2],
        small[1],
        o_attn[3],
        small[2],
        small[3],
        small[4],
        o_up.transpose(1, 0, 2).reshape(dr, 4 * D),
        wide,
        o_down.reshape(4 * dr, D),
        small[5],
        small[6],
        small[7],
    )


def solution(mesh):
    placed = (
        P(("dp", "fsdp"), None),
        P(("dp", "fsdp")),
        P(("dp", "fsdp")),
        P(("dp", "fsdp"), None),
        P(("dp", "fsdp")),
        P(("dp", "fsdp"), None),
        P(("dp", "fsdp"), None),
        P(("dp", "fsdp")),
        P(("dp", "fsdp"), None),
        P(("dp", "fsdp")),
        P(("dp", "fsdp")),
        P(("dp", "fsdp")),
        P(("dp", "fsdp"), None),
        P(("dp", "fsdp")),
        P(("dp", "fsdp"), None),
        P(("dp", "fsdp")),
        P(("dp", "fsdp")),
        P(("dp", "fsdp")),
        P(("dp", "fsdp"), None),
        P(("dp", "fsdp"), None),
    )
    return jax.shard_map(
        functools.partial(body, Grid(mesh.shape["dp"], mesh.shape["fsdp"])),
        mesh=mesh,
        in_specs=placed,
        out_specs=(
            P(("dp", "fsdp"), None),
            P(("dp", "fsdp"), None),
            P(("dp", "fsdp"), None),
            P(("dp", "fsdp"), None),
            P(("dp", "fsdp")),
            P(("dp", "fsdp"), None),
            P(("dp", "fsdp"), None),
            P(("dp", "fsdp")),
            P(("dp", "fsdp"), None),
            P(("dp", "fsdp")),
            P(("dp", "fsdp")),
            P(("dp", "fsdp")),
            P(("dp", "fsdp"), None),
            P(("dp", "fsdp")),
            P(("dp", "fsdp"), None),
            P(("dp", "fsdp")),
            P(("dp", "fsdp")),
            P(("dp", "fsdp")),
        ),
        check_vma=False,
    )
```

```python
import functools
import math

import jax
import jax.numpy as jnp
from jax import lax
from jax.experimental import pallas as pl
from jax.experimental.pallas import tpu as pltpu
from jax.sharding import PartitionSpec as P

MESH = pl.DeviceIdType.MESH
D = 768
F32 = jnp.float32
BF16 = jnp.bfloat16


class Grid:
    def __init__(self, nz, nf):
        self.nz = nz
        self.side = math.isqrt(nf // 2)
        assert 2 * self.side * self.side == nf
        self.chips = nz * self.side * self.side
        self.rows = D // self.chips
        self.dev_rows = self.rows // 2
        self.pad = -(-self.rows // 16) * 16

    def place(self):
        s = self.side
        self.z = lax.axis_index("dp")
        f = lax.axis_index("fsdp")
        self.core = lax.rem(f, 2)
        self.lo = lax.rem(f // 2, s)
        self.hi = f // (2 * s)

    def dev(self, z, hi, lo, core):
        return (z, (hi * self.side + lo) * 2 + core)

    def sib(self):
        return self.dev(self.z, self.hi, self.lo, 1 - self.core)

    def zs(self, d):
        return lax.rem(self.z + d, self.nz)

    def los(self, d):
        return lax.rem(self.lo + d, self.side)

    def his(self, d):
        return lax.rem(self.hi + d, self.side)

    def z_peer(self, d):
        return self.dev(self.zs(d), self.hi, self.lo, self.core)

    def lo_peer(self, d):
        return self.dev(self.z, self.hi, self.los(d), self.core)

    def hi_peer(self, d):
        return self.dev(self.z, self.his(d), self.lo, self.core)

    def chip(self, z, hi, lo):
        return (z * self.side + hi) * self.side + lo

    def peers(self):
        out = [self.sib()]
        out += [self.z_peer(d) for d in range(1, self.nz)]
        out += [self.lo_peer(d) for d in range(1, self.side)]
        out += [self.hi_peer(d) for d in range(1, self.side)]
        return out

    def barrier(self):
        sem = pltpu.get_barrier_semaphore()
        peers = self.peers()
        for peer in peers:
            pl.semaphore_signal(sem, inc=1, device_id=peer, device_id_type=MESH)
        pl.semaphore_wait(sem, len(peers))


class Sender:
    def __init__(self, sems):
        self.sems = sems
        self.started = []

    def start(self, src, dst, recv_sem, device):
        copy = pltpu.make_async_remote_copy(
            src_ref=src,
            dst_ref=dst,
            send_sem=self.sems.at[len(self.started)],
            recv_sem=recv_sem,
            device_id=device,
            device_id_type=MESH,
        )
        copy.start()
        self.started.append(copy)
        return copy

    def arrived(self, dst, recv_sem, grid):
        pltpu.make_async_remote_copy(
            src_ref=dst,
            dst_ref=dst,
            send_sem=self.sems.at[0],
            recv_sem=recv_sem,
            device_id=grid.sib(),
            device_id_type=MESH,
        ).wait_recv()

    def finish(self):
        for copy in self.started:
            copy.wait_send()


class Gather:
    def __init__(self, grid, sender, at, sem, per_core=2):
        self.grid, self.sender, self.at, self.sem = grid, sender, at, sem
        self.per_core = per_core

    def mine(self, jj):
        return self.grid.core * self.per_core + jj

    def send(self, j, p, device):
        self.sender.start(self.at(j, p), self.at(j, p), self.sem(j, p), device)

    def wait(self, j, p):
        self.sender.arrived(self.at(j, p), self.sem(j, p), self.grid)

    def own(self):
        g = self.grid
        for jj in range(self.per_core):
            j, p = self.mine(jj), g.chip(g.z, g.hi, g.lo)
            for d in range(1, g.nz):
                self.send(j, p, g.z_peer(d))
            self.spread(j, p)

    def spread(self, j, p):
        g = self.grid
        for d in range(1, g.side):
            self.send(j, p, g.lo_peer(d))
        for d in range(1, g.side):
            self.send(j, p, g.hi_peer(d))
        self.send(j, p, g.sib())

    def along_z(self, d):
        g = self.grid
        for jj in range(self.per_core):
            j, p = self.mine(jj), g.chip(g.zs(d), g.hi, g.lo)
            self.wait(j, p)
            self.spread(j, p)

    def second(self, d):
        g = self.grid
        for jj in range(self.per_core):
            j = self.mine(jj)
            for e in range(1, g.side):
                if jj % 2 == 0:
                    p = g.chip(g.zs(d), g.hi, g.los(e))
                else:
                    p = g.chip(g.zs(d), g.his(e), g.lo)
                self.wait(j, p)
                for k in range(1, g.side):
                    self.send(j, p, g.hi_peer(k) if jj % 2 == 0 else g.lo_peer(k))
                self.send(j, p, g.sib())

    def third(self, d):
        g = self.grid
        for jj in range(self.per_core):
            j = self.mine(jj)
            for e in range(1, g.side):
                for k in range(g.side):
                    if jj % 2 == 0:
                        p = g.chip(g.zs(d), g.his(e), g.los(k))
                    else:
                        p = g.chip(g.zs(d), g.his(k), g.los(e))
                    self.wait(j, p)
                    self.send(j, p, g.sib())

    def sibling(self):
        g = self.grid
        for jj in range(self.per_core):
            j = (1 - g.core) * self.per_core + jj
            for d in range(g.nz):
                for e in range(g.side):
                    for k in range(g.side):
                        self.wait(j, g.chip(g.zs(d), g.his(e), g.los(k)))

    @staticmethod
    def sends(grid, per_core):
        n, s = grid.nz, grid.side
        return per_core * (n - 1 + n * (s - 1) + n * s * (s - 1) + grid.chips)


def join_rows(grid, low, high):
    parts = [low.astype(F32), high.astype(F32)]
    if grid.pad != grid.rows:
        parts.append(jnp.zeros((grid.pad - grid.rows, low.shape[1]), F32))
    return jnp.concatenate(parts, axis=0).astype(BF16)


def gather_kernel(grid, attn_ref, up_ref, down_ref, vec_ref, w_attn, w_up, w_down, w_vec,
                  pre_ref, pre_vec, stage, stage_vec, rsem, vsem, ssem, psem, lsem):
    grid.place()
    grid.barrier()
    sender = Sender(ssem)
    c = grid.core
    me = grid.chip(grid.z, grid.hi, grid.lo)
    raws = (attn_ref, up_ref)
    for g, raw in enumerate(raws):
        for jj in range(2):
            sender.start(raw.at[(1 - c) * 2 + jj], pre_ref.at[g, jj], psem.at[g, jj], grid.sib())
    sender.start(vec_ref.at[1 - c], pre_vec, psem.at[2, 0], grid.sib())

    groups = [
        Gather(grid, sender, lambda j, p: w_attn.at[j, p], lambda j, p: rsem.at[0, j, p]),
        Gather(grid, sender, lambda j, p: w_up.at[j, p], lambda j, p: rsem.at[1, j, p]),
        Gather(grid, sender, lambda j, p: w_down.at[p, j], lambda j, p: rsem.at[2, j, p]),
    ]
    vec = Gather(grid, sender, lambda j, p: w_vec.at[j, p], lambda j, p: vsem.at[j, p], per_core=1)

    def put(src, dst, k):
        copy = pltpu.make_async_copy(src, dst, lsem.at[k])
        copy.start()
        copy.wait()

    def assemble(g):
        for jj in range(2):
            if g < 2:
                sender.arrived(pre_ref.at[g, jj], psem.at[g, jj], grid)
                own, other = raws[g][c * 2 + jj], pre_ref[g, jj]
                first = jnp.where(c == 0, own.astype(F32), other.astype(F32))
                last = jnp.where(c == 0, other.astype(F32), own.astype(F32))
            else:
                first, last = down_ref[2 * jj], down_ref[2 * jj + 1]
            stage[jj] = join_rows(grid, first, last)
            put(stage.at[jj], groups[g].at(c * 2 + jj, me), 0)

    assemble(0)
    groups[0].own()
    sender.arrived(pre_vec, psem.at[2, 0], grid)
    stage_vec[...] = (vec_ref[c].astype(F32) + pre_vec[...].astype(F32)).astype(BF16)
    put(stage_vec, w_vec.at[c, me], 0)
    vec.own()
    def z_steps(g):
        for d in range(grid.nz - 1, 0, -1):
            g.along_z(d)

    def second_steps(g):
        for d in range(grid.nz, 0, -1):
            g.second(d)

    def third_steps(g):
        for d in range(grid.nz, 0, -1):
            g.third(d)

    z_steps(vec)
    z_steps(groups[0])
    assemble(1)
    groups[1].own()
    second_steps(vec)
    second_steps(groups[0])
    z_steps(groups[1])
    assemble(2)
    groups[2].own()
    third_steps(vec)
    third_steps(groups[0])
    second_steps(groups[1])
    z_steps(groups[2])
    third_steps(groups[1])
    second_steps(groups[2])
    third_steps(groups[2])
    for g in [vec] + groups:
        g.sibling()
    sender.finish()


def gather_all(grid, raw_attn, raw_up, raw_down, raw_vec):
    n, pad, dr = grid.chips, grid.pad, grid.dev_rows
    nsend = 5 + 3 * Gather.sends(grid, 2) + Gather.sends(grid, 1)
    any_spec = pl.BlockSpec(memory_space=pl.ANY)
    vmem = pl.BlockSpec(memory_space=pltpu.VMEM)
    return pl.pallas_call(
        functools.partial(gather_kernel, grid),
        out_shape=[
            jax.ShapeDtypeStruct((4, n, pad, D), BF16),
            jax.ShapeDtypeStruct((4, n, pad, D), BF16),
            jax.ShapeDtypeStruct((n, 4, pad, D), BF16),
            jax.ShapeDtypeStruct((2, n, 16, D), BF16),
        ],
        in_specs=[vmem] * 4,
        out_specs=[any_spec] * 4,
        scratch_shapes=[
            pltpu.VMEM((2, 2, dr, D), BF16),
            pltpu.VMEM((16, D), BF16),
            pltpu.VMEM((2, pad, D), BF16),
            pltpu.VMEM((16, D), BF16),
            pltpu.SemaphoreType.DMA((3, 4, n)),
            pltpu.SemaphoreType.DMA((2, n)),
            pltpu.SemaphoreType.DMA((nsend,)),
            pltpu.SemaphoreType.DMA((3, 2)),
            pltpu.SemaphoreType.DMA((1,)),
        ],
        compiler_params=pltpu.CompilerParams(collective_id=0, has_side_effects=True, vmem_limit_bytes=32 * 2**20),
    )(raw_attn, raw_up, raw_down, raw_vec)
class Reduce:
    def __init__(self, grid, sender, part, held, second, third, last, sems):
        self.grid, self.sender, self.part = grid, sender, part
        self.held, self.from_second, self.from_third, self.from_z = held, second, third, last
        self.sem_sib, self.sem_second, self.sem_third, self.sem_z = sems

    def to_sibling(self, d):
        g = self.grid
        z = g.zs(d)
        for jj in range(2):
            j = (1 - g.core) * 2 + jj
            self.sender.start(self.part(j, z), self.held.at[jj, z], self.sem_sib.at[jj, z], g.sib())

    def add_sibling(self, d):
        g, s = self.grid, self.grid.side
        z = g.zs(d)
        for jj in range(2):
            held = self.held.at[jj, z]
            self.sender.arrived(held, self.sem_sib.at[jj, z], g)
            own = self.part(g.core * 2 + jj, z)
            for h in range(s):
                def add(l, carry, h=h):
                    held[h, l] = (held[h, l].astype(F32) + own[h, l].astype(F32)).astype(BF16)
                    return carry
                lax.fori_loop(0, s, add, 0)
            for k in range(1, s):
                if jj % 2 == 0:
                    src, peer = held.at[g.his(k)], g.hi_peer(k)
                else:
                    src, peer = held.at[:, g.los(k)], g.lo_peer(k)
                self.sender.start(src, self.from_second.at[jj, s - k - 1, z], self.sem_second.at[jj, s - k - 1, z], peer)

    def add_second(self, d):
        g, s = self.grid, self.grid.side
        z = g.zs(d)
        for jj in range(2):
            for k in range(s - 1):
                self.sender.arrived(self.from_second.at[jj, k, z], self.sem_second.at[jj, k, z], g)
            for e in range(s):
                at = self.held.at[jj, z, g.hi, e] if jj % 2 == 0 else self.held.at[jj, z, e, g.lo]
                total = at[...].astype(F32)
                for k in range(s - 1):
                    total = total + self.from_second[jj, k, z, e].astype(F32)
                at[...] = total.astype(BF16)
            for k in range(1, s):
                if jj % 2 == 0:
                    src, peer = self.held.at[jj, z, g.hi, g.los(k)], g.lo_peer(k)
                else:
                    src, peer = self.held.at[jj, z, g.his(k), g.lo], g.hi_peer(k)
                self.sender.start(src, self.from_third.at[jj, s - k - 1, z], self.sem_third.at[jj, s - k - 1, z], peer)

    def own(self, jj, z):
        g, s = self.grid, self.grid.side
        for k in range(s - 1):
            self.sender.arrived(self.from_third.at[jj, k, z], self.sem_third.at[jj, k, z], g)
        total = self.held[jj, z, g.hi, g.lo].astype(F32)
        for k in range(s - 1):
            total = total + self.from_third[jj, k, z].astype(F32)
        return total

    def add_third(self, d):
        g = self.grid
        z = g.zs(d)
        for jj in range(2):
            at = self.held.at[jj, z, g.hi, g.lo]
            at[...] = self.own(jj, z).astype(BF16)
            self.sender.start(at, self.from_z.at[jj, g.nz - d - 1], self.sem_z.at[jj, g.nz - d - 1], g.z_peer(d))

    def result(self, jj):
        g = self.grid
        total = self.own(jj, g.z)
        for k in range(g.nz - 1):
            self.sender.arrived(self.from_z.at[jj, k], self.sem_z.at[jj, k], g)
            total = total + self.from_z[jj, k].astype(F32)
        return total

    @staticmethod
    def sends(grid):
        n, s = grid.nz, grid.side
        return 2 * (n + n * (s - 1) * 2 + n - 1)

    @staticmethod
    def scratch(grid, groups):
        n, s, pad = grid.nz, grid.side, grid.pad
        return [
            pltpu.VMEM((groups, 2, n, s, s, pad, D), BF16),
            pltpu.VMEM((groups, 2, s - 1, n, s, pad, D), BF16),
            pltpu.VMEM((groups, 2, s - 1, n, pad, D), BF16),
            pltpu.VMEM((groups, 2, n - 1, pad, D), BF16),
            pltpu.SemaphoreType.DMA((groups, 2, n)),
            pltpu.SemaphoreType.DMA((groups, 2, s - 1, n)),
            pltpu.SemaphoreType.DMA((groups, 2, s - 1, n)),
            pltpu.SemaphoreType.DMA((groups, 2, n - 1)),
        ]


def sum_everywhere(grid, sender, own, landing, sem):
    steps = [[grid.sib()],
             [grid.lo_peer(d) for d in range(1, grid.side)],
             [grid.hi_peer(d) for d in range(1, grid.side)],
             [grid.z_peer(d) for d in range(1, grid.nz)]]
    slot = 0
    for n, peers in enumerate(steps):
        for k, peer in enumerate(peers):
            sender.start(own.at[n], landing.at[slot + len(peers) - 1 - k], sem.at[slot + len(peers) - 1 - k], peer)
        total = own[n]
        for k in range(len(peers)):
            sender.arrived(landing.at[slot + k], sem.at[slot + k], grid)
            total = total + landing[slot + k]
        slot += len(peers)
        own[n + 1] = total


def peer_count(grid):
    return 1 + 2 * (grid.side - 1) + grid.nz - 1


def reduce_kernel(grid, g_attn, g_up, g_down, g_vec, o_attn, o_up, o_down, o_vec,
                  held, second, third, last, s1, s2, s3, s4, swap_out, swap_in, wsem, vec, vec_in, vsem, ssem):
    grid.place()
    grid.barrier()
    sender = Sender(ssem)
    c = grid.core
    parts = [lambda j, z: g_attn.at[j, z], lambda j, z: g_up.at[j, z], lambda j, z: g_down.at[z, :, :, j]]
    groups = [
        Reduce(grid, sender, parts[g], held.at[g], second.at[g], third.at[g], last.at[g],
               (s1.at[g], s2.at[g], s3.at[g], s4.at[g]))
        for g in range(3)
    ]
    order = [groups[2], groups[1], groups[0]]
    n = grid.nz
    for g in order:
        for d in range(n, 0, -1):
            g.to_sibling(d)
    vec[0] = g_vec[...]
    for g in order:
        for d in range(n, 0, -1):
            g.add_sibling(d)
    for g in order:
        for d in range(n, 0, -1):
            g.add_second(d)
    for g in order:
        for d in range(n - 1, 0, -1):
            g.add_third(d)
    sum_everywhere(grid, sender, vec, vec_in, vsem)
    o_vec[...] = vec[4]
    r, dr = grid.rows, grid.dev_rows
    for i, (g, out) in enumerate(((groups[1], o_up), (groups[0], o_attn))):
        for jj in range(2):
            total = g.result(jj)
            top, bottom = total[:dr], total[dr:r]
            out[c * 2 + jj] = jnp.where(c == 0, top, bottom)
            swap_out[i, jj] = jnp.where(c == 0, bottom, top)
            sender.start(swap_out.at[i, jj], swap_in.at[i, jj], wsem.at[i, jj], grid.sib())
    for jj in range(2):
        o_down[jj] = groups[2].result(jj)[:r]
    for i, out in enumerate((o_up, o_attn)):
        for jj in range(2):
            sender.arrived(swap_in.at[i, jj], wsem.at[i, jj], grid)
            out[(1 - c) * 2 + jj] = swap_in[i, jj]
    sender.finish()


def reduce_all(grid, g_attn, g_up, g_down, g_vec):
    n, s, pad, dr = grid.nz, grid.side, grid.pad, grid.dev_rows
    nsend = 3 * Reduce.sends(grid) + 4 + peer_count(grid)
    vmem = pl.BlockSpec(memory_space=pltpu.VMEM)
    return pl.pallas_call(
        functools.partial(reduce_kernel, grid),
        out_shape=[
            jax.ShapeDtypeStruct((4, dr, D), F32),
            jax.ShapeDtypeStruct((4, dr, D), F32),
            jax.ShapeDtypeStruct((2, grid.rows, D), F32),
            jax.ShapeDtypeStruct((16, D), F32),
        ],
        in_specs=[vmem] * 4,
        out_specs=[vmem] * 4,
        scratch_shapes=Reduce.scratch(grid, 3) + [
            pltpu.VMEM((2, 2, dr, D), F32),
            pltpu.VMEM((2, 2, dr, D), F32),
            pltpu.SemaphoreType.DMA((2, 2)),
            pltpu.VMEM((5, 16, D), F32),
            pltpu.VMEM((peer_count(grid), 16, D), F32),
            pltpu.SemaphoreType.DMA((peer_count(grid),)),
            pltpu.SemaphoreType.DMA((nsend,)),
        ],
        compiler_params=pltpu.CompilerParams(collective_id=1, has_side_effects=True, vmem_limit_bytes=56 * 2**20),
    )(g_attn, g_up, g_down, g_vec)
HEADS = 12
HD = 64
ROW = 512
BLOCK = 64
PER_ROW = ROW // BLOCK
NEG = -1e30
TM = 256


def mm(a, b):
    return jnp.dot(a, b, preferred_element_type=F32)


def mm_nt(a, b):
    return lax.dot_general(a, b, (((1,), (1,)), ((), ())), preferred_element_type=F32)


def mm_tn(a, b):
    return lax.dot_general(a, b, (((0,), (0,)), ((), ())), preferred_element_type=F32)


def tile(i, size):
    return pl.ds(pl.multiple_of(i * size, size), size)


def loop(n, f):
    def step(i, carry):
        f(i)
        return carry
    lax.fori_loop(0, n, step, 0)


def row_blocks(bucket_ref, length_ref, row):
    starts, lens = [], []
    for b in range(PER_ROW):
        stride = bucket_ref[row * PER_ROW + b] // BLOCK
        first = b // stride * stride
        starts.append(first)
        lens.append(length_ref[row * PER_ROW + first])
    return starts, lens


def pick(ids, values):
    out = jnp.zeros_like(ids)
    for b, value in enumerate(values):
        out = jnp.where(ids == b, value, out)
    return out


def write_mask(mask_ref, starts, lens):
    query = pick(lax.broadcasted_iota(jnp.int32, (BLOCK, ROW), 1) // BLOCK, starts)
    place = lax.broadcasted_iota(jnp.int32, (BLOCK, ROW), 0)
    for b in range(PER_ROW):
        limit = lens[b] - (b - starts[b]) * BLOCK
        allowed = (query == starts[b]) & (place < limit)
        mask_ref[b * BLOCK : (b + 1) * BLOCK, :] = jnp.where(allowed, 0.0, NEG)


def member_matrix(starts, lens):
    lane = lax.broadcasted_iota(jnp.int32, (PER_ROW, ROW), 1)
    token_start = pick(lane // BLOCK, starts)
    token_len = pick(lane // BLOCK, lens)
    valid = lane - token_start * BLOCK < token_len
    block = lax.broadcasted_iota(jnp.int32, (PER_ROW, ROW), 0)
    member = jnp.where((token_start == pick(block, starts)) & valid, 1.0, 0.0).astype(F32)
    lens_col = pick(lax.broadcasted_iota(jnp.int32, (PER_ROW, 1), 0), lens)
    return member, 1.0 / lens_col.astype(F32)


def layer_norm_parts(v):
    center = v - jnp.mean(v, axis=-1, keepdims=True)
    spread = jnp.mean(center * center, axis=-1, keepdims=True)
    scale = lax.rsqrt(spread + 1e-05)
    return center * scale, scale


def layer_norm_back(grad, normed, scale, gain):
    g = grad * gain
    return scale * (g - jnp.mean(g, axis=-1, keepdims=True) - normed * jnp.mean(g * normed, axis=-1, keepdims=True))


def gelu_both(x):
    z = jnp.abs(x) * 0.7071067811865476
    t = 1.0 / (1.0 + 0.3275911 * z)
    e = jnp.exp(x * x * -0.5)
    poly = ((((1.061405429 * t - 1.453152027) * t + 1.421413741) * t - 0.284496736) * t + 0.254829592) * t
    tail = 0.5 * poly * e
    phi = jnp.where(x < 0, tail, 1.0 - tail)
    return x * phi, phi + x * e * 0.3989422804014327


def project(tokens, weight, out, bias=None, scale=None):
    def step(i):
        r = mm(tokens[tile(i, TM), :], weight)
        if bias is not None:
            r = r + bias
        r = r.astype(BF16)
        if scale is not None:
            r = (r.astype(F32) * scale).astype(BF16)
        out[tile(i, TM), :] = r
    loop(tokens.shape[0] // TM, step)


def half(shape, axis, h):
    return lax.broadcasted_iota(jnp.int32, shape, axis) // HD == h


def attend_pair(queries, keys, values, context, logs, mask, row, pair, chunk=256):
    rows, cols = pl.ds(row * ROW, ROW), tile(pair, 2 * HD)
    key_slab, value_slab = keys[rows, cols], values[rows, cols]
    value_turned = value_slab.astype(F32).T.astype(BF16)
    only = [jnp.where(half((ROW, 2 * HD), 1, h), key_slab.astype(F32), 0.0).astype(BF16) for h in range(2)]
    for c in range(ROW // chunk):
        query_slab = queries[pl.ds(row * ROW + c * chunk, chunk), cols]
        parts = []
        for h in range(2):
            s = mm_nt(only[h], query_slab) + mask[:, c * chunk : (c + 1) * chunk]
            peak = jnp.max(s, axis=0, keepdims=True)
            e = jnp.exp(s - peak)
            total = jnp.sum(e, axis=0, keepdims=True)
            logs[row, pair, h : h + 1, c * chunk : (c + 1) * chunk] = peak + jnp.log(total)
            parts.append(mm(value_turned, e.astype(BF16)) * (1.0 / total))
        turned = jnp.where(half((2 * HD, chunk), 0, 0), parts[0], parts[1])
        context[pl.ds(row * ROW + c * chunk, chunk), cols] = turned.T.astype(BF16)


def attend_pair_back(queries, keys, values, context, logs, mask, grad_context, grad_q, grad_k, grad_v, row, pair, chunk=256):
    rows, cols = pl.ds(row * ROW, ROW), tile(pair, 2 * HD)
    key_slab, value_slab = keys[rows, cols], values[rows, cols]
    key_turned = key_slab.astype(F32).T.astype(BF16)
    lane = [half((ROW, 2 * HD), 1, h) for h in range(2)]
    only_k = [jnp.where(lane[h], key_slab.astype(F32), 0.0).astype(BF16) for h in range(2)]
    only_v = [jnp.where(lane[h], value_slab.astype(F32), 0.0).astype(BF16) for h in range(2)]
    sums = []
    for c in range(ROW // chunk):
        part = pl.ds(row * ROW + c * chunk, chunk)
        query_slab, grad_slab = queries[part, cols], grad_context[part, cols]
        dot = (grad_slab.astype(F32) * context[part, cols].astype(F32)).T
        gq, gk, gv = [], [], []
        for h in range(2):
            delta = jnp.sum(dot[h * HD : (h + 1) * HD], axis=0, keepdims=True)
            s = mm_nt(only_k[h], query_slab) + mask[:, c * chunk : (c + 1) * chunk]
            p = jnp.exp(s - logs[row, pair, h : h + 1, c * chunk : (c + 1) * chunk])
            gp = mm_nt(only_v[h], grad_slab)
            gs = (p * (gp - delta)).astype(BF16)
            gv.append(mm(p.astype(BF16), grad_slab))
            gk.append(mm(gs, query_slab))
            gq.append(mm(key_turned, gs))
        turned = jnp.where(half((2 * HD, chunk), 0, 0), gq[0], gq[1]) * 0.125
        grad_q[part, cols] = turned.T.astype(BF16)
        now = (jnp.where(lane[0], gk[0], gk[1]), jnp.where(lane[0], gv[0], gv[1]))
        sums = now if c == 0 else tuple(a + b for a, b in zip(sums, now))
    grad_k[rows, cols] = sums[0].astype(BF16)
    grad_v[rows, cols] = sums[1].astype(BF16)


def attend_pair_rows(queries, keys, values, context, logs, mask, row, pair, chunk=256):
    rows, cols = pl.ds(row * ROW, ROW), tile(pair, 2 * HD)
    key_slab, value_slab = keys[rows, cols], values[rows, cols]
    for c in range(ROW // chunk):
        part = pl.ds(row * ROW + c * chunk, chunk)
        query_slab = queries[part, cols]
        parts, cols_log = [], []
        lane = [half((chunk, 2 * HD), 1, h) for h in range(2)]
        for h in range(2):
            only = jnp.where(lane[h], query_slab.astype(F32), 0.0).astype(BF16)
            s = mm_nt(only, key_slab) + mask[c * chunk : (c + 1) * chunk, :]
            peak = jnp.max(s, axis=1, keepdims=True)
            e = jnp.exp(s - peak)
            total = jnp.sum(e, axis=1, keepdims=True)
            cols_log.append(peak + jnp.log(total))
            parts.append(mm(e.astype(BF16), value_slab) * (1.0 / total))
        context[part, cols] = jnp.where(lane[0], parts[0], parts[1]).astype(BF16)
        both = jnp.where(lane[0], cols_log[0], cols_log[1]).T
        for h in range(2):
            logs[row, pair, h : h + 1, c * chunk : (c + 1) * chunk] = both[h * HD : h * HD + 1]


QB, VB, OB, G1, S1, DB, G2, S2 = range(8)
UB = 8


def after_attention(tokens, context, w_out, vec, normed, scale, hidden, i, tm):
    rows = tile(i, tm)
    first = tokens[rows, :].astype(F32) + mm(context[rows, :], w_out) + vec[OB : OB + 1, :]
    n, r = layer_norm_parts(first)
    normed[rows, :] = n
    scale[rows, :] = jnp.broadcast_to(r, (tm, 128))
    hidden[rows, :] = (n * vec[G1 : G1 + 1, :] + vec[S1 : S1 + 1, :]).astype(BF16)


def feed_up(hidden, w_up, vec, act, slope, i, j, tm):
    rows, cols = tile(i, tm), pl.ds(j * D, D)
    value, deriv = gelu_both(mm(hidden[rows, :], w_up[j]) + vec[UB + j : UB + j + 1, :])
    act[rows, cols] = value.astype(BF16)
    slope[rows, cols] = deriv.astype(BF16)


def feed_down(hidden, act, w_down, vec, normed, scale, i, tm):
    rows = tile(i, tm)
    second = hidden[rows, :].astype(F32) + mm(act[rows, :], w_down) + vec[DB : DB + 1, :]
    n, r = layer_norm_parts(second)
    normed[rows, :] = n
    scale[rows, :] = jnp.broadcast_to(r, (tm, 128))


WIDTHS = (D, 2 * D // 3, D // 3, D // 6, D // 12)


def split_low(x):
    high = x.astype(BF16)
    return high, (x - high.astype(F32)).astype(BF16)


def pool_row(normed, vec, layer_out, pools, pool_grad, out_grad, total, starts, lens, row):
    rows = pl.ds(row * ROW, ROW)
    member, inverse = member_matrix(starts, lens)
    member = member.astype(BF16)
    outputs = normed[rows, :] * vec[G2 : G2 + 1, :] + vec[S2 : S2 + 1, :]
    layer_out[rows, :] = outputs.astype(BF16)
    high, low = split_low(outputs)
    avg = (mm(member, high) + mm(member, low)) * inverse
    square = avg * avg
    blocks = pl.ds(row * PER_ROW, PER_ROW)
    grad = None
    at = 0
    for width in WIDTHS:
        r = lax.rsqrt(jnp.sum(square[:, :width], axis=-1, keepdims=True) / width + 1e-06)
        lead = avg[:, :width]
        pools[blocks, at : at + width] = lead * r
        g = pool_grad[blocks, at : at + width]
        back = g * r - lead * (r * r * r * (jnp.sum(g * lead, axis=-1, keepdims=True) / width))
        if width % 128:
            wide = -(-width // 128) * 128
            back = jnp.concatenate([back, jnp.zeros((PER_ROW, wide - width), F32)], axis=1)
        if grad is None:
            grad = back
        else:
            grad = jnp.concatenate([grad[:, : back.shape[1]] + back, grad[:, back.shape[1] :]], axis=1)
        at += width
    high, low = split_low(grad * inverse)
    both = jnp.concatenate([high, low], axis=0)
    total[rows, :] = out_grad[rows, :].astype(F32) + mm_tn(jnp.concatenate([member, member], axis=0), both)


def add_row(vec_grad, k, values):
    vec_grad[k : k + 1, :] += jnp.sum(values, axis=0, keepdims=True)


def second_norm_back(total, normed, scale, vec, vec_grad, branch, i, tm):
    rows = tile(i, tm)
    g, n = total[rows, :], normed[rows, :]
    add_row(vec_grad, G2, g * n)
    add_row(vec_grad, S2, g)
    back = layer_norm_back(g, n, scale[rows, :1], vec[G2 : G2 + 1, :])
    total[rows, :] = back
    low = back.astype(BF16)
    branch[rows, :] = low
    add_row(vec_grad, DB, low.astype(F32))


def feed_back(branch, w_down, slope, vec_grad, i, j, tm):
    rows, cols = tile(i, tm), pl.ds(j * D, D)
    g = (mm_nt(branch[rows, :], w_down[cols, :]) * slope[rows, cols].astype(F32)).astype(BF16)
    slope[rows, cols] = g
    add_row(vec_grad, UB + j, g.astype(F32))


def hidden_back(total, grad_pre, w_up, normed, scale, vec, vec_grad, attended, i, tm):
    rows = tile(i, tm)
    g = total[rows, :]
    for j in range(4):
        g = g + mm_nt(grad_pre[rows, j * D : (j + 1) * D], w_up[j])
    n = normed[rows, :]
    add_row(vec_grad, G1, g * n)
    add_row(vec_grad, S1, g)
    back = layer_norm_back(g, n, scale[rows, :1], vec[G1 : G1 + 1, :])
    total[rows, :] = back
    low = back.astype(BF16)
    attended[rows, :] = low
    add_row(vec_grad, OB, low.astype(F32))


def turn(x, out, tm=256):
    for i in range(x.shape[0] // tm):
        for j in range(x.shape[1] // tm):
            out[j * tm : (j + 1) * tm, i * tm : (i + 1) * tm] = x[i * tm : (i + 1) * tm, j * tm : (j + 1) * tm].T
class Memory:
    NAMES = ("attn", "up", "down", "spare", "act", "slope", "x", "ctx", "hidden", "turned", "norm", "total",
             "scale1", "scale2", "mask", "logs", "vec", "vec_grad", "lsem")

    def __init__(self, refs):
        for name, ref in zip(self.NAMES, refs):
            setattr(self, name, ref)

    @staticmethod
    def shapes(tokens):
        v = pltpu.VMEM
        weights = [v((4 * D, D), BF16)] * 4
        return weights + [
            v((4, tokens, D), BF16), v((4, tokens, D), BF16),
            v((tokens, D), BF16), v((tokens, D), BF16), v((tokens, D), BF16), v((D, tokens), BF16),
            v((tokens, D), F32), v((tokens, D), F32), v((tokens, 128), F32), v((tokens, 128), F32),
            v((ROW, ROW), F32), v((tokens // ROW, HEADS // 2, 8, ROW), F32), v((16, D), F32), v((16, D), F32),
            pltpu.SemaphoreType.DMA((12,)),
        ]


def panel(ref, j):
    return ref.at[j * D : (j + 1) * D]


class NoNetwork:
    def __getattr__(self, name):
        return lambda *a: None


def layer_steps(m, net, bucket, length, tokens_in, out_grad_in, pool_grad, layer_out, pools, token_grad, keep_qkv, keep_norm):
    count = m.x.shape[0]
    tiles, rows_total = count // TM, count // ROW

    def copy(src, dst, k):
        return pltpu.make_async_copy(src, dst, m.lsem.at[k])

    queries, keys, values = (m.slope.at[j] for j in range(3))
    load_tokens = copy(tokens_in, m.x, 0)
    load_tokens.start()
    net.begin()
    m.vec_grad[...] = jnp.zeros_like(m.vec_grad)
    load_tokens.wait()
    net.need_attn()
    w_query, w_key, w_value, w_out = (panel(m.attn, j) for j in range(4))

    def qkv(i):
        rows = tile(i, TM)
        t = m.x[rows, :]
        q = (mm(t, w_query[...]) + m.vec[QB : QB + 1, :]).astype(BF16)
        queries[rows, :] = (q.astype(F32) * 0.125).astype(BF16)
        keys[rows, :] = mm(t, w_key[...]).astype(BF16)
        values[rows, :] = (mm(t, w_value[...]) + m.vec[VB : VB + 1, :]).astype(BF16)

    loop(tiles, qkv)
    for row in range(rows_total):
        starts, lens = row_blocks(bucket, length, row)
        write_mask(m.mask, starts, lens)
        m.mask[...] = m.mask[...].T
        for part in range(2):
            net.during_attention(row * 2 + part)
            loop(3, lambda p: attend_pair_rows(queries, keys, values, m.ctx, m.logs, m.mask, row, p + 3 * part, ROW))
    stores = [copy(m.slope.at[j], keep_qkv.at[j], 1 + j) for j in range(3)]
    for s in stores:
        s.start()
    loop(tiles, lambda i: after_attention(m.x, m.ctx, w_out[...], m.vec, m.norm, m.scale1, m.hidden, i, TM))
    stores.append(copy(m.norm, keep_norm, 4))
    stores[-1].start()
    load_grad = copy(out_grad_in, m.x, 0)
    load_grad.start()
    net.need_up()
    for s in stores[:3]:
        s.wait()
    for j in range(4):
        w = panel(m.up, j)

        def feed(i, j=j, w=w):
            rows = tile(i, TM)
            value, deriv = gelu_both(mm(m.hidden[rows, :], w[...]) + m.vec[UB + j : UB + j + 1, :])
            m.act[j, rows, :] = value.astype(BF16)
            m.slope[j, rows, :] = deriv.astype(BF16)

        loop(tiles, feed)
        net.during_up(j)
    stores[3].wait()
    net.need_down()

    def down(i):
        rows = tile(i, TM)
        second = m.hidden[rows, :].astype(F32) + m.vec[DB : DB + 1, :]
        for j in range(4):
            second = second + mm(m.act[j, rows, :], panel(m.down, j)[...])
        n, r = layer_norm_parts(second)
        m.norm[rows, :] = n
        m.scale2[rows, :] = jnp.broadcast_to(r, (TM, 128))

    loop(tiles, down)
    load_grad.wait()
    out_low = m.spare.at[:count]
    for row in range(rows_total):
        starts, lens = row_blocks(bucket, length, row)
        pool_row(m.norm, m.vec, out_low, pools, pool_grad, m.x, m.total, starts, lens, row)
    store_out = copy(out_low, layer_out, 5)
    store_out.start()
    loop(tiles, lambda i: second_norm_back(m.total, m.norm, m.scale2, m.vec, m.vec_grad, m.x, i, TM))
    load_norm = copy(keep_norm, m.norm, 6)
    load_norm.start()
    store_out.wait()
    net.gathered()
    for j in range(4):
        def grad_down(i, j=j):
            cols = tile(i, TM)
            m.spare[pl.ds(pl.multiple_of(i * TM + j * D, TM), TM), :] = mm_tn(m.act[j, :, cols], m.x[...]).astype(BF16)
        loop(D // TM, grad_down)
    net.ready_down()
    for j in range(4):
        def back(i, j=j):
            rows = tile(i, TM)
            g = (mm_nt(m.x[rows, :], panel(m.down, j)[...]) * m.slope[j, rows, :].astype(F32)).astype(BF16)
            m.slope[j, rows, :] = g
            add_row(m.vec_grad, UB + j, g.astype(F32))
        loop(tiles, back)
        net.during_back(j)
    turn(m.hidden, m.turned)
    for j in range(4):
        def grad_up(i, j=j):
            at = pl.ds(pl.multiple_of(i * TM + j * D, TM), TM)
            m.down[at, :] = mm(m.turned[tile(i, TM), :], m.slope[j]).astype(BF16)
        loop(D // TM, grad_up)
    net.ready_up()
    load_norm.wait()

    def first_back(i):
        rows = tile(i, TM)
        g = m.total[rows, :]
        for j in range(4):
            g = g + mm_nt(m.slope[j, rows, :], panel(m.up, j)[...])
        n = m.norm[rows, :]
        add_row(m.vec_grad, G1, g * n)
        add_row(m.vec_grad, S1, g)
        back = layer_norm_back(g, n, m.scale1[rows, :1], m.vec[G1 : G1 + 1, :])
        m.total[rows, :] = back
        low = back.astype(BF16)
        m.x[rows, :] = low
        add_row(m.vec_grad, OB, low.astype(F32))

    loop(tiles, first_back)
    loads = [copy(keep_qkv.at[j], m.slope.at[j], 7 + j) for j in range(3)]
    loads.append(copy(tokens_in, m.hidden, 10))
    for s in loads:
        s.start()
    grad_context = m.act.at[3]

    def context_back(i):
        grad_context[tile(i, TM), :] = mm_nt(m.x[tile(i, TM), :], w_out[...]).astype(BF16)

    loop(tiles, context_back)
    turn(m.ctx, m.turned)

    def grad_out(i):
        at = pl.ds(pl.multiple_of(i * TM + 3 * D, TM), TM)
        m.up[at, :] = mm(m.turned[tile(i, TM), :], m.x[...]).astype(BF16)

    loop(D // TM, grad_out)
    for s in loads:
        s.wait()
    turn(m.hidden, m.turned)
    grads = [m.act.at[j] for j in range(3)]
    for row in range(rows_total):
        starts, lens = row_blocks(bucket, length, row)
        write_mask(m.mask, starts, lens)
        for part in range(2):
            net.during_attention_back(row * 2 + part)
            loop(3, lambda p: attend_pair_back(queries, keys, values, m.ctx, m.logs, m.mask, grad_context, *grads, row, p + 3 * part, 256))
    for j in range(3):
        def grad_qkv(i, j=j):
            at = pl.ds(pl.multiple_of(i * TM + j * D, TM), TM)
            m.up[at, :] = mm(m.turned[tile(i, TM), :], m.act[j]).astype(BF16)
        loop(D // TM, grad_qkv)
    net.ready_attn_weights()

    def finish(i):
        rows = tile(i, TM)
        g = m.total[rows, :]
        for j, w in enumerate((w_query, w_key, w_value)):
            g = g + mm_nt(m.act[j, rows, :], w[...])
        m.total[rows, :] = g
        add_row(m.vec_grad, QB, m.act[0, rows, :].astype(F32))
        add_row(m.vec_grad, VB, m.act[2, rows, :].astype(F32))

    loop(tiles, finish)
    store_grad = copy(m.total, token_grad, 11)
    store_grad.start()
    net.ready_vec()
    store_grad.wait()


def local_kernel(bucket, length, tokens_in, out_grad_in, pool_grad, vec, w_attn, w_up, w_down,
                 layer_out, pools, token_grad, g_attn, g_up, g_down, g_vec, keep_qkv, keep_norm, *scratch):
    m = Memory(scratch)

    class Local(NoNetwork):
        def begin(self):
            m.vec[...] = vec[...]
            for src, dst in ((w_attn, m.attn), (w_up, m.up), (w_down, m.down)):
                c = pltpu.make_async_copy(src, dst, m.lsem.at[1])
                c.start()
                c.wait()

    layer_steps(m, Local(), bucket, length, tokens_in, out_grad_in, pool_grad, layer_out, pools, token_grad, keep_qkv, keep_norm)
    for src, dst in ((m.up, g_attn), (m.down, g_up), (m.spare, g_down)):
        c = pltpu.make_async_copy(src, dst, m.lsem.at[1])
        c.start()
        c.wait()
    g_vec[...] = m.vec_grad[...]


def layer_local(bucket, length, tokens, out_grad, pool_grad, vec, w_attn, w_up, w_down):
    count = tokens.shape[0]
    v, any_spec, smem = pl.BlockSpec(memory_space=pltpu.VMEM), pl.BlockSpec(memory_space=pl.ANY), pl.BlockSpec(memory_space=pltpu.SMEM)
    s = jax.ShapeDtypeStruct
    return pl.pallas_call(
        local_kernel,
        out_shape=[s((count, D), BF16), s(pool_grad.shape, F32), s((count, D), F32), s((4 * D, D), BF16), s((4 * D, D), BF16),
                   s((4 * D, D), BF16), s((16, D), F32), s((3, count, D), BF16), s((count, D), F32)],
        in_specs=[smem, smem, any_spec, any_spec, v, v, any_spec, any_spec, any_spec],
        out_specs=[any_spec, v, any_spec, any_spec, any_spec, any_spec, v, any_spec, any_spec],
        scratch_shapes=Memory.shapes(count),
        compiler_params=pltpu.CompilerParams(vmem_limit_bytes=63 * 2**20),
    )(bucket, length, tokens, out_grad, pool_grad, vec, w_attn, w_up, w_down)[:7]
def body(
    grid,
    tokens,
    block_bucket,
    lengths,
    query_weight,
    query_bias,
    key_weight,
    value_weight,
    value_bias,
    out_weight,
    out_bias,
    first_gain,
    first_shift,
    up_weight,
    up_bias,
    down_weight,
    down_bias,
    second_gain,
    second_shift,
    out_grad,
    pool_grad,
):
    rank = lax.axis_index("dp") * lax.axis_size("fsdp") + lax.axis_index("fsdp")
    dr, n, s, pad, r = grid.dev_rows, grid.nz, grid.side, grid.pad, grid.rows
    raw_attn = jnp.stack([query_weight, key_weight, value_weight, out_weight])
    raw_up = up_weight.reshape(dr, 4, D).transpose(1, 0, 2)
    raw_down = down_weight.reshape(4, dr, D)
    small = jnp.stack([query_bias, value_bias, out_bias, first_gain, first_shift, down_bias, second_gain, second_shift])
    small = lax.dynamic_update_slice(jnp.zeros((16, D), BF16), small, (0, rank * dr))
    wide = lax.dynamic_update_slice(jnp.zeros((16 * D,), BF16), up_bias, (rank * 4 * dr,)).reshape(16, D)
    raw_vec = jnp.stack([small, wide])
    w_attn, w_up, w_down, w_vec = gather_all(grid, raw_attn, raw_up, raw_down, raw_vec)
    w_attn, w_up, w_down = (w[:, :, :r].reshape(4 * D, D) for w in (w_attn, w_up, w_down))
    vec = jnp.sum(w_vec.astype(F32), axis=1)
    vec = jnp.concatenate([vec[0, :8], vec[1, :8]])
    layer_out, pools, token_grad, g_attn, g_up, g_down, g_vec = layer_local(
        block_bucket, lengths, tokens, out_grad, pool_grad, vec, w_attn, w_up, w_down)

    def blocks(grad):
        return jnp.pad(grad.reshape(-1, r, D), ((0, 0), (0, pad - r), (0, 0)))

    g_attn, g_up = (blocks(g).reshape(4, n, s, s, pad, D) for g in (g_attn, g_up))
    g_down = blocks(g_down).reshape(n, s, s, 4, pad, D)
    o_attn, o_up, o_down, o_vec = reduce_all(grid, g_attn, g_up, g_down, g_vec)
    small = lax.dynamic_slice(o_vec, (0, rank * dr), (8, dr))
    wide = lax.dynamic_slice(o_vec[8:12].reshape(4 * D), (rank * 4 * dr,), (4 * dr,))
    return (
        layer_out,
        pools,
        token_grad,
        o_attn[0],
        small[QB],
        o_attn[1],
        o_attn[2],
        small[VB],
        o_attn[3],
        small[OB],
        small[G1],
        small[S1],
        o_up.transpose(1, 0, 2).reshape(dr, 4 * D),
        wide,
        o_down.reshape(4 * dr, D),
        small[DB],
        small[G2],
        small[S2],
    )


def solution(mesh):
    whole, line = P(("dp", "fsdp"), None), P(("dp", "fsdp"))
    grid = Grid(mesh.shape["dp"], mesh.shape["fsdp"])
    return jax.shard_map(
        functools.partial(body, grid),
        mesh=mesh,
        in_specs=(
            whole, line, line, whole, line, whole, whole, line, whole, line,
            line, line, whole, line, whole, line, line, line, whole, whole,
        ),
        out_specs=(
            whole, whole, whole, whole, line, whole, whole, line, whole, line,
            line, line, whole, line, whole, line, line, line,
        ),
        check_vma=False,
    )
```

```python
import functools
import math

import jax
import jax.numpy as jnp
from jax import lax
from jax.experimental import pallas as pl
from jax.experimental.pallas import tpu as pltpu
from jax.sharding import PartitionSpec as P

MESH = pl.DeviceIdType.MESH
D = 768
F32 = jnp.float32
BF16 = jnp.bfloat16


class Grid:
    def __init__(self, nz, nf):
        self.nz = nz
        self.side = math.isqrt(nf // 2)
        assert 2 * self.side * self.side == nf
        self.chips = nz * self.side * self.side
        self.rows = D // self.chips
        self.dev_rows = self.rows // 2
        self.pad = -(-self.rows // 16) * 16

    def place(self):
        s = self.side
        self.z = lax.axis_index("dp")
        f = lax.axis_index("fsdp")
        self.core = lax.rem(f, 2)
        self.lo = lax.rem(f // 2, s)
        self.hi = f // (2 * s)

    def dev(self, z, hi, lo, core):
        return (z, (hi * self.side + lo) * 2 + core)

    def sib(self):
        return self.dev(self.z, self.hi, self.lo, 1 - self.core)

    def zs(self, d):
        return lax.rem(self.z + d, self.nz)

    def los(self, d):
        return lax.rem(self.lo + d, self.side)

    def his(self, d):
        return lax.rem(self.hi + d, self.side)

    def z_peer(self, d):
        return self.dev(self.zs(d), self.hi, self.lo, self.core)

    def lo_peer(self, d):
        return self.dev(self.z, self.hi, self.los(d), self.core)

    def hi_peer(self, d):
        return self.dev(self.z, self.his(d), self.lo, self.core)

    def chip(self, z, hi, lo):
        return (z * self.side + hi) * self.side + lo

    def peers(self):
        out = [self.sib()]
        out += [self.z_peer(d) for d in range(1, self.nz)]
        out += [self.lo_peer(d) for d in range(1, self.side)]
        out += [self.hi_peer(d) for d in range(1, self.side)]
        return out

    def barrier(self):
        sem = pltpu.get_barrier_semaphore()
        peers = self.peers()
        for peer in peers:
            pl.semaphore_signal(sem, inc=1, device_id=peer, device_id_type=MESH)
        pl.semaphore_wait(sem, len(peers))


class Sender:
    def __init__(self, sems):
        self.sems = sems
        self.started = []

    def start(self, src, dst, recv_sem, device):
        copy = pltpu.make_async_remote_copy(
            src_ref=src,
            dst_ref=dst,
            send_sem=self.sems.at[len(self.started)],
            recv_sem=recv_sem,
            device_id=device,
            device_id_type=MESH,
        )
        copy.start()
        self.started.append(copy)
        return copy

    def arrived(self, dst, recv_sem, grid):
        pltpu.make_async_remote_copy(
            src_ref=dst,
            dst_ref=dst,
            send_sem=self.sems.at[0],
            recv_sem=recv_sem,
            device_id=grid.sib(),
            device_id_type=MESH,
        ).wait_recv()

    def finish(self):
        for copy in self.started:
            copy.wait_send()


class Gather:
    def __init__(self, grid, sender, at, sem, per_core=2):
        self.grid, self.sender, self.at, self.sem = grid, sender, at, sem
        self.per_core = per_core

    def mine(self, jj):
        return self.grid.core * self.per_core + jj

    def send(self, j, p, device):
        self.sender.start(self.at(j, p), self.at(j, p), self.sem(j, p), device)

    def wait(self, j, p):
        self.sender.arrived(self.at(j, p), self.sem(j, p), self.grid)

    def own(self):
        g = self.grid
        for jj in range(self.per_core):
            j, p = self.mine(jj), g.chip(g.z, g.hi, g.lo)
            for d in range(1, g.nz):
                self.send(j, p, g.z_peer(d))
            self.spread(j, p)

    def spread(self, j, p):
        g = self.grid
        for d in range(1, g.side):
            self.send(j, p, g.lo_peer(d))
        for d in range(1, g.side):
            self.send(j, p, g.hi_peer(d))
        self.send(j, p, g.sib())

    def along_z(self, d):
        g = self.grid
        for jj in range(self.per_core):
            j, p = self.mine(jj), g.chip(g.zs(d), g.hi, g.lo)
            self.wait(j, p)
            self.spread(j, p)

    def second(self, d):
        g = self.grid
        for jj in range(self.per_core):
            j = self.mine(jj)
            for e in range(1, g.side):
                if jj % 2 == 0:
                    p = g.chip(g.zs(d), g.hi, g.los(e))
                else:
                    p = g.chip(g.zs(d), g.his(e), g.lo)
                self.wait(j, p)
                for k in range(1, g.side):
                    self.send(j, p, g.hi_peer(k) if jj % 2 == 0 else g.lo_peer(k))
                self.send(j, p, g.sib())

    def third(self, d):
        g = self.grid
        for jj in range(self.per_core):
            j = self.mine(jj)
            for e in range(1, g.side):
                for k in range(g.side):
                    if jj % 2 == 0:
                        p = g.chip(g.zs(d), g.his(e), g.los(k))
                    else:
                        p = g.chip(g.zs(d), g.his(k), g.los(e))
                    self.wait(j, p)
                    self.send(j, p, g.sib())

    def sibling(self):
        g = self.grid
        for jj in range(self.per_core):
            j = (1 - g.core) * self.per_core + jj
            for d in range(g.nz):
                for e in range(g.side):
                    for k in range(g.side):
                        self.wait(j, g.chip(g.zs(d), g.his(e), g.los(k)))

    @staticmethod
    def sends(grid, per_core):
        n, s = grid.nz, grid.side
        return per_core * (n - 1 + n * (s - 1) + n * s * (s - 1) + grid.chips)


def join_rows(grid, low, high):
    parts = [low.astype(F32), high.astype(F32)]
    if grid.pad != grid.rows:
        parts.append(jnp.zeros((grid.pad - grid.rows, low.shape[1]), F32))
    return jnp.concatenate(parts, axis=0).astype(BF16)


def gather_kernel(grid, attn_ref, up_ref, down_ref, vec_ref, w_attn, w_up, w_down, w_vec,
                  pre_ref, pre_vec, stage, stage_vec, rsem, vsem, ssem, psem, lsem):
    grid.place()
    grid.barrier()
    sender = Sender(ssem)
    c = grid.core
    me = grid.chip(grid.z, grid.hi, grid.lo)
    raws = (attn_ref, up_ref)
    for g, raw in enumerate(raws):
        for jj in range(2):
            sender.start(raw.at[(1 - c) * 2 + jj], pre_ref.at[g, jj], psem.at[g, jj], grid.sib())
    sender.start(vec_ref.at[1 - c], pre_vec, psem.at[2, 0], grid.sib())

    groups = [
        Gather(grid, sender, lambda j, p: w_attn.at[j, p], lambda j, p: rsem.at[0, j, p]),
        Gather(grid, sender, lambda j, p: w_up.at[j, p], lambda j, p: rsem.at[1, j, p]),
        Gather(grid, sender, lambda j, p: w_down.at[p, j], lambda j, p: rsem.at[2, j, p]),
    ]
    vec = Gather(grid, sender, lambda j, p: w_vec.at[j, p], lambda j, p: vsem.at[j, p], per_core=1)

    def put(src, dst, k):
        copy = pltpu.make_async_copy(src, dst, lsem.at[k])
        copy.start()
        copy.wait()

    def assemble(g):
        for jj in range(2):
            if g < 2:
                sender.arrived(pre_ref.at[g, jj], psem.at[g, jj], grid)
                own, other = raws[g][c * 2 + jj], pre_ref[g, jj]
                first = jnp.where(c == 0, own.astype(F32), other.astype(F32))
                last = jnp.where(c == 0, other.astype(F32), own.astype(F32))
            else:
                first, last = down_ref[2 * jj], down_ref[2 * jj + 1]
            stage[jj] = join_rows(grid, first, last)
            put(stage.at[jj], groups[g].at(c * 2 + jj, me), 0)

    assemble(0)
    groups[0].own()
    sender.arrived(pre_vec, psem.at[2, 0], grid)
    stage_vec[...] = (vec_ref[c].astype(F32) + pre_vec[...].astype(F32)).astype(BF16)
    put(stage_vec, w_vec.at[c, me], 0)
    vec.own()
    def z_steps(g):
        for d in range(grid.nz - 1, 0, -1):
            g.along_z(d)

    def second_steps(g):
        for d in range(grid.nz, 0, -1):
            g.second(d)

    def third_steps(g):
        for d in range(grid.nz, 0, -1):
            g.third(d)

    z_steps(vec)
    z_steps(groups[0])
    assemble(1)
    groups[1].own()
    second_steps(vec)
    second_steps(groups[0])
    z_steps(groups[1])
    assemble(2)
    groups[2].own()
    third_steps(vec)
    third_steps(groups[0])
    second_steps(groups[1])
    z_steps(groups[2])
    third_steps(groups[1])
    second_steps(groups[2])
    third_steps(groups[2])
    for g in [vec] + groups:
        g.sibling()
    sender.finish()


def gather_all(grid, raw_attn, raw_up, raw_down, raw_vec):
    n, pad, dr = grid.chips, grid.pad, grid.dev_rows
    nsend = 5 + 3 * Gather.sends(grid, 2) + Gather.sends(grid, 1)
    any_spec = pl.BlockSpec(memory_space=pl.ANY)
    vmem = pl.BlockSpec(memory_space=pltpu.VMEM)
    return pl.pallas_call(
        functools.partial(gather_kernel, grid),
        out_shape=[
            jax.ShapeDtypeStruct((4, n, pad, D), BF16),
            jax.ShapeDtypeStruct((4, n, pad, D), BF16),
            jax.ShapeDtypeStruct((n, 4, pad, D), BF16),
            jax.ShapeDtypeStruct((2, n, 16, D), BF16),
        ],
        in_specs=[vmem] * 4,
        out_specs=[any_spec] * 4,
        scratch_shapes=[
            pltpu.VMEM((2, 2, dr, D), BF16),
            pltpu.VMEM((16, D), BF16),
            pltpu.VMEM((2, pad, D), BF16),
            pltpu.VMEM((16, D), BF16),
            pltpu.SemaphoreType.DMA((3, 4, n)),
            pltpu.SemaphoreType.DMA((2, n)),
            pltpu.SemaphoreType.DMA((nsend,)),
            pltpu.SemaphoreType.DMA((3, 2)),
            pltpu.SemaphoreType.DMA((1,)),
        ],
        compiler_params=pltpu.CompilerParams(collective_id=0, has_side_effects=True, vmem_limit_bytes=32 * 2**20),
    )(raw_attn, raw_up, raw_down, raw_vec)
class Reduce:
    def __init__(self, grid, sender, part, held, second, third, last, sems):
        self.grid, self.sender, self.part = grid, sender, part
        self.held, self.from_second, self.from_third, self.from_z = held, second, third, last
        self.sem_sib, self.sem_second, self.sem_third, self.sem_z = sems

    def to_sibling(self, d):
        g = self.grid
        z = g.zs(d)
        for jj in range(2):
            j = (1 - g.core) * 2 + jj
            self.sender.start(self.part(j, z), self.held.at[jj, z], self.sem_sib.at[jj, z], g.sib())

    def add_sibling(self, d):
        g, s = self.grid, self.grid.side
        z = g.zs(d)
        for jj in range(2):
            held = self.held.at[jj, z]
            self.sender.arrived(held, self.sem_sib.at[jj, z], g)
            own = self.part(g.core * 2 + jj, z)
            for h in range(s):
                def add(l, carry, h=h):
                    held[h, l] = (held[h, l].astype(F32) + own[h, l].astype(F32)).astype(BF16)
                    return carry
                lax.fori_loop(0, s, add, 0)
            for k in range(1, s):
                if jj % 2 == 0:
                    src, peer = held.at[g.his(k)], g.hi_peer(k)
                else:
                    src, peer = held.at[:, g.los(k)], g.lo_peer(k)
                self.sender.start(src, self.from_second.at[jj, s - k - 1, z], self.sem_second.at[jj, s - k - 1, z], peer)

    def add_second(self, d):
        g, s = self.grid, self.grid.side
        z = g.zs(d)
        for jj in range(2):
            for k in range(s - 1):
                self.sender.arrived(self.from_second.at[jj, k, z], self.sem_second.at[jj, k, z], g)
            for e in range(s):
                at = self.held.at[jj, z, g.hi, e] if jj % 2 == 0 else self.held.at[jj, z, e, g.lo]
                total = at[...].astype(F32)
                for k in range(s - 1):
                    total = total + self.from_second[jj, k, z, e].astype(F32)
                at[...] = total.astype(BF16)
            for k in range(1, s):
                if jj % 2 == 0:
                    src, peer = self.held.at[jj, z, g.hi, g.los(k)], g.lo_peer(k)
                else:
                    src, peer = self.held.at[jj, z, g.his(k), g.lo], g.hi_peer(k)
                self.sender.start(src, self.from_third.at[jj, s - k - 1, z], self.sem_third.at[jj, s - k - 1, z], peer)

    def own(self, jj, z):
        g, s = self.grid, self.grid.side
        for k in range(s - 1):
            self.sender.arrived(self.from_third.at[jj, k, z], self.sem_third.at[jj, k, z], g)
        total = self.held[jj, z, g.hi, g.lo].astype(F32)
        for k in range(s - 1):
            total = total + self.from_third[jj, k, z].astype(F32)
        return total

    def add_third(self, d):
        g = self.grid
        z = g.zs(d)
        for jj in range(2):
            at = self.held.at[jj, z, g.hi, g.lo]
            at[...] = self.own(jj, z).astype(BF16)
            self.sender.start(at, self.from_z.at[jj, g.nz - d - 1], self.sem_z.at[jj, g.nz - d - 1], g.z_peer(d))

    def result(self, jj):
        g = self.grid
        total = self.own(jj, g.z)
        for k in range(g.nz - 1):
            self.sender.arrived(self.from_z.at[jj, k], self.sem_z.at[jj, k], g)
            total = total + self.from_z[jj, k].astype(F32)
        return total

    @staticmethod
    def sends(grid):
        n, s = grid.nz, grid.side
        return 2 * (n + n * (s - 1) * 2 + n - 1)

    @staticmethod
    def scratch(grid, groups):
        n, s, pad = grid.nz, grid.side, grid.pad
        return [
            pltpu.VMEM((groups, 2, n, s, s, pad, D), BF16),
            pltpu.VMEM((groups, 2, s - 1, n, s, pad, D), BF16),
            pltpu.VMEM((groups, 2, s - 1, n, pad, D), BF16),
            pltpu.VMEM((groups, 2, n - 1, pad, D), BF16),
            pltpu.SemaphoreType.DMA((groups, 2, n)),
            pltpu.SemaphoreType.DMA((groups, 2, s - 1, n)),
            pltpu.SemaphoreType.DMA((groups, 2, s - 1, n)),
            pltpu.SemaphoreType.DMA((groups, 2, n - 1)),
        ]


def sum_everywhere(grid, sender, own, landing, sem):
    steps = [[grid.sib()],
             [grid.lo_peer(d) for d in range(1, grid.side)],
             [grid.hi_peer(d) for d in range(1, grid.side)],
             [grid.z_peer(d) for d in range(1, grid.nz)]]
    slot = 0
    for n, peers in enumerate(steps):
        for k, peer in enumerate(peers):
            sender.start(own.at[n], landing.at[slot + len(peers) - 1 - k], sem.at[slot + len(peers) - 1 - k], peer)
        total = own[n]
        for k in range(len(peers)):
            sender.arrived(landing.at[slot + k], sem.at[slot + k], grid)
            total = total + landing[slot + k]
        slot += len(peers)
        own[n + 1] = total


def peer_count(grid):
    return 1 + 2 * (grid.side - 1) + grid.nz - 1


def reduce_kernel(grid, g_attn, g_up, g_down, g_vec, o_attn, o_up, o_down, o_vec,
                  held, second, third, last, s1, s2, s3, s4, swap_out, swap_in, wsem, vec, vec_in, vsem, ssem):
    grid.place()
    grid.barrier()
    sender = Sender(ssem)
    c = grid.core
    parts = [lambda j, z: g_attn.at[j, z], lambda j, z: g_up.at[j, z], lambda j, z: g_down.at[z, :, :, j]]
    groups = [
        Reduce(grid, sender, parts[g], held.at[g], second.at[g], third.at[g], last.at[g],
               (s1.at[g], s2.at[g], s3.at[g], s4.at[g]))
        for g in range(3)
    ]
    order = [groups[2], groups[1], groups[0]]
    n = grid.nz
    for g in order:
        for d in range(n, 0, -1):
            g.to_sibling(d)
    vec[0] = g_vec[...]
    for g in order:
        for d in range(n, 0, -1):
            g.add_sibling(d)
    for g in order:
        for d in range(n, 0, -1):
            g.add_second(d)
    for g in order:
        for d in range(n - 1, 0, -1):
            g.add_third(d)
    sum_everywhere(grid, sender, vec, vec_in, vsem)
    o_vec[...] = vec[4]
    r, dr = grid.rows, grid.dev_rows
    for i, (g, out) in enumerate(((groups[1], o_up), (groups[0], o_attn))):
        for jj in range(2):
            total = g.result(jj)
            top, bottom = total[:dr], total[dr:r]
            out[c * 2 + jj] = jnp.where(c == 0, top, bottom)
            swap_out[i, jj] = jnp.where(c == 0, bottom, top)
            sender.start(swap_out.at[i, jj], swap_in.at[i, jj], wsem.at[i, jj], grid.sib())
    for jj in range(2):
        o_down[jj] = groups[2].result(jj)[:r]
    for i, out in enumerate((o_up, o_attn)):
        for jj in range(2):
            sender.arrived(swap_in.at[i, jj], wsem.at[i, jj], grid)
            out[(1 - c) * 2 + jj] = swap_in[i, jj]
    sender.finish()


def reduce_all(grid, g_attn, g_up, g_down, g_vec):
    n, s, pad, dr = grid.nz, grid.side, grid.pad, grid.dev_rows
    nsend = 3 * Reduce.sends(grid) + 4 + peer_count(grid)
    vmem = pl.BlockSpec(memory_space=pltpu.VMEM)
    return pl.pallas_call(
        functools.partial(reduce_kernel, grid),
        out_shape=[
            jax.ShapeDtypeStruct((4, dr, D), F32),
            jax.ShapeDtypeStruct((4, dr, D), F32),
            jax.ShapeDtypeStruct((2, grid.rows, D), F32),
            jax.ShapeDtypeStruct((16, D), F32),
        ],
        in_specs=[vmem] * 4,
        out_specs=[vmem] * 4,
        scratch_shapes=Reduce.scratch(grid, 3) + [
            pltpu.VMEM((2, 2, dr, D), F32),
            pltpu.VMEM((2, 2, dr, D), F32),
            pltpu.SemaphoreType.DMA((2, 2)),
            pltpu.VMEM((5, 16, D), F32),
            pltpu.VMEM((peer_count(grid), 16, D), F32),
            pltpu.SemaphoreType.DMA((peer_count(grid),)),
            pltpu.SemaphoreType.DMA((nsend,)),
        ],
        compiler_params=pltpu.CompilerParams(collective_id=1, has_side_effects=True, vmem_limit_bytes=56 * 2**20),
    )(g_attn, g_up, g_down, g_vec)
HEADS = 12
HD = 64
ROW = 512
BLOCK = 64
PER_ROW = ROW // BLOCK
NEG = -1e30
TM = 256


def mm(a, b):
    return jnp.dot(a, b, preferred_element_type=F32)


def mm_nt(a, b):
    return lax.dot_general(a, b, (((1,), (1,)), ((), ())), preferred_element_type=F32)


def mm_tn(a, b):
    return lax.dot_general(a, b, (((0,), (0,)), ((), ())), preferred_element_type=F32)


def tile(i, size):
    return pl.ds(pl.multiple_of(i * size, size), size)


def loop(n, f):
    def step(i, carry):
        f(i)
        return carry
    lax.fori_loop(0, n, step, 0)


def row_blocks(bucket_ref, length_ref, row):
    starts, lens = [], []
    for b in range(PER_ROW):
        stride = bucket_ref[row * PER_ROW + b] // BLOCK
        first = b // stride * stride
        starts.append(first)
        lens.append(length_ref[row * PER_ROW + first])
    return starts, lens


def pick(ids, values):
    out = jnp.zeros_like(ids)
    for b, value in enumerate(values):
        out = jnp.where(ids == b, value, out)
    return out


def write_mask(mask_ref, starts, lens):
    query = pick(lax.broadcasted_iota(jnp.int32, (BLOCK, ROW), 1) // BLOCK, starts)
    place = lax.broadcasted_iota(jnp.int32, (BLOCK, ROW), 0)
    for b in range(PER_ROW):
        limit = lens[b] - (b - starts[b]) * BLOCK
        allowed = (query == starts[b]) & (place < limit)
        mask_ref[b * BLOCK : (b + 1) * BLOCK, :] = jnp.where(allowed, 0.0, NEG)


def member_matrix(starts, lens):
    lane = lax.broadcasted_iota(jnp.int32, (PER_ROW, ROW), 1)
    token_start = pick(lane // BLOCK, starts)
    token_len = pick(lane // BLOCK, lens)
    valid = lane - token_start * BLOCK < token_len
    block = lax.broadcasted_iota(jnp.int32, (PER_ROW, ROW), 0)
    member = jnp.where((token_start == pick(block, starts)) & valid, 1.0, 0.0).astype(F32)
    lens_col = pick(lax.broadcasted_iota(jnp.int32, (PER_ROW, 1), 0), lens)
    return member, 1.0 / lens_col.astype(F32)


def layer_norm_parts(v):
    center = v - jnp.mean(v, axis=-1, keepdims=True)
    spread = jnp.mean(center * center, axis=-1, keepdims=True)
    scale = lax.rsqrt(spread + 1e-05)
    return center * scale, scale


def layer_norm_back(grad, normed, scale, gain):
    g = grad * gain
    return scale * (g - jnp.mean(g, axis=-1, keepdims=True) - normed * jnp.mean(g * normed, axis=-1, keepdims=True))


def gelu_both(x):
    z = jnp.abs(x) * 0.7071067811865476
    t = 1.0 / (1.0 + 0.3275911 * z)
    e = jnp.exp(x * x * -0.5)
    poly = ((((1.061405429 * t - 1.453152027) * t + 1.421413741) * t - 0.284496736) * t + 0.254829592) * t
    tail = 0.5 * poly * e
    phi = jnp.where(x < 0, tail, 1.0 - tail)
    return x * phi, phi + x * e * 0.3989422804014327


def project(tokens, weight, out, bias=None, scale=None):
    def step(i):
        r = mm(tokens[tile(i, TM), :], weight)
        if bias is not None:
            r = r + bias
        r = r.astype(BF16)
        if scale is not None:
            r = (r.astype(F32) * scale).astype(BF16)
        out[tile(i, TM), :] = r
    loop(tokens.shape[0] // TM, step)


def half(shape, axis, h):
    return lax.broadcasted_iota(jnp.int32, shape, axis) // HD == h


def attend_pair(queries, keys, values, context, logs, mask, row, pair, chunk=256):
    rows, cols = pl.ds(row * ROW, ROW), tile(pair, 2 * HD)
    key_slab, value_slab = keys[rows, cols], values[rows, cols]
    value_turned = value_slab.astype(F32).T.astype(BF16)
    only = [jnp.where(half((ROW, 2 * HD), 1, h), key_slab.astype(F32), 0.0).astype(BF16) for h in range(2)]
    for c in range(ROW // chunk):
        query_slab = queries[pl.ds(row * ROW + c * chunk, chunk), cols]
        parts = []
        for h in range(2):
            s = mm_nt(only[h], query_slab) + mask[:, c * chunk : (c + 1) * chunk]
            peak = jnp.max(s, axis=0, keepdims=True)
            e = jnp.exp(s - peak)
            total = jnp.sum(e, axis=0, keepdims=True)
            logs[row, pair, h : h + 1, c * chunk : (c + 1) * chunk] = peak + jnp.log(total)
            parts.append(mm(value_turned, e.astype(BF16)) * (1.0 / total))
        turned = jnp.where(half((2 * HD, chunk), 0, 0), parts[0], parts[1])
        context[pl.ds(row * ROW + c * chunk, chunk), cols] = turned.T.astype(BF16)


def attend_pair_back(queries, keys, values, context, logs, mask, grad_context, grad_q, grad_k, grad_v, row, pair, chunk=256):
    rows, cols = pl.ds(row * ROW, ROW), tile(pair, 2 * HD)
    key_slab, value_slab = keys[rows, cols], values[rows, cols]
    key_turned = key_slab.astype(F32).T.astype(BF16)
    lane = [half((ROW, 2 * HD), 1, h) for h in range(2)]
    only_k = [jnp.where(lane[h], key_slab.astype(F32), 0.0).astype(BF16) for h in range(2)]
    only_v = [jnp.where(lane[h], value_slab.astype(F32), 0.0).astype(BF16) for h in range(2)]
    sums = []
    for c in range(ROW // chunk):
        part = pl.ds(row * ROW + c * chunk, chunk)
        query_slab, grad_slab = queries[part, cols], grad_context[part, cols]
        dot = (grad_slab.astype(F32) * context[part, cols].astype(F32)).T
        gq, gk, gv = [], [], []
        for h in range(2):
            delta = jnp.sum(dot[h * HD : (h + 1) * HD], axis=0, keepdims=True)
            s = mm_nt(only_k[h], query_slab) + mask[:, c * chunk : (c + 1) * chunk]
            p = jnp.exp(s - logs[row, pair, h : h + 1, c * chunk : (c + 1) * chunk])
            gp = mm_nt(only_v[h], grad_slab)
            gs = (p * (gp - delta)).astype(BF16)
            gv.append(mm(p.astype(BF16), grad_slab))
            gk.append(mm(gs, query_slab))
            gq.append(mm(key_turned, gs))
        turned = jnp.where(half((2 * HD, chunk), 0, 0), gq[0], gq[1]) * 0.125
        grad_q[part, cols] = turned.T.astype(BF16)
        now = (jnp.where(lane[0], gk[0], gk[1]), jnp.where(lane[0], gv[0], gv[1]))
        sums = now if c == 0 else tuple(a + b for a, b in zip(sums, now))
    grad_k[rows, cols] = sums[0].astype(BF16)
    grad_v[rows, cols] = sums[1].astype(BF16)


def attend_pair_rows(queries, keys, values, context, logs, mask, row, pair, chunk=256):
    rows, cols = pl.ds(row * ROW, ROW), tile(pair, 2 * HD)
    key_slab, value_slab = keys[rows, cols], values[rows, cols]
    for c in range(ROW // chunk):
        part = pl.ds(row * ROW + c * chunk, chunk)
        query_slab = queries[part, cols]
        parts, cols_log = [], []
        lane = [half((chunk, 2 * HD), 1, h) for h in range(2)]
        for h in range(2):
            only = jnp.where(lane[h], query_slab.astype(F32), 0.0).astype(BF16)
            s = mm_nt(only, key_slab) + mask[c * chunk : (c + 1) * chunk, :]
            peak = jnp.max(s, axis=1, keepdims=True)
            e = jnp.exp(s - peak)
            total = jnp.sum(e, axis=1, keepdims=True)
            cols_log.append(peak + jnp.log(total))
            parts.append(mm(e.astype(BF16), value_slab) * (1.0 / total))
        context[part, cols] = jnp.where(lane[0], parts[0], parts[1]).astype(BF16)
        both = jnp.where(lane[0], cols_log[0], cols_log[1]).T
        for h in range(2):
            logs[row, pair, h : h + 1, c * chunk : (c + 1) * chunk] = both[h * HD : h * HD + 1]


QB, VB, OB, G1, S1, DB, G2, S2 = range(8)
UB = 8


def after_attention(tokens, context, w_out, vec, normed, scale, hidden, i, tm):
    rows = tile(i, tm)
    first = tokens[rows, :].astype(F32) + mm(context[rows, :], w_out) + vec[OB : OB + 1, :]
    n, r = layer_norm_parts(first)
    normed[rows, :] = n
    scale[rows, :64] = jnp.broadcast_to(r, (tm, 64))
    hidden[rows, :] = (n * vec[G1 : G1 + 1, :] + vec[S1 : S1 + 1, :]).astype(BF16)


WIDTHS = (D, 2 * D // 3, D // 3, D // 6, D // 12)


def split_low(x):
    high = x.astype(BF16)
    return high, (x - high.astype(F32)).astype(BF16)


def pool_row(normed, vec, layer_out, pools, pool_grad, out_grad, total, starts, lens, row):
    rows = pl.ds(row * ROW, ROW)
    member, inverse = member_matrix(starts, lens)
    member = member.astype(BF16)
    outputs = normed[rows, :] * vec[G2 : G2 + 1, :] + vec[S2 : S2 + 1, :]
    layer_out[rows, :] = outputs.astype(BF16)
    high, low = split_low(outputs)
    avg = (mm(member, high) + mm(member, low)) * inverse
    square = avg * avg
    blocks = pl.ds(row * PER_ROW, PER_ROW)
    grad = None
    at = 0
    for width in WIDTHS:
        r = lax.rsqrt(jnp.sum(square[:, :width], axis=-1, keepdims=True) / width + 1e-06)
        lead = avg[:, :width]
        pools[blocks, at : at + width] = lead * r
        g = pool_grad[blocks, at : at + width]
        back = g * r - lead * (r * r * r * (jnp.sum(g * lead, axis=-1, keepdims=True) / width))
        if width % 128:
            wide = -(-width // 128) * 128
            back = jnp.concatenate([back, jnp.zeros((PER_ROW, wide - width), F32)], axis=1)
        if grad is None:
            grad = back
        else:
            grad = jnp.concatenate([grad[:, : back.shape[1]] + back, grad[:, back.shape[1] :]], axis=1)
        at += width
    high, low = split_low(grad * inverse)
    both = jnp.concatenate([high, low], axis=0)
    total[rows, :] = out_grad[rows, :].astype(F32) + mm_tn(jnp.concatenate([member, member], axis=0), both)


def add_row(vec_grad, k, values):
    vec_grad[k : k + 1, :] += jnp.sum(values, axis=0, keepdims=True)


def second_norm_back(total, normed, scale, vec, vec_grad, branch, i, tm):
    rows = tile(i, tm)
    g, n = total[rows, :], normed[rows, :]
    add_row(vec_grad, G2, g * n)
    add_row(vec_grad, S2, g)
    back = layer_norm_back(g, n, scale[rows, 64:65], vec[G2 : G2 + 1, :])
    total[rows, :] = back
    low = back.astype(BF16)
    branch[rows, :] = low
    add_row(vec_grad, DB, low.astype(F32))


def turn(x, out, tm=256):
    for i in range(x.shape[0] // tm):
        for j in range(x.shape[1] // tm):
            out[j * tm : (j + 1) * tm, i * tm : (i + 1) * tm] = x[i * tm : (i + 1) * tm, j * tm : (j + 1) * tm].T
class Memory:
    NAMES = ("attn", "up", "down", "spare", "act", "slope", "x", "ctx", "hidden", "turned", "norm", "total",
             "scale", "mask", "logs", "vec", "vec_grad", "lsem")

    def __init__(self, refs):
        for name, ref in zip(self.NAMES, refs):
            setattr(self, name, ref)

    @staticmethod
    def shapes(tokens):
        v = pltpu.VMEM
        weights = [v((4 * D, D), BF16)] * 4
        return weights + [
            v((4, tokens, D), BF16), v((4, tokens, D), BF16),
            v((tokens, D), BF16), v((tokens, D), BF16), v((tokens, D), BF16), v((D, tokens), BF16),
            v((tokens, D), F32), v((tokens, D), F32), v((tokens, 128), F32),
            v((ROW, ROW), F32), v((tokens // ROW, HEADS // 2, 8, ROW), F32), v((16, D), F32), v((16, D), F32),
            pltpu.SemaphoreType.DMA((12,)),
        ]


def panel(ref, j):
    return ref.at[j * D : (j + 1) * D]


class NoNetwork:
    def __getattr__(self, name):
        return lambda *a: None


def layer_steps(m, net, bucket, length, tokens_in, out_grad_in, pool_grad, layer_out, pools, token_grad, keep_qkv, keep_norm, block=None):
    count = m.x.shape[0]
    tiles, rows_total = count // TM, count // ROW

    def copy(src, dst, k):
        return pltpu.make_async_copy(src, dst, m.lsem.at[k])

    queries, keys, values = (m.slope.at[j] for j in range(3))
    load_tokens = copy(tokens_in, m.x, 0)
    load_tokens.start()
    net.begin()
    m.vec_grad[...] = jnp.zeros_like(m.vec_grad)
    load_tokens.wait()
    net.need_attn()
    w_query, w_key, w_value, w_out = (panel(m.attn, j) for j in range(4))

    def qkv(i):
        rows = tile(i, TM)
        t = m.x[rows, :]
        q = (mm(t, w_query[...]) + m.vec[QB : QB + 1, :]).astype(BF16)
        queries[rows, :] = (q.astype(F32) * 0.125).astype(BF16)
        keys[rows, :] = mm(t, w_key[...]).astype(BF16)
        values[rows, :] = (mm(t, w_value[...]) + m.vec[VB : VB + 1, :]).astype(BF16)

    loop(tiles, qkv)
    for row in range(rows_total):
        starts, lens = row_blocks(bucket, length, row)
        write_mask(m.mask, starts, lens)
        m.mask[...] = m.mask[...].T
        for part in range(2):
            net.during_attention(row * 2 + part)
            loop(3, lambda p: attend_pair_rows(queries, keys, values, m.ctx, m.logs, m.mask, row, p + 3 * part, ROW))
    stores = [copy(m.slope.at[j], keep_qkv.at[j], 1 + j) for j in range(3)]
    for s in stores:
        s.start()
    loop(tiles, lambda i: after_attention(m.x, m.ctx, w_out[...], m.vec, m.norm, m.scale, m.hidden, i, TM))
    stores.append(copy(m.norm, keep_norm, 4))
    stores[-1].start()
    load_grad = copy(out_grad_in, m.x, 0)
    load_grad.start()
    net.need_up()
    for s in stores[:3]:
        s.wait()
    for j in range(4):
        w = panel(m.up, j)

        def feed(i, j=j, w=w):
            rows = tile(i, TM)
            value, deriv = gelu_both(mm(m.hidden[rows, :], w[...]) + m.vec[UB + j : UB + j + 1, :])
            m.act[j, rows, :] = value.astype(BF16)
            m.slope[j, rows, :] = deriv.astype(BF16)

        loop(tiles, feed)
        net.during_up(j)
    stores[3].wait()
    net.need_down()

    def down(i):
        rows = tile(i, TM)
        second = m.hidden[rows, :].astype(F32) + m.vec[DB : DB + 1, :]
        for j in range(4):
            second = second + mm(m.act[j, rows, :], panel(m.down, j)[...])
        n, r = layer_norm_parts(second)
        m.norm[rows, :] = n
        m.scale[rows, 64:] = jnp.broadcast_to(r, (TM, 64))

    loop(tiles, down)
    load_grad.wait()
    out_low = m.spare.at[:count]
    for row in range(rows_total):
        starts, lens = row_blocks(bucket, length, row)
        pool_row(m.norm, m.vec, out_low, pools, pool_grad, m.x, m.total, starts, lens, row)
    store_out = copy(out_low, layer_out, 5)
    store_out.start()
    loop(tiles, lambda i: second_norm_back(m.total, m.norm, m.scale, m.vec, m.vec_grad, m.x, i, TM))
    load_norm = copy(keep_norm, m.norm, 6)
    load_norm.start()
    store_out.wait()
    net.gathered()
    group = D // 2

    def grad_down(i):
        for j in range(4):
            part = mm_tn(m.act[j, :, tile(i, group)], m.x[...]).astype(BF16)
            if block is None:
                m.spare[pl.ds(pl.multiple_of(i * group + j * D, group), group), :] = part
            else:
                for b in range(group // block):
                    chip = (i * group + j * D) // (4 * block) + b // 4
                    at = ((b % 4) * (D // block) + chip) * block
                    m.spare[pl.ds(pl.multiple_of(at, block), block), :] = part[b * block : (b + 1) * block]

    loop(D // group, grad_down)
    net.ready_down()
    for j in range(4):
        def back(i, j=j):
            rows = tile(i, TM)
            g = (mm_nt(m.x[rows, :], panel(m.down, j)[...]) * m.slope[j, rows, :].astype(F32)).astype(BF16)
            m.slope[j, rows, :] = g
            add_row(m.vec_grad, UB + j, g.astype(F32))
        loop(tiles, back)
        net.during_back(j)
    turn(m.hidden, m.turned)
    for j in range(4):
        def grad_up(i, j=j):
            at = pl.ds(pl.multiple_of(i * TM + j * D, TM), TM)
            m.down[at, :] = mm(m.turned[tile(i, TM), :], m.slope[j]).astype(BF16)
        loop(D // TM, grad_up)
    net.ready_up()
    load_norm.wait()

    def first_back(i):
        rows = tile(i, TM)
        g = m.total[rows, :]
        for j in range(4):
            g = g + mm_nt(m.slope[j, rows, :], panel(m.up, j)[...])
        n = m.norm[rows, :]
        add_row(m.vec_grad, G1, g * n)
        add_row(m.vec_grad, S1, g)
        back = layer_norm_back(g, n, m.scale[rows, :1], m.vec[G1 : G1 + 1, :])
        m.total[rows, :] = back
        low = back.astype(BF16)
        m.x[rows, :] = low
        add_row(m.vec_grad, OB, low.astype(F32))

    loop(tiles, first_back)
    net.after_first_back()
    loads = [copy(keep_qkv.at[j], m.slope.at[j], 7 + j) for j in range(3)]
    loads.append(copy(tokens_in, m.hidden, 10))
    for s in loads:
        s.start()
    grad_context = m.act.at[3]

    def context_back(i):
        grad_context[tile(i, TM), :] = mm_nt(m.x[tile(i, TM), :], w_out[...]).astype(BF16)

    loop(tiles, context_back)
    turn(m.ctx, m.turned)

    def grad_out(i):
        at = pl.ds(pl.multiple_of(i * TM + 3 * D, TM), TM)
        m.up[at, :] = mm(m.turned[tile(i, TM), :], m.x[...]).astype(BF16)

    loop(D // TM, grad_out)
    net.after_out()
    for s in loads:
        s.wait()
    turn(m.hidden, m.turned)
    grads = [m.act.at[j] for j in range(3)]
    for row in range(rows_total):
        starts, lens = row_blocks(bucket, length, row)
        write_mask(m.mask, starts, lens)
        for part in range(2):
            net.during_attention_back(row * 2 + part)
            loop(3, lambda p: attend_pair_back(queries, keys, values, m.ctx, m.logs, m.mask, grad_context, *grads, row, p + 3 * part, 256))
    for j in range(3):
        def grad_qkv(i, j=j):
            at = pl.ds(pl.multiple_of(i * TM + j * D, TM), TM)
            m.up[at, :] = mm(m.turned[tile(i, TM), :], m.act[j]).astype(BF16)
        loop(D // TM, grad_qkv)
    net.ready_attn_weights()

    def finish(i):
        rows = tile(i, TM)
        g = m.total[rows, :]
        for j, w in enumerate((w_query, w_key, w_value)):
            g = g + mm_nt(m.act[j, rows, :], w[...])
        m.total[rows, :] = g
        add_row(m.vec_grad, QB, m.act[0, rows, :].astype(F32))
        add_row(m.vec_grad, VB, m.act[2, rows, :].astype(F32))

    loop(tiles, finish)
    store_grad = copy(m.total, token_grad, 11)
    store_grad.start()
    net.ready_vec()
    store_grad.wait()


def local_kernel(bucket, length, tokens_in, out_grad_in, pool_grad, vec, w_attn, w_up, w_down,
                 layer_out, pools, token_grad, g_attn, g_up, g_down, g_vec, keep_qkv, keep_norm, *scratch):
    m = Memory(scratch)

    class Local(NoNetwork):
        def begin(self):
            m.vec[...] = vec[...]
            for src, dst in ((w_attn, m.attn), (w_up, m.up), (w_down, m.down)):
                c = pltpu.make_async_copy(src, dst, m.lsem.at[1])
                c.start()
                c.wait()

    layer_steps(m, Local(), bucket, length, tokens_in, out_grad_in, pool_grad, layer_out, pools, token_grad, keep_qkv, keep_norm)
    for src, dst in ((m.up, g_attn), (m.down, g_up), (m.spare, g_down)):
        c = pltpu.make_async_copy(src, dst, m.lsem.at[1])
        c.start()
        c.wait()
    g_vec[...] = m.vec_grad[...]


def layer_local(bucket, length, tokens, out_grad, pool_grad, vec, w_attn, w_up, w_down):
    count = tokens.shape[0]
    v, any_spec, smem = pl.BlockSpec(memory_space=pltpu.VMEM), pl.BlockSpec(memory_space=pl.ANY), pl.BlockSpec(memory_space=pltpu.SMEM)
    s = jax.ShapeDtypeStruct
    return pl.pallas_call(
        local_kernel,
        out_shape=[s((count, D), BF16), s(pool_grad.shape, F32), s((count, D), F32), s((4 * D, D), BF16), s((4 * D, D), BF16),
                   s((4 * D, D), BF16), s((16, D), F32), s((3, count, D), BF16), s((count, D), F32)],
        in_specs=[smem, smem, any_spec, any_spec, v, v, any_spec, any_spec, any_spec],
        out_specs=[any_spec, v, any_spec, any_spec, any_spec, any_spec, v, any_spec, any_spec],
        scratch_shapes=Memory.shapes(count),
        compiler_params=pltpu.CompilerParams(vmem_limit_bytes=63 * 2**20),
    )(bucket, length, tokens, out_grad, pool_grad, vec, w_attn, w_up, w_down)[:7]
class Reduce2:
    def __init__(self, grid, sender, source, held, second, third, last, sems):
        self.grid, self.sender, self.source = grid, sender, source
        self.held, self.from_second, self.from_third, self.from_z = held, second, third, last
        self.sem_sib, self.sem_second, self.sem_third, self.sem_z = sems
        self.slab = grid.side * grid.side * grid.rows

    def part(self, j, z):
        size = self.slab
        return self.source.at[pl.ds(pl.multiple_of((j * self.grid.nz + z) * size, size), size)]

    def block(self, h, l, count=1):
        r = self.grid.rows
        return pl.ds(pl.multiple_of((h * self.grid.side + l) * r, r), count * r)

    def to_sibling(self, d, jjs=(0, 1)):
        g = self.grid
        z = g.zs(d)
        for jj in jjs:
            j = (1 - g.core) * 2 + jj
            self.sender.start(self.part(j, z), self.held.at[jj, z], self.sem_sib.at[jj, z], g.sib())

    def add_sibling(self, d):
        g, s, r = self.grid, self.grid.side, self.grid.rows
        z = g.zs(d)
        for jj in range(2):
            held = self.held.at[jj, z]
            self.sender.arrived(held, self.sem_sib.at[jj, z], g)
            own = self.part(g.core * 2 + jj, z)
            def add(b):
                at = pl.ds(pl.multiple_of(b * r, r), r)
                held[at, :] = (held[at, :].astype(F32) + own[at, :].astype(F32)).astype(BF16)
            loop(s * s, add)
            for k in range(1, s):
                peer = g.hi_peer(k) if jj % 2 == 0 else g.lo_peer(k)
                sem = self.sem_second.at[jj, s - k - 1, z]
                if jj % 2 == 0:
                    self.sender.start(held.at[self.block(g.his(k), 0, s)], self.from_second.at[jj, s - k - 1, z], sem.at[0], peer)
                else:
                    for h in range(s):
                        self.sender.start(held.at[self.block(h, g.los(k))],
                                          self.from_second.at[jj, s - k - 1, z, h * r : (h + 1) * r], sem.at[h], peer)

    def add_second(self, d):
        g, s, r = self.grid, self.grid.side, self.grid.rows
        z = g.zs(d)
        for jj in range(2):
            for k in range(s - 1):
                landing, sem = self.from_second.at[jj, k, z], self.sem_second.at[jj, k, z]
                if jj % 2 == 0:
                    self.sender.arrived(landing, sem.at[0], g)
                else:
                    for h in range(s):
                        self.sender.arrived(landing.at[h * r : (h + 1) * r], sem.at[h], g)
            for e in range(s):
                at = self.held.at[jj, z, self.block(g.hi, e) if jj % 2 == 0 else self.block(e, g.lo)]
                total = at[...].astype(F32)
                for k in range(s - 1):
                    total = total + self.from_second[jj, k, z, e * r : (e + 1) * r].astype(F32)
                at[...] = total.astype(BF16)
            for k in range(1, s):
                if jj % 2 == 0:
                    src, peer = self.held.at[jj, z, self.block(g.hi, g.los(k))], g.lo_peer(k)
                else:
                    src, peer = self.held.at[jj, z, self.block(g.his(k), g.lo)], g.hi_peer(k)
                self.sender.start(src, self.from_third.at[jj, s - k - 1, z], self.sem_third.at[jj, s - k - 1, z], peer)

    def own(self, jj, z):
        g, s = self.grid, self.grid.side
        for k in range(s - 1):
            self.sender.arrived(self.from_third.at[jj, k, z], self.sem_third.at[jj, k, z], g)
        total = self.held[jj, z, self.block(g.hi, g.lo)].astype(F32)
        for k in range(s - 1):
            total = total + self.from_third[jj, k, z].astype(F32)
        return total

    def add_third(self, d):
        g = self.grid
        z = g.zs(d)
        for jj in range(2):
            at = self.held.at[jj, z, self.block(g.hi, g.lo)]
            at[...] = self.own(jj, z).astype(BF16)
            self.sender.start(at, self.from_z.at[jj, g.nz - d - 1], self.sem_z.at[jj, g.nz - d - 1], g.z_peer(d))

    def result(self, jj):
        g = self.grid
        total = self.own(jj, g.z)
        for k in range(g.nz - 1):
            self.sender.arrived(self.from_z.at[jj, k], self.sem_z.at[jj, k], g)
            total = total + self.from_z[jj, k].astype(F32)
        return total

    @staticmethod
    def sends(grid):
        n, s = grid.nz, grid.side
        return 2 * n + n * (s - 1) * (1 + s) + 2 * n * (s - 1) + 2 * (n - 1)

    @staticmethod
    def scratch(grid, groups):
        n, s, r = grid.nz, grid.side, grid.rows
        return [
            pltpu.VMEM((groups, 2, n, s * s * r, D), BF16),
            pltpu.VMEM((groups, 2, s - 1, n, s * r, D), BF16),
            pltpu.VMEM((groups, 2, s - 1, n, r, D), BF16),
            pltpu.VMEM((groups, 2, n - 1, r, D), BF16),
            pltpu.SemaphoreType.DMA((groups, 2, n)),
            pltpu.SemaphoreType.DMA((groups, 2, s - 1, n, s)),
            pltpu.SemaphoreType.DMA((groups, 2, s - 1, n)),
            pltpu.SemaphoreType.DMA((groups, 2, n - 1)),
        ]


class Network:
    def __init__(self, grid, m, raws, outs, scratch):
        self.grid, self.m = grid, m
        self.attn_ref, self.up_ref, self.down_ref, self.vec_ref = raws
        self.o_attn, self.o_up, self.o_down, self.o_vec = outs
        (self.pre_ref, self.pre_vec, rsem, vsem, self.psem, ssem,
         held, second, third, last, s1, s2, s3, s4, self.swap_out, self.swap_in, self.wsem,
         self.sums, self.sums_in, self.sums_sem) = scratch
        self.sender = Sender(ssem)
        r, chips = grid.rows, grid.chips

        def at(ref, index):
            return ref.at[pl.ds(pl.multiple_of(index * r, r), r)]

        self.gathers = [
            Gather(grid, self.sender, lambda j, p: at(m.attn, j * chips + p), lambda j, p: rsem.at[0, j, p]),
            Gather(grid, self.sender, lambda j, p: at(m.up, j * chips + p), lambda j, p: rsem.at[1, j, p]),
            Gather(grid, self.sender, lambda j, p: at(m.down, p * 4 + j), lambda j, p: rsem.at[2, j, p]),
        ]
        self.vec_gather = Gather(grid, self.sender, self.vec_at, lambda j, p: vsem.at[j, p], per_core=1)
        self.reduces = [
            Reduce2(grid, self.sender, src, held.at[g], second.at[g], third.at[g], last.at[g],
                    (s1.at[g], s2.at[g], s3.at[g], s4.at[g]))
            for g, src in enumerate((m.up, m.down, m.spare))
        ]

    def vec_at(self, j, p):
        base = self.m.x.shape[0]
        return self.m.spare.at[pl.ds(pl.multiple_of(base + (j * self.grid.chips + p) * 16, 16), 16)]

    def assemble(self, g):
        grid, c = self.grid, self.grid.core
        for jj in range(2):
            if g < 2:
                self.sender.arrived(self.pre_ref.at[g, jj], self.psem.at[g, jj], grid)
                own, other = (self.attn_ref, self.up_ref)[g][c * 2 + jj].astype(F32), self.pre_ref[g, jj].astype(F32)
                first, last = jnp.where(c == 0, own, other), jnp.where(c == 0, other, own)
            else:
                first, last = self.down_ref[2 * jj].astype(F32), self.down_ref[2 * jj + 1].astype(F32)
            place = self.gathers[g].at(c * 2 + jj, grid.chip(grid.z, grid.hi, grid.lo))
            place[...] = jnp.concatenate([first, last], axis=0).astype(BF16)

    def z_steps(self, g):
        for d in range(self.grid.nz - 1, 0, -1):
            g.along_z(d)

    def second_steps(self, g):
        for d in range(self.grid.nz, 0, -1):
            g.second(d)

    def third_steps(self, g):
        for d in range(self.grid.nz, 0, -1):
            g.third(d)

    def begin(self):
        grid, c = self.grid, self.grid.core
        grid.barrier()
        for g, raw in enumerate((self.attn_ref, self.up_ref)):
            for jj in range(2):
                self.sender.start(raw.at[(1 - c) * 2 + jj], self.pre_ref.at[g, jj], self.psem.at[g, jj], grid.sib())
        self.sender.start(self.vec_ref.at[1 - c], self.pre_vec, self.psem.at[2, 0], grid.sib())
        self.assemble(0)
        self.gathers[0].own()
        self.sender.arrived(self.pre_vec, self.psem.at[2, 0], grid)
        self.vec_at(c, grid.chip(grid.z, grid.hi, grid.lo))[...] = (self.vec_ref[c].astype(F32) + self.pre_vec[...].astype(F32)).astype(BF16)
        self.vec_gather.own()

    def need_attn(self):
        attn, up, down = self.gathers
        vec = self.vec_gather
        self.z_steps(attn)
        self.z_steps(vec)
        self.assemble(1)
        up.own()
        self.second_steps(attn)
        self.second_steps(vec)
        self.third_steps(attn)
        self.third_steps(vec)
        attn.sibling()
        vec.sibling()
        self.assemble(2)
        for half_vec in range(2):
            total = self.vec_at(half_vec, 0)[...].astype(F32)
            for p in range(1, self.grid.chips):
                total = total + self.vec_at(half_vec, p)[...].astype(F32)
            self.m.vec[half_vec * 8 : half_vec * 8 + 8] = total[:8]
        self.z_steps(up)
        down.own()

    def during_attention(self, k):
        _, up, down = self.gathers
        if k == 0:
            self.second_steps(up)
        if k == 1:
            self.z_steps(down)
        if k == 2:
            self.third_steps(up)
            self.second_steps(down)

    def need_up(self):
        self.gathers[1].sibling()

    def during_up(self, j):
        if j == 1:
            self.third_steps(self.gathers[2])

    def need_down(self):
        self.gathers[2].sibling()

    def gathered(self):
        self.sender.finish()
        self.sender.started = Started(len(self.sender.started))

    def ready_down(self):
        for d in range(self.grid.nz, 0, -1):
            self.reduces[2].to_sibling(d)

    def during_back(self, j):
        n = self.grid.nz
        for d in range(n - j * n // 4, n - (j + 1) * n // 4, -1):
            self.reduces[2].add_sibling(d)

    def ready_up(self):
        for d in range(self.grid.nz, 0, -1):
            self.reduces[1].to_sibling(d)

    def after_first_back(self):
        for d in range(self.grid.nz, 0, -1):
            self.reduces[1].add_sibling(d)

    def after_out(self):
        for d in range(self.grid.nz, 0, -1):
            self.reduces[2].add_second(d)

    def during_attention_back(self, k):
        n = self.grid.nz
        if k == 1:
            for d in range(n, 0, -1):
                self.reduces[1].add_second(d)
            for d in range(n - 1, 0, -1):
                self.reduces[2].add_third(d)
        if k == 3:
            for d in range(n - 1, 0, -1):
                self.reduces[1].add_third(d)

    def ready_attn_weights(self):
        for d in range(self.grid.nz, 0, -1):
            self.reduces[0].to_sibling(d)

    def during_finish(self, i):
        pass

    def ready_vec(self):
        grid, n, c = self.grid, self.grid.nz, self.grid.core
        attn, up, down = self.reduces
        for d in range(n, 0, -1):
            attn.add_sibling(d)
        r, dr = grid.rows, grid.dev_rows
        for jj in range(2):
            self.o_down[jj] = down.result(jj)
        self.split(0, up)
        self.sums[0] = self.m.vec_grad[...]
        for d in range(n, 0, -1):
            attn.add_second(d)
        for d in range(n - 1, 0, -1):
            attn.add_third(d)
        sum_everywhere(grid, self.sender, self.sums, self.sums_in, self.sums_sem)
        self.o_vec[...] = self.sums[4]
        self.split(1, attn)
        for i, out in enumerate((self.o_up, self.o_attn)):
            for jj in range(2):
                self.sender.arrived(self.swap_in.at[i, jj], self.wsem.at[i, jj], grid)
                out[(1 - c) * 2 + jj] = self.swap_in[i, jj]
        self.sender.finish()

    def split(self, i, reduce):
        grid, c, dr = self.grid, self.grid.core, self.grid.dev_rows
        out = (self.o_up, self.o_attn)[i]
        for jj in range(2):
            total = reduce.result(jj)
            top, bottom = total[:dr], total[dr:]
            out[c * 2 + jj] = jnp.where(c == 0, top, bottom)
            self.swap_out[i, jj] = jnp.where(c == 0, bottom, top)
            self.sender.start(self.swap_out.at[i, jj], self.swap_in.at[i, jj], self.wsem.at[i, jj], grid.sib())

    @staticmethod
    def sends(grid):
        return 5 + 3 * Gather.sends(grid, 2) + Gather.sends(grid, 1) + 3 * Reduce2.sends(grid) + 4 + peer_count(grid)

    @staticmethod
    def scratch(grid):
        chips, dr = grid.chips, grid.dev_rows
        return [
            pltpu.VMEM((2, 2, dr, D), BF16),
            pltpu.VMEM((16, D), BF16),
            pltpu.SemaphoreType.DMA((3, 4, chips)),
            pltpu.SemaphoreType.DMA((2, chips)),
            pltpu.SemaphoreType.DMA((3, 2)),
            pltpu.SemaphoreType.DMA((Network.sends(grid),)),
        ] + Reduce2.scratch(grid, 3) + [
            pltpu.VMEM((2, 2, dr, D), F32),
            pltpu.VMEM((2, 2, dr, D), F32),
            pltpu.SemaphoreType.DMA((2, 2)),
            pltpu.VMEM((5, 16, D), F32),
            pltpu.VMEM((peer_count(grid), 16, D), F32),
            pltpu.SemaphoreType.DMA((peer_count(grid),)),
        ]


class Started(list):
    def __init__(self, offset):
        super().__init__()
        self.offset = offset

    def __len__(self):
        return self.offset + super().__len__()


def fused_kernel(grid, memory, bucket, length, tokens_in, out_grad_in, pool_grad, attn_ref, up_ref, down_ref, vec_ref,
                 layer_out, pools, token_grad, o_attn, o_up, o_down, o_vec, keep_qkv, keep_norm, *scratch):
    grid.place()
    m = Memory(scratch[:memory])
    net = Network(grid, m, (attn_ref, up_ref, down_ref, vec_ref), (o_attn, o_up, o_down, o_vec), scratch[memory:])
    layer_steps(m, net, bucket, length, tokens_in, out_grad_in, pool_grad, layer_out, pools, token_grad, keep_qkv, keep_norm, grid.rows)


def layer_fused(grid, bucket, length, tokens, out_grad, pool_grad, raw_attn, raw_up, raw_down, raw_vec):
    count, dr = tokens.shape[0], grid.dev_rows
    v, any_spec, smem = pl.BlockSpec(memory_space=pltpu.VMEM), pl.BlockSpec(memory_space=pl.ANY), pl.BlockSpec(memory_space=pltpu.SMEM)
    s = jax.ShapeDtypeStruct
    memory = Memory.shapes(count)
    return pl.pallas_call(
        functools.partial(fused_kernel, grid, len(memory)),
        out_shape=[s((count, D), BF16), s(pool_grad.shape, F32), s((count, D), F32), s((4, dr, D), F32), s((4, dr, D), F32),
                   s((2, grid.rows, D), F32), s((16, D), F32), s((3, count, D), BF16), s((count, D), F32)],
        in_specs=[smem, smem, any_spec, any_spec, v, v, v, v, v],
        out_specs=[any_spec, v, any_spec, v, v, v, v, any_spec, any_spec],
        scratch_shapes=memory + Network.scratch(grid),
        compiler_params=pltpu.CompilerParams(collective_id=2, has_side_effects=True, vmem_limit_bytes=63 * 2**20),
    )(bucket, length, tokens, out_grad, pool_grad, raw_attn, raw_up, raw_down, raw_vec)[:7]
def body(
    grid,
    tokens,
    block_bucket,
    lengths,
    query_weight,
    query_bias,
    key_weight,
    value_weight,
    value_bias,
    out_weight,
    out_bias,
    first_gain,
    first_shift,
    up_weight,
    up_bias,
    down_weight,
    down_bias,
    second_gain,
    second_shift,
    out_grad,
    pool_grad,
):
    rank = lax.axis_index("dp") * lax.axis_size("fsdp") + lax.axis_index("fsdp")
    dr, n, s, pad, r = grid.dev_rows, grid.nz, grid.side, grid.pad, grid.rows
    raw_attn = jnp.stack([query_weight, key_weight, value_weight, out_weight])
    raw_up = up_weight.reshape(dr, 4, D).transpose(1, 0, 2)
    raw_down = down_weight.reshape(4, dr, D)
    small = jnp.stack([query_bias, value_bias, out_bias, first_gain, first_shift, down_bias, second_gain, second_shift])
    small = lax.dynamic_update_slice(jnp.zeros((16, D), BF16), small, (0, rank * dr))
    wide = lax.dynamic_update_slice(jnp.zeros((16 * D,), BF16), up_bias, (rank * 4 * dr,)).reshape(16, D)
    raw_vec = jnp.stack([small, wide])
    if pad == r:
        layer_out, pools, token_grad, o_attn, o_up, o_down, o_vec = layer_fused(
            grid, block_bucket, lengths, tokens, out_grad, pool_grad, raw_attn, raw_up, raw_down, raw_vec)
    else:
        w_attn, w_up, w_down, w_vec = gather_all(grid, raw_attn, raw_up, raw_down, raw_vec)
        w_attn, w_up, w_down = (w[:, :, :r].reshape(4 * D, D) for w in (w_attn, w_up, w_down))
        vec = jnp.sum(w_vec.astype(F32), axis=1)
        vec = jnp.concatenate([vec[0, :8], vec[1, :8]])
        layer_out, pools, token_grad, g_attn, g_up, g_down, g_vec = layer_local(
            block_bucket, lengths, tokens, out_grad, pool_grad, vec, w_attn, w_up, w_down)

        def blocks(grad):
            return jnp.pad(grad.reshape(-1, r, D), ((0, 0), (0, pad - r), (0, 0)))

        g_attn, g_up = (blocks(g).reshape(4, n, s, s, pad, D) for g in (g_attn, g_up))
        g_down = blocks(g_down).reshape(n, s, s, 4, pad, D)
        o_attn, o_up, o_down, o_vec = reduce_all(grid, g_attn, g_up, g_down, g_vec)
    small = lax.dynamic_slice(o_vec, (0, rank * dr), (8, dr))
    wide = lax.dynamic_slice(o_vec[8:12].reshape(4 * D), (rank * 4 * dr,), (4 * dr,))
    return (
        layer_out,
        pools,
        token_grad,
        o_attn[0],
        small[QB],
        o_attn[1],
        o_attn[2],
        small[VB],
        o_attn[3],
        small[OB],
        small[G1],
        small[S1],
        o_up.transpose(1, 0, 2).reshape(dr, 4 * D),
        wide,
        o_down.reshape(4 * dr, D),
        small[DB],
        small[G2],
        small[S2],
    )


def solution(mesh):
    whole, line = P(("dp", "fsdp"), None), P(("dp", "fsdp"))
    grid = Grid(mesh.shape["dp"], mesh.shape["fsdp"])
    return jax.shard_map(
        functools.partial(body, grid),
        mesh=mesh,
        in_specs=(
            whole, line, line, whole, line, whole, whole, line, whole, line,
            line, line, whole, line, whole, line, line, line, whole, whole,
        ),
        out_specs=(
            whole, whole, whole, whole, line, whole, whole, line, whole, line,
            line, line, whole, line, whole, line, line, line,
        ),
        check_vma=False,
    )
```

```python
import functools
import math

import jax
import jax.numpy as jnp
from jax import lax
from jax.experimental import pallas as pl
from jax.experimental.pallas import tpu as pltpu
from jax.sharding import PartitionSpec as P

MESH = pl.DeviceIdType.MESH
D = 768
F32 = jnp.float32
BF16 = jnp.bfloat16


class Grid:
    def __init__(self, nz, nf):
        self.nz = nz
        self.side = math.isqrt(nf // 2)
        assert 2 * self.side * self.side == nf
        self.chips = nz * self.side * self.side
        self.rows = D // self.chips
        self.dev_rows = self.rows // 2
        self.pad = -(-self.rows // 16) * 16

    def place(self):
        s = self.side
        self.z = lax.axis_index("dp")
        f = lax.axis_index("fsdp")
        self.core = lax.rem(f, 2)
        self.lo = lax.rem(f // 2, s)
        self.hi = f // (2 * s)

    def dev(self, z, hi, lo, core):
        return (z, (hi * self.side + lo) * 2 + core)

    def sib(self):
        return self.dev(self.z, self.hi, self.lo, 1 - self.core)

    def zs(self, d):
        return lax.rem(self.z + d, self.nz)

    def los(self, d):
        return lax.rem(self.lo + d, self.side)

    def his(self, d):
        return lax.rem(self.hi + d, self.side)

    def z_peer(self, d):
        return self.dev(self.zs(d), self.hi, self.lo, self.core)

    def lo_peer(self, d):
        return self.dev(self.z, self.hi, self.los(d), self.core)

    def hi_peer(self, d):
        return self.dev(self.z, self.his(d), self.lo, self.core)

    def chip(self, z, hi, lo):
        return (z * self.side + hi) * self.side + lo

    def peers(self):
        out = [self.sib()]
        out += [self.z_peer(d) for d in range(1, self.nz)]
        out += [self.lo_peer(d) for d in range(1, self.side)]
        out += [self.hi_peer(d) for d in range(1, self.side)]
        return out

    def barrier(self):
        sem = pltpu.get_barrier_semaphore()
        peers = self.peers()
        for peer in peers:
            pl.semaphore_signal(sem, inc=1, device_id=peer, device_id_type=MESH)
        pl.semaphore_wait(sem, len(peers))


class Sender:
    def __init__(self, sems):
        self.sems = sems
        self.started = []

    def start(self, src, dst, recv_sem, device):
        copy = pltpu.make_async_remote_copy(
            src_ref=src,
            dst_ref=dst,
            send_sem=self.sems.at[len(self.started)],
            recv_sem=recv_sem,
            device_id=device,
            device_id_type=MESH,
        )
        copy.start()
        self.started.append(copy)
        return copy

    def arrived(self, dst, recv_sem, grid):
        pltpu.make_async_remote_copy(
            src_ref=dst,
            dst_ref=dst,
            send_sem=self.sems.at[0],
            recv_sem=recv_sem,
            device_id=grid.sib(),
            device_id_type=MESH,
        ).wait_recv()

    def finish(self):
        for copy in self.started:
            copy.wait_send()


class Gather:
    def __init__(self, grid, sender, at, sem, per_core=2):
        self.grid, self.sender, self.at, self.sem = grid, sender, at, sem
        self.per_core = per_core

    def mine(self, jj):
        return self.grid.core * self.per_core + jj

    def send(self, j, p, device):
        self.sender.start(self.at(j, p), self.at(j, p), self.sem(j, p), device)

    def wait(self, j, p):
        self.sender.arrived(self.at(j, p), self.sem(j, p), self.grid)

    def own(self):
        g = self.grid
        for jj in range(self.per_core):
            j, p = self.mine(jj), g.chip(g.z, g.hi, g.lo)
            for d in range(1, g.nz):
                self.send(j, p, g.z_peer(d))
            self.spread(j, p)

    def spread(self, j, p):
        g = self.grid
        for d in range(1, g.side):
            self.send(j, p, g.lo_peer(d))
        for d in range(1, g.side):
            self.send(j, p, g.hi_peer(d))
        self.send(j, p, g.sib())

    def along_z(self, d):
        g = self.grid
        for jj in range(self.per_core):
            j, p = self.mine(jj), g.chip(g.zs(d), g.hi, g.lo)
            self.wait(j, p)
            self.spread(j, p)

    def second(self, d):
        g = self.grid
        for jj in range(self.per_core):
            j = self.mine(jj)
            for e in range(1, g.side):
                if jj % 2 == 0:
                    p = g.chip(g.zs(d), g.hi, g.los(e))
                else:
                    p = g.chip(g.zs(d), g.his(e), g.lo)
                self.wait(j, p)
                for k in range(1, g.side):
                    self.send(j, p, g.hi_peer(k) if jj % 2 == 0 else g.lo_peer(k))
                self.send(j, p, g.sib())

    def third(self, d):
        g = self.grid
        for jj in range(self.per_core):
            j = self.mine(jj)
            for e in range(1, g.side):
                for k in range(g.side):
                    if jj % 2 == 0:
                        p = g.chip(g.zs(d), g.his(e), g.los(k))
                    else:
                        p = g.chip(g.zs(d), g.his(k), g.los(e))
                    self.wait(j, p)
                    self.send(j, p, g.sib())

    def sibling(self):
        g = self.grid
        for jj in range(self.per_core):
            j = (1 - g.core) * self.per_core + jj
            for d in range(g.nz):
                for e in range(g.side):
                    for k in range(g.side):
                        self.wait(j, g.chip(g.zs(d), g.his(e), g.los(k)))

    @staticmethod
    def sends(grid, per_core):
        n, s = grid.nz, grid.side
        return per_core * (n - 1 + n * (s - 1) + n * s * (s - 1) + grid.chips)


def join_rows(grid, low, high):
    parts = [low.astype(F32), high.astype(F32)]
    if grid.pad != grid.rows:
        parts.append(jnp.zeros((grid.pad - grid.rows, low.shape[1]), F32))
    return jnp.concatenate(parts, axis=0).astype(BF16)


def gather_kernel(grid, attn_ref, up_ref, down_ref, vec_ref, w_attn, w_up, w_down, w_vec,
                  pre_ref, pre_vec, stage, stage_vec, rsem, vsem, ssem, psem, lsem):
    grid.place()
    grid.barrier()
    sender = Sender(ssem)
    c = grid.core
    me = grid.chip(grid.z, grid.hi, grid.lo)
    raws = (attn_ref, up_ref)
    for g, raw in enumerate(raws):
        for jj in range(2):
            sender.start(raw.at[(1 - c) * 2 + jj], pre_ref.at[g, jj], psem.at[g, jj], grid.sib())
    sender.start(vec_ref.at[1 - c], pre_vec, psem.at[2, 0], grid.sib())

    groups = [
        Gather(grid, sender, lambda j, p: w_attn.at[j, p], lambda j, p: rsem.at[0, j, p]),
        Gather(grid, sender, lambda j, p: w_up.at[j, p], lambda j, p: rsem.at[1, j, p]),
        Gather(grid, sender, lambda j, p: w_down.at[p, j], lambda j, p: rsem.at[2, j, p]),
    ]
    vec = Gather(grid, sender, lambda j, p: w_vec.at[j, p], lambda j, p: vsem.at[j, p], per_core=1)

    def put(src, dst, k):
        copy = pltpu.make_async_copy(src, dst, lsem.at[k])
        copy.start()
        copy.wait()

    def assemble(g):
        for jj in range(2):
            if g < 2:
                sender.arrived(pre_ref.at[g, jj], psem.at[g, jj], grid)
                own, other = raws[g][c * 2 + jj], pre_ref[g, jj]
                first = jnp.where(c == 0, own.astype(F32), other.astype(F32))
                last = jnp.where(c == 0, other.astype(F32), own.astype(F32))
            else:
                first, last = down_ref[2 * jj], down_ref[2 * jj + 1]
            stage[jj] = join_rows(grid, first, last)
            put(stage.at[jj], groups[g].at(c * 2 + jj, me), 0)

    assemble(0)
    groups[0].own()
    sender.arrived(pre_vec, psem.at[2, 0], grid)
    stage_vec[...] = (vec_ref[c].astype(F32) + pre_vec[...].astype(F32)).astype(BF16)
    put(stage_vec, w_vec.at[c, me], 0)
    vec.own()
    def z_steps(g):
        for d in range(grid.nz - 1, 0, -1):
            g.along_z(d)

    def second_steps(g):
        for d in range(grid.nz, 0, -1):
            g.second(d)

    def third_steps(g):
        for d in range(grid.nz, 0, -1):
            g.third(d)

    z_steps(vec)
    z_steps(groups[0])
    assemble(1)
    groups[1].own()
    second_steps(vec)
    second_steps(groups[0])
    z_steps(groups[1])
    assemble(2)
    groups[2].own()
    third_steps(vec)
    third_steps(groups[0])
    second_steps(groups[1])
    z_steps(groups[2])
    third_steps(groups[1])
    second_steps(groups[2])
    third_steps(groups[2])
    for g in [vec] + groups:
        g.sibling()
    sender.finish()


def gather_all(grid, raw_attn, raw_up, raw_down, raw_vec):
    n, pad, dr = grid.chips, grid.pad, grid.dev_rows
    nsend = 5 + 3 * Gather.sends(grid, 2) + Gather.sends(grid, 1)
    any_spec = pl.BlockSpec(memory_space=pl.ANY)
    vmem = pl.BlockSpec(memory_space=pltpu.VMEM)
    return pl.pallas_call(
        functools.partial(gather_kernel, grid),
        out_shape=[
            jax.ShapeDtypeStruct((4, n, pad, D), BF16),
            jax.ShapeDtypeStruct((4, n, pad, D), BF16),
            jax.ShapeDtypeStruct((n, 4, pad, D), BF16),
            jax.ShapeDtypeStruct((2, n, 16, D), BF16),
        ],
        in_specs=[vmem] * 4,
        out_specs=[any_spec] * 4,
        scratch_shapes=[
            pltpu.VMEM((2, 2, dr, D), BF16),
            pltpu.VMEM((16, D), BF16),
            pltpu.VMEM((2, pad, D), BF16),
            pltpu.VMEM((16, D), BF16),
            pltpu.SemaphoreType.DMA((3, 4, n)),
            pltpu.SemaphoreType.DMA((2, n)),
            pltpu.SemaphoreType.DMA((nsend,)),
            pltpu.SemaphoreType.DMA((3, 2)),
            pltpu.SemaphoreType.DMA((1,)),
        ],
        compiler_params=pltpu.CompilerParams(collective_id=0, has_side_effects=True, vmem_limit_bytes=32 * 2**20),
    )(raw_attn, raw_up, raw_down, raw_vec)
class Reduce:
    def __init__(self, grid, sender, part, held, second, third, last, sems):
        self.grid, self.sender, self.part = grid, sender, part
        self.held, self.from_second, self.from_third, self.from_z = held, second, third, last
        self.sem_sib, self.sem_second, self.sem_third, self.sem_z = sems

    def to_sibling(self, d):
        g = self.grid
        z = g.zs(d)
        for jj in range(2):
            j = (1 - g.core) * 2 + jj
            self.sender.start(self.part(j, z), self.held.at[jj, z], self.sem_sib.at[jj, z], g.sib())

    def add_sibling(self, d):
        g, s = self.grid, self.grid.side
        z = g.zs(d)
        for jj in range(2):
            held = self.held.at[jj, z]
            self.sender.arrived(held, self.sem_sib.at[jj, z], g)
            own = self.part(g.core * 2 + jj, z)
            for h in range(s):
                def add(l, carry, h=h):
                    held[h, l] = (held[h, l].astype(F32) + own[h, l].astype(F32)).astype(BF16)
                    return carry
                lax.fori_loop(0, s, add, 0)
            for k in range(1, s):
                if jj % 2 == 0:
                    src, peer = held.at[g.his(k)], g.hi_peer(k)
                else:
                    src, peer = held.at[:, g.los(k)], g.lo_peer(k)
                self.sender.start(src, self.from_second.at[jj, s - k - 1, z], self.sem_second.at[jj, s - k - 1, z], peer)

    def add_second(self, d):
        g, s = self.grid, self.grid.side
        z = g.zs(d)
        for jj in range(2):
            for k in range(s - 1):
                self.sender.arrived(self.from_second.at[jj, k, z], self.sem_second.at[jj, k, z], g)
            for e in range(s):
                at = self.held.at[jj, z, g.hi, e] if jj % 2 == 0 else self.held.at[jj, z, e, g.lo]
                total = at[...].astype(F32)
                for k in range(s - 1):
                    total = total + self.from_second[jj, k, z, e].astype(F32)
                at[...] = total.astype(BF16)
            for k in range(1, s):
                if jj % 2 == 0:
                    src, peer = self.held.at[jj, z, g.hi, g.los(k)], g.lo_peer(k)
                else:
                    src, peer = self.held.at[jj, z, g.his(k), g.lo], g.hi_peer(k)
                self.sender.start(src, self.from_third.at[jj, s - k - 1, z], self.sem_third.at[jj, s - k - 1, z], peer)

    def own(self, jj, z):
        g, s = self.grid, self.grid.side
        for k in range(s - 1):
            self.sender.arrived(self.from_third.at[jj, k, z], self.sem_third.at[jj, k, z], g)
        total = self.held[jj, z, g.hi, g.lo].astype(F32)
        for k in range(s - 1):
            total = total + self.from_third[jj, k, z].astype(F32)
        return total

    def add_third(self, d):
        g = self.grid
        z = g.zs(d)
        for jj in range(2):
            at = self.held.at[jj, z, g.hi, g.lo]
            at[...] = self.own(jj, z).astype(BF16)
            self.sender.start(at, self.from_z.at[jj, g.nz - d - 1], self.sem_z.at[jj, g.nz - d - 1], g.z_peer(d))

    def result(self, jj):
        g = self.grid
        total = self.own(jj, g.z)
        for k in range(g.nz - 1):
            self.sender.arrived(self.from_z.at[jj, k], self.sem_z.at[jj, k], g)
            total = total + self.from_z[jj, k].astype(F32)
        return total

    @staticmethod
    def sends(grid):
        n, s = grid.nz, grid.side
        return 2 * (n + n * (s - 1) * 2 + n - 1)

    @staticmethod
    def scratch(grid, groups):
        n, s, pad = grid.nz, grid.side, grid.pad
        return [
            pltpu.VMEM((groups, 2, n, s, s, pad, D), BF16),
            pltpu.VMEM((groups, 2, s - 1, n, s, pad, D), BF16),
            pltpu.VMEM((groups, 2, s - 1, n, pad, D), BF16),
            pltpu.VMEM((groups, 2, n - 1, pad, D), BF16),
            pltpu.SemaphoreType.DMA((groups, 2, n)),
            pltpu.SemaphoreType.DMA((groups, 2, s - 1, n)),
            pltpu.SemaphoreType.DMA((groups, 2, s - 1, n)),
            pltpu.SemaphoreType.DMA((groups, 2, n - 1)),
        ]


def sum_everywhere(grid, sender, own, landing, sem):
    steps = [[grid.sib()],
             [grid.lo_peer(d) for d in range(1, grid.side)],
             [grid.hi_peer(d) for d in range(1, grid.side)],
             [grid.z_peer(d) for d in range(1, grid.nz)]]
    slot = 0
    for n, peers in enumerate(steps):
        for k, peer in enumerate(peers):
            sender.start(own.at[n], landing.at[slot + len(peers) - 1 - k], sem.at[slot + len(peers) - 1 - k], peer)
        total = own[n]
        for k in range(len(peers)):
            sender.arrived(landing.at[slot + k], sem.at[slot + k], grid)
            total = total + landing[slot + k]
        slot += len(peers)
        own[n + 1] = total


def peer_count(grid):
    return 1 + 2 * (grid.side - 1) + grid.nz - 1


def reduce_kernel(grid, g_attn, g_up, g_down, g_vec, o_attn, o_up, o_down, o_vec,
                  held, second, third, last, s1, s2, s3, s4, swap_out, swap_in, wsem, vec, vec_in, vsem, ssem):
    grid.place()
    grid.barrier()
    sender = Sender(ssem)
    c = grid.core
    parts = [lambda j, z: g_attn.at[j, z], lambda j, z: g_up.at[j, z], lambda j, z: g_down.at[z, :, :, j]]
    groups = [
        Reduce(grid, sender, parts[g], held.at[g], second.at[g], third.at[g], last.at[g],
               (s1.at[g], s2.at[g], s3.at[g], s4.at[g]))
        for g in range(3)
    ]
    order = [groups[2], groups[1], groups[0]]
    n = grid.nz
    for g in order:
        for d in range(n, 0, -1):
            g.to_sibling(d)
    vec[0] = g_vec[...]
    for g in order:
        for d in range(n, 0, -1):
            g.add_sibling(d)
    for g in order:
        for d in range(n, 0, -1):
            g.add_second(d)
    for g in order:
        for d in range(n - 1, 0, -1):
            g.add_third(d)
    sum_everywhere(grid, sender, vec, vec_in, vsem)
    o_vec[...] = vec[4]
    r, dr = grid.rows, grid.dev_rows
    for i, (g, out) in enumerate(((groups[1], o_up), (groups[0], o_attn))):
        for jj in range(2):
            total = g.result(jj)
            top, bottom = total[:dr], total[dr:r]
            out[c * 2 + jj] = jnp.where(c == 0, top, bottom)
            swap_out[i, jj] = jnp.where(c == 0, bottom, top)
            sender.start(swap_out.at[i, jj], swap_in.at[i, jj], wsem.at[i, jj], grid.sib())
    for jj in range(2):
        o_down[jj] = groups[2].result(jj)[:r]
    for i, out in enumerate((o_up, o_attn)):
        for jj in range(2):
            sender.arrived(swap_in.at[i, jj], wsem.at[i, jj], grid)
            out[(1 - c) * 2 + jj] = swap_in[i, jj]
    sender.finish()


def reduce_all(grid, g_attn, g_up, g_down, g_vec):
    n, s, pad, dr = grid.nz, grid.side, grid.pad, grid.dev_rows
    nsend = 3 * Reduce.sends(grid) + 4 + peer_count(grid)
    vmem = pl.BlockSpec(memory_space=pltpu.VMEM)
    return pl.pallas_call(
        functools.partial(reduce_kernel, grid),
        out_shape=[
            jax.ShapeDtypeStruct((4, dr, D), F32),
            jax.ShapeDtypeStruct((4, dr, D), F32),
            jax.ShapeDtypeStruct((2, grid.rows, D), F32),
            jax.ShapeDtypeStruct((16, D), F32),
        ],
        in_specs=[vmem] * 4,
        out_specs=[vmem] * 4,
        scratch_shapes=Reduce.scratch(grid, 3) + [
            pltpu.VMEM((2, 2, dr, D), F32),
            pltpu.VMEM((2, 2, dr, D), F32),
            pltpu.SemaphoreType.DMA((2, 2)),
            pltpu.VMEM((5, 16, D), F32),
            pltpu.VMEM((peer_count(grid), 16, D), F32),
            pltpu.SemaphoreType.DMA((peer_count(grid),)),
            pltpu.SemaphoreType.DMA((nsend,)),
        ],
        compiler_params=pltpu.CompilerParams(collective_id=1, has_side_effects=True, vmem_limit_bytes=56 * 2**20),
    )(g_attn, g_up, g_down, g_vec)
HEADS = 12
HD = 64
ROW = 512
BLOCK = 64
PER_ROW = ROW // BLOCK
NEG = -1e30
TM = 256


def mm(a, b):
    return jnp.dot(a, b, preferred_element_type=F32)


def mm_nt(a, b):
    return lax.dot_general(a, b, (((1,), (1,)), ((), ())), preferred_element_type=F32)


def mm_tn(a, b):
    return lax.dot_general(a, b, (((0,), (0,)), ((), ())), preferred_element_type=F32)


def tile(i, size):
    return pl.ds(pl.multiple_of(i * size, size), size)


def loop(n, f, unroll=1):
    def step(i, carry):
        for k in range(unroll):
            f(i * unroll + k)
        return carry
    lax.fori_loop(0, n // unroll, step, 0)


def row_blocks(bucket_ref, length_ref, row):
    starts, lens = [], []
    for b in range(PER_ROW):
        stride = bucket_ref[row * PER_ROW + b] // BLOCK
        first = b // stride * stride
        starts.append(first)
        lens.append(length_ref[row * PER_ROW + first])
    return starts, lens


def pick(ids, values):
    out = jnp.zeros_like(ids)
    for b, value in enumerate(values):
        out = jnp.where(ids == b, value, out)
    return out


def write_mask(mask_ref, starts, lens):
    query = pick(lax.broadcasted_iota(jnp.int32, (BLOCK, ROW), 1) // BLOCK, starts)
    place = lax.broadcasted_iota(jnp.int32, (BLOCK, ROW), 0)
    for b in range(PER_ROW):
        limit = lens[b] - (b - starts[b]) * BLOCK
        allowed = (query == starts[b]) & (place < limit)
        mask_ref[b * BLOCK : (b + 1) * BLOCK, :] = jnp.where(allowed, 0.0, NEG)


def member_matrix(starts, lens):
    lane = lax.broadcasted_iota(jnp.int32, (PER_ROW, ROW), 1)
    token_start = pick(lane // BLOCK, starts)
    token_len = pick(lane // BLOCK, lens)
    valid = lane - token_start * BLOCK < token_len
    block = lax.broadcasted_iota(jnp.int32, (PER_ROW, ROW), 0)
    member = jnp.where((token_start == pick(block, starts)) & valid, 1.0, 0.0).astype(F32)
    lens_col = pick(lax.broadcasted_iota(jnp.int32, (PER_ROW, 1), 0), lens)
    return member, 1.0 / lens_col.astype(F32)


def layer_norm_parts(v):
    center = v - jnp.mean(v, axis=-1, keepdims=True)
    spread = jnp.mean(center * center, axis=-1, keepdims=True)
    scale = lax.rsqrt(spread + 1e-05)
    return center * scale, scale


def layer_norm_back(grad, normed, scale, gain):
    g = grad * gain
    return scale * (g - jnp.mean(g, axis=-1, keepdims=True) - normed * jnp.mean(g * normed, axis=-1, keepdims=True))


def gelu_both(x):
    t = 1.0 / (1.0 + 0.23164189 * jnp.abs(x))
    density = jnp.exp(x * x * -0.5 - 0.9189385332046727)
    poly = ((((1.330274429 * t - 1.821255978) * t + 1.781477937) * t - 0.356563782) * t + 0.319381530) * t
    tail = poly * density
    phi = jnp.where(x < 0, tail, 1.0 - tail)
    return x * phi, phi + x * density


def half(shape, axis, h):
    return lax.broadcasted_iota(jnp.int32, shape, axis) // HD == h


def attend_pair_back(queries, keys, values, context, logs, mask, grad_context, grad_q, grad_k, grad_v, row, pair, chunk=256):
    rows, cols = tile(row, ROW), tile(pair, 2 * HD)
    key_slab, value_slab = keys[rows, cols], values[rows, cols]
    key_turned = key_slab.astype(F32).T.astype(BF16)
    lane = [half((ROW, 2 * HD), 1, h) for h in range(2)]
    only_k = [jnp.where(lane[h], key_slab.astype(F32), 0.0).astype(BF16) for h in range(2)]
    only_v = [jnp.where(lane[h], value_slab.astype(F32), 0.0).astype(BF16) for h in range(2)]
    sums = []
    for c in range(ROW // chunk):
        part = tile(row * (ROW // chunk) + c, chunk)
        query_slab, grad_slab = queries[part, cols], grad_context[part, cols]
        dot = (grad_slab.astype(F32) * context[part, cols].astype(F32)).T
        gq, gk, gv = [], [], []
        for h in range(2):
            delta = jnp.sum(dot[h * HD : (h + 1) * HD], axis=0, keepdims=True)
            s = mm_nt(only_k[h], query_slab) + mask[rows, c * chunk : (c + 1) * chunk]
            p = jnp.exp(s - logs[row, pair, h : h + 1, c * chunk : (c + 1) * chunk])
            gp = mm_nt(only_v[h], grad_slab)
            gs = (p * (gp - delta)).astype(BF16)
            gv.append(mm(p.astype(BF16), grad_slab))
            gk.append(mm(gs, query_slab))
            gq.append(mm(key_turned, gs))
        turned = jnp.where(half((2 * HD, chunk), 0, 0), gq[0], gq[1]) * 0.125
        grad_q[part, cols] = turned.T.astype(BF16)
        now = (jnp.where(lane[0], gk[0], gk[1]), jnp.where(lane[0], gv[0], gv[1]))
        sums = now if c == 0 else tuple(a + b for a, b in zip(sums, now))
    grad_k[rows, cols] = sums[0].astype(BF16)
    grad_v[rows, cols] = sums[1].astype(BF16)


def attend_pair_rows(queries, keys, values, context, logs, mask, row, pair, chunk=256):
    rows, cols = tile(row, ROW), tile(pair, 2 * HD)
    key_slab, value_slab = keys[rows, cols], values[rows, cols]
    for c in range(ROW // chunk):
        part = tile(row * (ROW // chunk) + c, chunk)
        query_slab = queries[part, cols]
        parts, cols_log = [], []
        lane = [half((chunk, 2 * HD), 1, h) for h in range(2)]
        for h in range(2):
            only = jnp.where(lane[h], query_slab.astype(F32), 0.0).astype(BF16)
            s = mm_nt(only, key_slab) + mask[part, :ROW]
            peak = jnp.max(s, axis=1, keepdims=True)
            e = jnp.exp(s - peak)
            total = jnp.sum(e, axis=1, keepdims=True)
            cols_log.append(peak + jnp.log(total))
            parts.append(mm(e.astype(BF16), value_slab) * (1.0 / total))
        context[part, cols] = jnp.where(lane[0], parts[0], parts[1]).astype(BF16)
        both = jnp.where(lane[0], cols_log[0], cols_log[1]).T
        for h in range(2):
            logs[row, pair, h : h + 1, c * chunk : (c + 1) * chunk] = both[h * HD : h * HD + 1]


QB, VB, OB, G1, S1, DB, G2, S2 = range(8)
UB = 8


def after_attention(tokens, context, w_out, vec, normed, scale, hidden, i, tm):
    rows = tile(i, tm)
    first = tokens[rows, :].astype(F32) + mm(context[rows, :], w_out) + vec[OB : OB + 1, :]
    n, r = layer_norm_parts(first)
    normed[rows, :] = n
    scale[rows, :64] = jnp.broadcast_to(r, (tm, 64))
    hidden[rows, :] = (n * vec[G1 : G1 + 1, :] + vec[S1 : S1 + 1, :]).astype(BF16)


WIDTHS = (D, 2 * D // 3, D // 3, D // 6, D // 12)


def split_low(x):
    high = x.astype(BF16)
    return high, (x - high.astype(F32)).astype(BF16)


def pool_row(normed, vec, layer_out, pools, pool_grad, out_grad, total, starts, lens, row):
    rows = pl.ds(row * ROW, ROW)
    member, inverse = member_matrix(starts, lens)
    member = member.astype(BF16)
    outputs = normed[rows, :] * vec[G2 : G2 + 1, :] + vec[S2 : S2 + 1, :]
    layer_out[rows, :] = outputs.astype(BF16)
    high, low = split_low(outputs)
    avg = (mm(member, high) + mm(member, low)) * inverse
    square = avg * avg
    blocks = pl.ds(row * PER_ROW, PER_ROW)
    grad = None
    at = 0
    for width in WIDTHS:
        r = lax.rsqrt(jnp.sum(square[:, :width], axis=-1, keepdims=True) / width + 1e-06)
        lead = avg[:, :width]
        pools[blocks, at : at + width] = lead * r
        g = pool_grad[blocks, at : at + width]
        back = g * r - lead * (r * r * r * (jnp.sum(g * lead, axis=-1, keepdims=True) / width))
        if width % 128:
            wide = -(-width // 128) * 128
            back = jnp.concatenate([back, jnp.zeros((PER_ROW, wide - width), F32)], axis=1)
        if grad is None:
            grad = back
        else:
            grad = jnp.concatenate([grad[:, : back.shape[1]] + back, grad[:, back.shape[1] :]], axis=1)
        at += width
    high, low = split_low(grad * inverse)
    both = jnp.concatenate([high, low], axis=0)
    total[rows, :] = out_grad[rows, :].astype(F32) + mm_tn(jnp.concatenate([member, member], axis=0), both)


def add_row(vec_grad, k, values):
    vec_grad[k : k + 1, :] += jnp.sum(values, axis=0, keepdims=True)


def second_norm_back(total, normed, scale, vec, vec_grad, branch, i, tm):
    rows = tile(i, tm)
    g, n = total[rows, :], normed[rows, :]
    add_row(vec_grad, G2, g * n)
    add_row(vec_grad, S2, g)
    back = layer_norm_back(g, n, scale[rows, 64:65], vec[G2 : G2 + 1, :])
    total[rows, :] = back
    low = back.astype(BF16)
    branch[rows, :] = low
    add_row(vec_grad, DB, low.astype(F32))


def turn(x, out, tm=256):
    for i in range(x.shape[0] // tm):
        for j in range(x.shape[1] // tm):
            out[j * tm : (j + 1) * tm, i * tm : (i + 1) * tm] = x[i * tm : (i + 1) * tm, j * tm : (j + 1) * tm].T
class Memory:
    NAMES = ("attn", "up", "down", "spare", "act", "slope", "x", "ctx", "hidden", "norm", "total",
             "scale", "logs", "vec", "vec_grad", "lsem")

    def __init__(self, refs):
        for name, ref in zip(self.NAMES, refs):
            setattr(self, name, ref)

    @staticmethod
    def shapes(tokens):
        v = pltpu.VMEM
        weights = [v((4 * D, D), BF16)] * 4
        return weights + [
            v((4, tokens, D), BF16), v((4, tokens, D), BF16),
            v((tokens, D), BF16), v((tokens, D), BF16), v((tokens, D), BF16),
            v((tokens, D), F32), v((tokens, D), F32), v((tokens, 128), F32),
            v((tokens // ROW, HEADS // 2, 8, ROW), F32), v((16, D), F32), v((16, D), F32),
            pltpu.SemaphoreType.DMA((12,)),
        ]


def panel(ref, j):
    return ref.at[j * D : (j + 1) * D]


class NoNetwork:
    def __getattr__(self, name):
        return lambda *a: None


def layer_steps(m, net, bucket, length, tokens_in, out_grad_in, pool_grad, layer_out, pools, token_grad, keep_qkv, keep_norm, block=None):
    count = m.x.shape[0]
    tiles, rows_total = count // TM, count // ROW

    def copy(src, dst, k):
        return pltpu.make_async_copy(src, dst, m.lsem.at[k])

    queries, keys, values = (m.slope.at[j] for j in range(3))
    load_tokens = copy(tokens_in, m.x, 0)
    load_tokens.start()
    net.begin()
    m.vec_grad[...] = jnp.zeros_like(m.vec_grad)
    load_tokens.wait()
    net.need_attn()
    w_query, w_key, w_value, w_out = (panel(m.attn, j) for j in range(4))

    def qkv(i):
        rows = tile(i, TM)
        t = m.x[rows, :]
        q = (mm(t, w_query[...]) + m.vec[QB : QB + 1, :]).astype(BF16)
        queries[rows, :] = (q.astype(F32) * 0.125).astype(BF16)
        keys[rows, :] = mm(t, w_key[...]).astype(BF16)
        values[rows, :] = (mm(t, w_value[...]) + m.vec[VB : VB + 1, :]).astype(BF16)

    loop(tiles, qkv)
    for row in range(rows_total):
        starts, lens = row_blocks(bucket, length, row)
        mask = m.total.at[row * ROW : (row + 1) * ROW, :ROW]
        write_mask(mask, starts, lens)
        mask[...] = mask[...].T
        for part in range(2):
            net.during_attention(row * 2 + part)
            loop(3, lambda p: attend_pair_rows(queries, keys, values, m.ctx, m.logs, m.total, row, p + 3 * part, ROW), 3)
    stores = [copy(m.slope.at[j], keep_qkv.at[j], 1 + j) for j in range(3)]
    for s in stores:
        s.start()
    loop(tiles, lambda i: after_attention(m.x, m.ctx, w_out[...], m.vec, m.norm, m.scale, m.hidden, i, TM), 2)
    stores.append(copy(m.norm, keep_norm, 4))
    stores[-1].start()
    load_grad = copy(out_grad_in, m.x, 0)
    load_grad.start()
    net.need_up()
    for s in stores[:3]:
        s.wait()
    def feed(i):
        rows = tile(i, TM)
        for j in range(4):
            value, deriv = gelu_both(mm(m.hidden[rows, :], panel(m.up, j)[...]) + m.vec[UB + j : UB + j + 1, :])
            m.act[j, rows, :] = value.astype(BF16)
            m.slope[j, rows, :] = deriv.astype(BF16)

    for part in range(2):
        loop(tiles // 2, lambda i: feed(i + part * (tiles // 2)))
        net.during_up(part)
    stores[3].wait()
    net.need_down()

    def down(i):
        rows = tile(i, TM)
        second = m.hidden[rows, :].astype(F32) + m.vec[DB : DB + 1, :]
        for j in range(4):
            second = second + mm(m.act[j, rows, :], panel(m.down, j)[...])
        n, r = layer_norm_parts(second)
        m.norm[rows, :] = n
        m.scale[rows, 64:] = jnp.broadcast_to(r, (TM, 64))

    loop(tiles, down)
    load_grad.wait()
    out_low = m.spare.at[:count]
    for row in range(rows_total):
        starts, lens = row_blocks(bucket, length, row)
        pool_row(m.norm, m.vec, out_low, pools, pool_grad, m.x, m.total, starts, lens, row)
    store_out = copy(out_low, layer_out, 5)
    store_out.start()
    loop(tiles, lambda i: second_norm_back(m.total, m.norm, m.scale, m.vec, m.vec_grad, m.x, i, TM))
    load_norm = copy(keep_norm, m.norm, 6)
    load_norm.start()
    store_out.wait()
    net.gathered()
    group = D // 2

    def grad_down(i):
        for j in range(4):
            part = mm_tn(m.act[j, :, tile(i, group)], m.x[...]).astype(BF16)
            if block is None:
                m.spare[pl.ds(pl.multiple_of(i * group + j * D, group), group), :] = part
            else:
                for b in range(group // block):
                    chip = (i * group + j * D) // (4 * block) + b // 4
                    at = ((b % 4) * (D // block) + chip) * block
                    m.spare[pl.ds(pl.multiple_of(at, block), block), :] = part[b * block : (b + 1) * block]

    loop(D // group, grad_down)
    net.ready_down()
    def back(i):
        rows = tile(i, TM)
        for j in range(4):
            g = (mm_nt(m.x[rows, :], panel(m.down, j)[...]) * m.slope[j, rows, :].astype(F32)).astype(BF16)
            m.slope[j, rows, :] = g
            add_row(m.vec_grad, UB + j, g.astype(F32))

    for part in range(2):
        loop(tiles // 2, lambda i: back(i + part * (tiles // 2)))
        net.during_back(part)
    for j in range(4):
        def grad_up(i, j=j):
            at = pl.ds(pl.multiple_of(i * TM + j * D, TM), TM)
            m.down[at, :] = mm_tn(m.hidden[:, tile(i, TM)], m.slope[j]).astype(BF16)
        loop(D // TM, grad_up, D // TM)
        net.during_up_grad(j)
    load_norm.wait()

    def first_back(i):
        rows = tile(i, TM)
        g = m.total[rows, :]
        for j in range(4):
            g = g + mm_nt(m.slope[j, rows, :], panel(m.up, j)[...])
        n = m.norm[rows, :]
        add_row(m.vec_grad, G1, g * n)
        add_row(m.vec_grad, S1, g)
        back = layer_norm_back(g, n, m.scale[rows, :1], m.vec[G1 : G1 + 1, :])
        m.total[rows, :] = back
        low = back.astype(BF16)
        m.x[rows, :] = low
        add_row(m.vec_grad, OB, low.astype(F32))

    loop(tiles, first_back)
    net.after_first_back()
    loads = [copy(keep_qkv.at[j], m.slope.at[j], 7 + j) for j in range(3)]
    loads.append(copy(tokens_in, m.hidden, 10))
    for s in loads:
        s.start()
    grad_context = m.act.at[3]

    def context_back(i):
        grad_context[tile(i, TM), :] = mm_nt(m.x[tile(i, TM), :], w_out[...]).astype(BF16)

    loop(tiles, context_back)

    def grad_out(i):
        m.up[tile(i, TM), :] = mm_tn(m.ctx[:, tile(i, TM)], m.x[...]).astype(BF16)

    loop(D // TM, grad_out)
    net.after_out()
    for s in loads:
        s.wait()
    grads = [m.act.at[j] for j in range(3)]
    for row in range(rows_total):
        starts, lens = row_blocks(bucket, length, row)
        write_mask(m.norm.at[row * ROW : (row + 1) * ROW, :ROW], starts, lens)
    wide = D // 3
    for k in range(3):
        for part in range(2):
            net.after_chunk(k, part)
            loop(rows_total, lambda row: attend_pair_back(
                queries, keys, values, m.ctx, m.logs, m.norm, grad_context, *grads, row, 2 * k + part, 256), rows_total)
        cols = slice(k * wide, (k + 1) * wide)

        def grad_qkv(i):
            at = pl.ds(pl.multiple_of(i * TM + (k + 1) * D, TM), TM)
            for j in range(3):
                m.up[at, j * wide : (j + 1) * wide] = mm_tn(m.hidden[:, tile(i, TM)], m.act[j, :, cols]).astype(BF16)

        loop(D // TM, grad_qkv, D // TM)
        net.after_chunk(k, 2)
        for place, j in ((QB, 0), (VB, 2)):
            m.vec_grad[place : place + 1, cols] = jnp.sum(m.act[j, :, cols].astype(F32), axis=0, keepdims=True)
    net.ready_vec()
    for i in range(tiles):
        rows = slice(i * TM, (i + 1) * TM)
        g = m.total[rows, :]
        for j, w in enumerate((w_query, w_key, w_value)):
            g = g + mm_nt(m.act[j, rows, :], w[...])
        m.total[rows, :] = g
        net.during_finish(i)
    store_grad = copy(m.total, token_grad, 11)
    store_grad.start()
    net.end()
    store_grad.wait()


def local_kernel(bucket, length, tokens_in, out_grad_in, pool_grad, vec, w_attn, w_up, w_down,
                 layer_out, pools, token_grad, g_attn, g_up, g_down, g_vec, keep_qkv, keep_norm, *scratch):
    m = Memory(scratch)

    class Local(NoNetwork):
        def begin(self):
            m.vec[...] = vec[...]
            for src, dst in ((w_attn, m.attn), (w_up, m.up), (w_down, m.down)):
                c = pltpu.make_async_copy(src, dst, m.lsem.at[1])
                c.start()
                c.wait()

    layer_steps(m, Local(), bucket, length, tokens_in, out_grad_in, pool_grad, layer_out, pools, token_grad, keep_qkv, keep_norm)
    for src, dst in ((m.up, g_attn), (m.down, g_up), (m.spare, g_down)):
        c = pltpu.make_async_copy(src, dst, m.lsem.at[1])
        c.start()
        c.wait()
    g_vec[...] = m.vec_grad[...]


def layer_local(bucket, length, tokens, out_grad, pool_grad, vec, w_attn, w_up, w_down):
    count = tokens.shape[0]
    v, any_spec, smem = pl.BlockSpec(memory_space=pltpu.VMEM), pl.BlockSpec(memory_space=pl.ANY), pl.BlockSpec(memory_space=pltpu.SMEM)
    s = jax.ShapeDtypeStruct
    return pl.pallas_call(
        local_kernel,
        out_shape=[s((count, D), BF16), s(pool_grad.shape, F32), s((count, D), F32), s((4 * D, D), BF16), s((4 * D, D), BF16),
                   s((4 * D, D), BF16), s((16, D), F32), s((3, count, D), BF16), s((count, D), F32)],
        in_specs=[smem, smem, any_spec, any_spec, v, v, any_spec, any_spec, any_spec],
        out_specs=[any_spec, v, any_spec, any_spec, any_spec, any_spec, v, any_spec, any_spec],
        scratch_shapes=Memory.shapes(count),
        compiler_params=pltpu.CompilerParams(vmem_limit_bytes=63 * 2**20),
    )(bucket, length, tokens, out_grad, pool_grad, vec, w_attn, w_up, w_down)[:7]
def flip(x, d):
    bit = 1
    while bit <= d:
        if d & bit:
            x = x + bit - 2 * bit * lax.rem(x // bit, 2)
        bit *= 2
    return x


def near_first(n):
    return sorted(range(1, n), key=lambda d: (d == n // 2, d % 2 == 0, d))


class Place:
    def __init__(self, grid):
        self.grid = grid
        self.sizes = {"z": grid.nz, "hi": grid.side, "lo": grid.side}
        assert all(n & (n - 1) == 0 for n in self.sizes.values())

    def at(self, offsets):
        g = self.grid
        return {name: flip(getattr(g, name), offsets.get(name, 0)) for name in self.sizes}

    def chip(self, offsets):
        a = self.at(offsets)
        return self.grid.chip(a["z"], a["hi"], a["lo"])

    def peer(self, name, d):
        a = self.at({name: d})
        return self.grid.dev(a["z"], a["hi"], a["lo"], self.grid.core)


class Spread:
    def __init__(self, place, sender, route, at, sem, unit, other):
        self.place, self.sender, self.route, self.at, self.sem = place, sender, route, at, sem
        self.unit, self.other = unit, other

    def send(self, offsets, device):
        p = self.place.chip(offsets)
        self.sender.start(self.at(self.unit, p), self.at(self.unit, p), self.sem(self.unit, p), device)

    def pass_on(self, offsets, axes):
        for name in axes:
            for d in near_first(self.place.sizes[name]):
                self.send(offsets, self.place.peer(name, d))

    def arrived(self, offsets):
        p = self.place.chip(offsets)
        self.sender.arrived(self.at(self.unit, p), self.sem(self.unit, p), self.place.grid)

    def to_sibling(self, offsets):
        self.send(offsets, self.place.grid.sib())

    def own(self, axes=None, sibling=True):
        self.pass_on({}, self.route if axes is None else axes)
        if sibling:
            self.to_sibling({})

    def first(self, d, axes=None, sibling=True):
        offsets = {self.route[0]: d}
        self.arrived(offsets)
        self.pass_on(offsets, self.route[1:])
        self.to_sibling(offsets)

    def second(self, a, d):
        offsets = {self.route[0]: a, self.route[1]: d}
        self.arrived(offsets)
        self.pass_on(offsets, self.route[2:])
        self.to_sibling(offsets)

    def third(self, a, b, d):
        offsets = {self.route[0]: a, self.route[1]: b, self.route[2]: d}
        self.arrived(offsets)
        self.to_sibling(offsets)

    def firsts(self):
        return [functools.partial(self.first, d) for d in near_first(self.place.sizes[self.route[0]])]

    def seconds(self):
        a_all = [0] + near_first(self.place.sizes[self.route[0]])
        return [functools.partial(self.second, a, d) for a in a_all for d in near_first(self.place.sizes[self.route[1]])]

    def thirds(self):
        a_all, b_all = ([0] + near_first(self.place.sizes[name]) for name in self.route[:2])
        return [functools.partial(self.third, a, b, d) for a in a_all for b in b_all for d in near_first(self.place.sizes[self.route[2]])]

    def from_sibling(self):
        offsets = [[0] + near_first(self.place.sizes[name]) for name in self.route]
        for a in offsets[0]:
            for b in offsets[1]:
                for c in offsets[2]:
                    p = self.place.chip({self.route[0]: a, self.route[1]: b, self.route[2]: c})
                    self.sender.arrived(self.at(self.other, p), self.sem(self.other, p), self.place.grid)

    @staticmethod
    def sends(grid):
        return 2 * grid.chips - 1


def mix(*lists):
    return [step for group in zip(*lists) for step in group]


class Stage:
    def __init__(self, place, sender, turn_over, source, held, second, third, last, sems):
        self.place, self.sender, self.source = place, sender, source
        self.held, self.from_second, self.from_third, self.from_z = held, second, third, last
        self.sem_sib, self.sem_second, self.sem_third, self.sem_z = sems
        g = place.grid
        self.grid = g
        self.which = lax.rem(g.core + turn_over, 2)
        self.a, self.b = self.swap(g.hi, g.lo)

    def swap(self, x, y):
        return x * (1 - self.which) + y * self.which, y * (1 - self.which) + x * self.which

    def z(self, d):
        return flip(self.grid.z, d)

    def block(self, a, b):
        r, s = self.grid.rows, self.grid.side
        hi, lo = self.swap(a, b)
        index = hi * s + lo
        return pl.ds(pl.multiple_of(index * r, r), r)

    def peer(self, a, b):
        hi, lo = self.swap(a, b)
        return self.grid.dev(self.grid.z, hi, lo, self.grid.core)

    def to_sibling(self):
        for d in self.z_order():
            z = self.z(d)
            self.sender.start(self.source(1 - self.grid.core, z), self.held.at[z], self.sem_sib.at[z], self.grid.sib())

    def z_order(self):
        return near_first(self.grid.nz)[::-1] + [0]

    def add_sibling(self, d):
        s, r, z = self.grid.side, self.grid.rows, self.z(d)
        held, own = self.held.at[z], self.source(self.grid.core, z)
        self.sender.arrived(held, self.sem_sib.at[z], self.grid)

        def add(i):
            at = pl.ds(pl.multiple_of(i * r, r), r)
            held[at, :] = (held[at, :].astype(F32) + own[at, :].astype(F32)).astype(BF16)

        loop(s * s, add)
        for k in range(1, s):
            a = flip(self.a, k)
            for b in range(s):
                self.sender.start(held.at[self.block(a, b)], self.from_second.at[k - 1, z, b * r : (b + 1) * r],
                                  self.sem_second.at[k - 1, z, b], self.peer(a, self.b))

    def add_second(self, d):
        s, r, z = self.grid.side, self.grid.rows, self.z(d)
        for k in range(s - 1):
            for b in range(s):
                self.sender.arrived(self.from_second.at[k, z, b * r : (b + 1) * r], self.sem_second.at[k, z, b], self.grid)
        for b in range(s):
            at = self.held.at[z, self.block(self.a, b)]
            total = at[...].astype(F32)
            for k in range(s - 1):
                total = total + self.from_second[k, z, b * r : (b + 1) * r].astype(F32)
            at[...] = total.astype(BF16)
        for k in range(1, s):
            b = flip(self.b, k)
            self.sender.start(self.held.at[z, self.block(self.a, b)], self.from_third.at[k - 1, z],
                              self.sem_third.at[k - 1, z], self.peer(self.a, b))

    def own(self, z):
        s = self.grid.side
        for k in range(s - 1):
            self.sender.arrived(self.from_third.at[k, z], self.sem_third.at[k, z], self.grid)
        total = self.held[z, self.block(self.a, self.b)].astype(F32)
        for k in range(s - 1):
            total = total + self.from_third[k, z].astype(F32)
        return total

    def add_third(self, d):
        z = self.z(d)
        at = self.held.at[z, self.block(self.a, self.b)]
        at[...] = self.own(z).astype(BF16)
        self.sender.start(at, self.from_z.at[d - 1], self.sem_z.at[d - 1], self.place.peer("z", d))

    def result(self):
        total = self.own(self.grid.z)
        for k in range(self.grid.nz - 1):
            self.sender.arrived(self.from_z.at[k], self.sem_z.at[k], self.grid)
            total = total + self.from_z[k].astype(F32)
        return total

    def add_siblings(self):
        for d in self.z_order():
            self.add_sibling(d)

    def add_seconds(self):
        for d in self.z_order():
            self.add_second(d)

    def add_thirds(self):
        for d in self.z_order()[:-1]:
            self.add_third(d)

    @staticmethod
    def sends(grid):
        n, s = grid.nz, grid.side
        return n + n * (s - 1) * s + n * (s - 1) + n - 1

    @staticmethod
    def scratch(grid, stages, width):
        n, s, r = grid.nz, grid.side, grid.rows
        return [
            pltpu.VMEM((stages, n, s * s * r, width), BF16),
            pltpu.VMEM((stages, s - 1, n, s * r, width), BF16),
            pltpu.VMEM((stages, s - 1, n, r, width), BF16),
            pltpu.VMEM((stages, n - 1, r, width), BF16),
            pltpu.SemaphoreType.DMA((stages, n)),
            pltpu.SemaphoreType.DMA((stages, s - 1, n, s)),
            pltpu.SemaphoreType.DMA((stages, s - 1, n)),
            pltpu.SemaphoreType.DMA((stages, n - 1)),
        ]


class SumAll:
    def __init__(self, place, sender, held, landing, sem):
        g = place.grid
        self.grid, self.sender, self.held, self.landing, self.sem = g, sender, held, landing, sem
        self.peers = [[g.sib()]] + [[place.peer(name, d) for d in range(1, place.sizes[name])] for name in ("lo", "hi", "z")]
        self.slots = [sum(len(p) for p in self.peers[:n]) for n in range(4)]

    def send(self, n):
        for k, peer in enumerate(self.peers[n]):
            slot = self.slots[n] + k
            self.sender.start(self.held.at[n], self.landing.at[slot], self.sem.at[slot], peer)

    def add(self, n):
        total = self.held[n]
        for k in range(len(self.peers[n])):
            slot = self.slots[n] + k
            self.sender.arrived(self.landing.at[slot], self.sem.at[slot], self.grid)
            total = total + self.landing[slot]
        self.held[n + 1] = total


def lane_places(grid, width):
    rank = grid.chip(grid.z, grid.hi, grid.lo) * 2 + grid.core
    first = lax.rem(rank * width, D)
    entry = lax.broadcasted_iota(jnp.int32, (128, D), 0)
    lane = lax.broadcasted_iota(jnp.int32, (128, D), 1)
    return jnp.where((lane == first + entry) & (entry < width), 1.0, 0.0).astype(BF16), rank * width // D


class Network:
    FFN, ATTN = 4, 4

    def __init__(self, grid, m, raws, outs, scratch):
        self.grid, self.m, self.raws, self.outs = grid, m, raws, outs
        (self.pre_out, self.pre_in, self.vec_out, self.vec_in, rsem, vsem, self.psem, ssem) = scratch[:8]
        ffn, attn = scratch[8:16], scratch[16:24]
        (self.swap_out, self.swap_in, self.wsem, self.swap_up_out, self.swap_up_in, self.wsem_up, sums, sums_in, sums_sem) = scratch[24:]
        self.sender = Sender(ssem)
        self.place = place = Place(grid)
        r, chips, c = grid.rows, grid.chips, grid.core

        def rows(ref, index):
            return ref.at[pl.ds(pl.multiple_of(index * r, r), r)]

        def spread(g, ref, jj, route, by_chip):
            def at(j, p):
                return rows(ref, p * 4 + j) if by_chip else rows(ref, j * chips + p)
            return Spread(place, self.sender, route, at, lambda j, p: rsem.at[g, j, p], c * 2 + jj, (1 - c) * 2 + jj)

        even, odd = ("z", "lo", "hi"), ("z", "hi", "lo")
        self.attn = [spread(0, m.attn, 0, even, False), spread(0, m.attn, 1, odd, False)]
        self.up = [spread(1, m.up, 0, even, False), spread(1, m.up, 1, odd, False)]
        self.down = [spread(2, m.down, 0, ("lo", "z", "hi"), True), spread(2, m.down, 1, ("hi", "z", "lo"), True)]
        self.vec = Spread(place, self.sender, even, self.vec_at, lambda j, p: vsem.at[j, p], c, 1 - c)

        z_rows = grid.side * grid.side * r

        def ffn_source(ref, quarter):
            def source(core, z):
                at = (quarter(core) * grid.nz + z) * z_rows
                return ref.at[pl.ds(pl.multiple_of(at, z_rows), z_rows)]
            return source

        def attn_source(t):
            def source(core, z):
                at = (t * grid.nz + z) * z_rows
                return m.up.at[pl.ds(pl.multiple_of(at, z_rows), z_rows), pl.ds(pl.multiple_of(core * (D // 2), D // 2), D // 2)]
            return source

        def stage(source, refs, slot, t):
            return Stage(place, self.sender, t, source, *(x.at[slot] for x in refs[:4]), tuple(x.at[slot] for x in refs[4:]))

        self.r_down = [stage(ffn_source(m.spare, lambda core, t=t: 2 * core + t), ffn, t, t) for t in range(2)]
        self.r_up = [stage(ffn_source(m.down, lambda core, t=t: 2 * t + core), ffn, 2 + t, t) for t in range(2)]
        self.r_attn = [stage(attn_source(t), attn, t, t) for t in range(4)]
        self.sums, self.sum_all = sums, SumAll(place, self.sender, sums, sums_in, sums_sem)


    def vec_at(self, j, p):
        base = self.m.x.shape[0]
        half_width = D // 2
        return self.m.spare.at[pl.ds(pl.multiple_of(base + p * 16, 16), 16), pl.ds(pl.multiple_of(j * half_width, half_width), half_width)]

    def mine(self, first, second):
        return jnp.where(self.grid.core == 0, first.astype(F32), second.astype(F32))

    def begin(self):
        grid, c = self.grid, self.grid.core
        query, key, value, out, up, down, small = self.raws
        pairs = [[(query[...], value[...]), (key[...], out[...])],
                 [(up[:, j * D : (j + 1) * D], up[:, (2 + j) * D : (3 + j) * D]) for j in range(2)]]
        for g in range(2):
            for jj in range(2):
                first, second = pairs[g][jj]
                self.pre_out[g, jj] = self.mine(second, first).astype(BF16)
        matrix, _ = lane_places(grid, grid.dev_rows)
        matrix_up, row_up = lane_places(grid, 4 * grid.dev_rows)
        here = mm(small[...], matrix)
        up_row = mm(small[...], matrix_up)[8:9]
        sub = lax.broadcasted_iota(jnp.int32, (16, D), 0)
        placed = jnp.where(sub < 8, here, jnp.where(sub == UB + row_up, jnp.broadcast_to(up_row, (16, D)), 0.0))
        width = D // 2
        self.vec_out[...] = self.mine(placed[:, width:], placed[:, :width]).astype(BF16)
        grid.barrier()
        for jj in range(2):
            self.sender.start(self.pre_out.at[0, jj], self.pre_in.at[0, jj], self.psem.at[0, jj], grid.sib())
        self.sender.start(self.vec_out, self.vec_in, self.psem.at[2, 0], grid.sib())
        for jj in range(2):
            self.sender.start(self.pre_out.at[1, jj], self.pre_in.at[1, jj], self.psem.at[1, jj], grid.sib())
        chip = self.place.chip({})
        for g, units in enumerate((self.attn, self.up)):
            for jj, unit in enumerate(units):
                self.sender.arrived(self.pre_in.at[g, jj], self.psem.at[g, jj], grid)
                own, other = self.mine(*pairs[g][jj]), self.pre_in[g, jj].astype(F32)
                both = jnp.concatenate([self.mine(own, other), self.mine(other, own)], axis=0)
                unit.at(unit.unit, chip)[...] = both.astype(BF16)
                if g == 0:
                    unit.own(("z",), sibling=False)
            if g == 0:
                self.sender.arrived(self.vec_in, self.psem.at[2, 0], grid)
                total = self.mine(placed[:, :width], placed[:, width:]) + self.vec_in[...].astype(F32)
                self.vec.at(self.vec.unit, chip)[...] = total.astype(BF16)
                self.vec.own()
                for unit in units:
                    unit.own(("lo", "hi"))
        for jj, unit in enumerate(self.down):
            r = grid.rows
            unit.at(unit.unit, chip)[...] = down[jj * r : (jj + 1) * r, :]
            unit.own(unit.route[:1])
        for unit in self.up:
            unit.own(("lo", "hi"))

    def run(self, steps):
        for step in steps:
            step()

    def need_attn(self):
        a, up = self.attn, self.up
        firsts = mix(a[0].firsts(), a[1].firsts(), self.vec.firsts())
        self.run(firsts[:6])
        for unit in up:
            unit.own(("z",), sibling=False)
        self.run(firsts[6:])
        self.run(mix(a[0].seconds(), a[1].seconds(), self.vec.seconds()))
        self.run(mix(a[0].thirds(), a[1].thirds(), self.vec.thirds()))
        for unit in a + [self.vec]:
            unit.from_sibling()
        base = self.m.x.shape[0]
        total = self.m.spare[base : base + 16, :].astype(F32)
        for p in range(1, self.grid.chips):
            total = total + self.m.spare[base + p * 16 : base + (p + 1) * 16, :].astype(F32)
        self.m.vec[...] = total
        up_firsts, down_firsts = mix(up[0].firsts(), up[1].firsts()), mix(self.down[0].firsts(), self.down[1].firsts())
        up_seconds, up_thirds = mix(up[0].seconds(), up[1].seconds()), mix(up[0].thirds(), up[1].thirds())
        down_seconds, down_thirds = mix(self.down[0].seconds(), self.down[1].seconds()), mix(self.down[0].thirds(), self.down[1].thirds())

        def own_down_z():
            for unit in self.down:
                unit.own(("z",), sibling=False)

        def own_down_last():
            for unit in self.down:
                unit.own(unit.route[2:], sibling=False)

        self.plan = [
            up_firsts,
            [own_down_z] + down_firsts + [own_down_last],
            up_seconds,
            up_thirds,
            down_seconds,
            [],
            down_thirds,
        ]
        self.next()

    def next(self):
        if self.plan:
            self.run(self.plan.pop(0))

    def during_attention(self, k):
        self.next()

    def need_up(self):
        for unit in self.up:
            unit.from_sibling()

    def during_up(self, j):
        self.next()

    def need_down(self):
        while self.plan:
            self.next()
        for unit in self.down:
            unit.from_sibling()

    def gathered(self):
        self.sender.finish()
        self.sender.started = Started(len(self.sender.started))


    def ready_down(self):
        for stage in self.r_down:
            stage.to_sibling()

    def during_back(self, j):
        if j < 2:
            self.r_down[j].add_siblings()

    def during_up_grad(self, j):
        if j % 2 == 1:
            self.r_up[j // 2].to_sibling()
        if j == 2:
            self.r_up[0].add_siblings()
        if j == 3:
            self.r_down[0].add_seconds()

    def after_first_back(self):
        self.r_up[1].add_siblings()
        self.r_down[1].add_seconds()

    def after_out(self):
        self.r_attn[0].to_sibling()
        self.r_up[0].add_seconds()
        self.r_down[0].add_thirds()

    def after_chunk(self, k, middle):
        if middle == 0 and k == 0:
            self.r_attn[0].add_siblings()
        if middle == 1 and k == 0:
            self.r_up[1].add_seconds()
            self.r_down[1].add_thirds()
        if middle == 2:
            self.r_attn[1 + k].to_sibling()
        if middle == 0 and k > 0:
            self.r_attn[k].add_siblings()
        if middle == 1 and k == 1:
            self.r_attn[0].add_seconds()
            self.r_up[0].add_thirds()
        if middle == 1 and k == 2:
            self.r_attn[1].add_seconds()
            self.r_up[1].add_thirds()
            self.r_attn[0].add_thirds()

    def ready_vec(self):
        self.sums[0] = self.m.vec_grad[...]
        self.sum_all.send(0)

    def during_finish(self, i):
        attn = self.r_attn
        if i == 0:
            attn[3].add_siblings()
            attn[2].add_seconds()
            self.sum_all.add(0)
            self.sum_all.send(1)
        if i == 1:
            attn[1].add_thirds()
            self.down_result()
        if i == 2:
            self.sum_all.add(1)
            self.sum_all.send(2)
            self.up_result()
        if i == 3:
            self.attn_result(0)

    def end(self):
        attn = self.r_attn
        attn[3].add_seconds()
        self.sum_all.add(2)
        self.sum_all.send(3)
        attn[2].add_thirds()
        self.attn_result(1)
        attn[3].add_thirds()
        self.attn_result(2)
        self.sum_all.add(3)
        self.small_result()
        self.attn_result(3)
        self.finish_results()
        self.sender.finish()

    def down_result(self):
        r, down = self.grid.rows, self.outs[5]
        for t in range(2):
            down[t * r : (t + 1) * r, :] = self.r_down[t].result()

    def trade(self, total, out, landing, sem):
        c, dr = self.grid.core, self.grid.dev_rows
        top, bottom = total[:dr], total[dr:]
        out[...] = jnp.where(c == 0, bottom, top)
        self.sender.start(out, landing, sem, self.grid.sib())
        return jnp.where(c == 0, top, bottom)

    def by_core(self, put, own, landing=None):
        for core in range(2):
            @pl.when(self.grid.core == core)
            def _(core=core):
                put(core, own)

    def put_up(self, t):
        def put(core, value):
            at = (2 * t + core) * D
            self.outs[4][:, at : at + D] = value
        return put

    def put_attn(self, t):
        query, key, value, out = self.outs[:4]

        def put(core, v):
            if t == 0:
                out[:, core * (D // 2) : (core + 1) * (D // 2)] = v
                return
            at, wide = (t - 1) * (D // 3), D // 3
            if core == 0:
                query[:, at : at + wide] = v[:, :wide]
                key[:, at : at + wide // 2] = v[:, wide:]
            else:
                key[:, at + wide // 2 : at + wide] = v[:, : wide // 2]
                value[:, at : at + wide] = v[:, wide // 2 :]
        return put

    def up_result(self):
        for t in range(2):
            mine = self.trade(self.r_up[t].result(), self.swap_up_out.at[t], self.swap_up_in.at[t], self.wsem_up.at[t])
            self.by_core(self.put_up(t), mine)

    def attn_result(self, t):
        mine = self.trade(self.r_attn[t].result(), self.swap_out.at[t], self.swap_in.at[t], self.wsem.at[t])
        self.by_core(self.put_attn(t), mine)

    def finish_results(self):
        for n, put, landing, sems in ((2, self.put_up, self.swap_up_in, self.wsem_up), (4, self.put_attn, self.swap_in, self.wsem)):
            for t in range(n):
                self.sender.arrived(landing.at[t], sems.at[t], self.grid)
                for core in range(2):
                    @pl.when(self.grid.core == 1 - core)
                    def _(core=core):
                        put(t)(core, landing[t])

    def small_result(self):
        x = self.sums[4]
        high = x.astype(BF16)
        rest = x - high.astype(F32)
        middle = rest.astype(BF16)
        low = (rest - middle.astype(F32)).astype(BF16)
        matrix, _ = lane_places(self.grid, self.grid.dev_rows)
        matrix_up, row_up = lane_places(self.grid, 4 * self.grid.dev_rows)
        narrow, wide = (mm_nt(high, k) + mm_nt(middle, k) + mm_nt(low, k) for k in (matrix, matrix_up))
        sub = lax.broadcasted_iota(jnp.int32, (16, 128), 0)
        up = jnp.sum(jnp.where(sub == UB + row_up, wide, 0.0), axis=0, keepdims=True)
        self.outs[6][...] = jnp.where(sub < 8, narrow, jnp.broadcast_to(up, (16, 128)))

    @staticmethod
    def sends(grid):
        return 5 + 7 * Spread.sends(grid) + 8 * Stage.sends(grid) + 6 + peer_count(grid)

    @staticmethod
    def scratch(grid):
        chips, dr = grid.chips, grid.dev_rows
        dma = pltpu.SemaphoreType.DMA
        return [
            pltpu.VMEM((2, 2, dr, D), BF16),
            pltpu.VMEM((2, 2, dr, D), BF16),
            pltpu.VMEM((16, D // 2), BF16),
            pltpu.VMEM((16, D // 2), BF16),
            dma((3, 4, chips)),
            dma((2, chips)),
            dma((3, 2)),
            dma((Network.sends(grid),)),
        ] + Stage.scratch(grid, 4, D) + Stage.scratch(grid, 4, D // 2) + [
            pltpu.VMEM((4, dr, D // 2), F32),
            pltpu.VMEM((4, dr, D // 2), F32),
            dma((4,)),
            pltpu.VMEM((2, dr, D), F32),
            pltpu.VMEM((2, dr, D), F32),
            dma((2,)),
            pltpu.VMEM((5, 16, D), F32),
            pltpu.VMEM((peer_count(grid), 16, D), F32),
            dma((peer_count(grid),)),
        ]


class Started(list):
    def __init__(self, offset):
        super().__init__()
        self.offset = offset

    def __len__(self):
        return self.offset + super().__len__()


def fused_kernel(grid, memory, bucket, length, tokens_in, out_grad_in, pool_grad, *refs):
    raws, (layer_out, pools, token_grad), outs, (keep_qkv, keep_norm), scratch = refs[:7], refs[7:10], refs[10:17], refs[17:19], refs[19:]
    grid.place()
    m = Memory(scratch[:memory])
    net = Network(grid, m, raws, outs, scratch[memory:])
    layer_steps(m, net, bucket, length, tokens_in, out_grad_in, pool_grad, layer_out, pools, token_grad, keep_qkv, keep_norm, grid.rows)


def layer_fused(grid, bucket, length, tokens, out_grad, pool_grad, query, key, value, out, up, down, small):
    count, dr = tokens.shape[0], grid.dev_rows
    v, any_spec, smem = pl.BlockSpec(memory_space=pltpu.VMEM), pl.BlockSpec(memory_space=pl.ANY), pl.BlockSpec(memory_space=pltpu.SMEM)
    s = jax.ShapeDtypeStruct
    memory = Memory.shapes(count)
    return pl.pallas_call(
        functools.partial(fused_kernel, grid, len(memory)),
        out_shape=[s((count, D), BF16), s(pool_grad.shape, F32), s((count, D), F32)] + [s((dr, D), F32)] * 4
        + [s((dr, 4 * D), F32), s((4 * dr, D), F32), s((16, 128), F32), s((3, count, D), BF16), s((count, D), F32)],
        in_specs=[smem, smem, any_spec, any_spec] + [v] * 8,
        out_specs=[any_spec, v, any_spec] + [v] * 7 + [any_spec, any_spec],
        scratch_shapes=memory + Network.scratch(grid),
        compiler_params=pltpu.CompilerParams(collective_id=2, has_side_effects=True, vmem_limit_bytes=255 * 2**18),
    )(bucket, length, tokens, out_grad, pool_grad, query, key, value, out, up, down, small)[:10]
def body(
    grid,
    tokens,
    block_bucket,
    lengths,
    query_weight,
    query_bias,
    key_weight,
    value_weight,
    value_bias,
    out_weight,
    out_bias,
    first_gain,
    first_shift,
    up_weight,
    up_bias,
    down_weight,
    down_bias,
    second_gain,
    second_shift,
    out_grad,
    pool_grad,
):
    rank = lax.axis_index("dp") * lax.axis_size("fsdp") + lax.axis_index("fsdp")
    dr, n, s, pad, r = grid.dev_rows, grid.nz, grid.side, grid.pad, grid.rows
    if pad == r:
        vectors = (query_bias, value_bias, out_bias, first_gain, first_shift, down_bias, second_gain, second_shift)
        small = jnp.concatenate([
            jnp.pad(jnp.stack(vectors), ((0, 0), (0, 128 - dr))),
            jnp.pad(up_bias[None], ((0, 7), (0, 128 - 4 * dr)))])
        layer_out, pools, token_grad, g_query, g_key, g_value, g_out, g_up, g_down, small = layer_fused(
            grid, block_bucket, lengths, tokens, out_grad, pool_grad, query_weight, key_weight, value_weight, out_weight,
            up_weight, down_weight, small)
        small, wide = small[:8, :dr], small[8, : 4 * dr]
        return (
            layer_out, pools, token_grad, g_query, small[QB], g_key, g_value, small[VB], g_out, small[OB], small[G1], small[S1],
            g_up, wide, g_down, small[DB], small[G2], small[S2],
        )
    raw_attn = jnp.stack([query_weight, key_weight, value_weight, out_weight])
    raw_up = up_weight.reshape(dr, 4, D).transpose(1, 0, 2)
    raw_down = down_weight.reshape(4, dr, D)
    small = jnp.stack([query_bias, value_bias, out_bias, first_gain, first_shift, down_bias, second_gain, second_shift])
    small = lax.dynamic_update_slice(jnp.zeros((16, D), BF16), small, (0, rank * dr))
    wide = lax.dynamic_update_slice(jnp.zeros((16 * D,), BF16), up_bias, (rank * 4 * dr,)).reshape(16, D)
    raw_vec = jnp.stack([small, wide])
    w_attn, w_up, w_down, w_vec = gather_all(grid, raw_attn, raw_up, raw_down, raw_vec)
    w_attn, w_up, w_down = (w[:, :, :r].reshape(4 * D, D) for w in (w_attn, w_up, w_down))
    vec = jnp.sum(w_vec.astype(F32), axis=1)
    vec = jnp.concatenate([vec[0, :8], vec[1, :8]])
    layer_out, pools, token_grad, g_attn, g_up, g_down, g_vec = layer_local(
        block_bucket, lengths, tokens, out_grad, pool_grad, vec, w_attn, w_up, w_down)
    panels = g_attn[D:].reshape(3, D, 3, D // 3).transpose(2, 1, 0, 3).reshape(3 * D, D)
    g_attn = jnp.concatenate([panels, g_attn[:D]])

    def blocks(grad):
        return jnp.pad(grad.reshape(-1, r, D), ((0, 0), (0, pad - r), (0, 0)))

    g_attn, g_up = (blocks(g).reshape(4, n, s, s, pad, D) for g in (g_attn, g_up))
    g_down = blocks(g_down).reshape(n, s, s, 4, pad, D)
    o_attn, o_up, o_down, o_vec = reduce_all(grid, g_attn, g_up, g_down, g_vec)
    small = lax.dynamic_slice(o_vec, (0, rank * dr), (8, dr))
    wide = lax.dynamic_slice(o_vec[8:12].reshape(4 * D), (rank * 4 * dr,), (4 * dr,))
    return (
        layer_out,
        pools,
        token_grad,
        o_attn[0],
        small[QB],
        o_attn[1],
        o_attn[2],
        small[VB],
        o_attn[3],
        small[OB],
        small[G1],
        small[S1],
        o_up.transpose(1, 0, 2).reshape(dr, 4 * D),
        wide,
        o_down.reshape(4 * dr, D),
        small[DB],
        small[G2],
        small[S2],
    )


def solution(mesh):
    whole, line = P(("dp", "fsdp"), None), P(("dp", "fsdp"))
    grid = Grid(mesh.shape["dp"], mesh.shape["fsdp"])
    return jax.shard_map(
        functools.partial(body, grid),
        mesh=mesh,
        in_specs=(
            whole, line, line, whole, line, whole, whole, line, whole, line,
            line, line, whole, line, whole, line, line, line, whole, whole,
        ),
        out_specs=(
            whole, whole, whole, whole, line, whole, whole, line, whole, line,
            line, line, whole, line, whole, line, line, line,
        ),
        check_vma=False,
    )
```

```python
import functools
import math

import jax
import jax.numpy as jnp
from jax import lax
from jax.experimental import pallas as pl
from jax.experimental.pallas import tpu as pltpu
from jax.sharding import PartitionSpec as P

MESH = pl.DeviceIdType.MESH
D = 768
F32 = jnp.float32
BF16 = jnp.bfloat16


class Grid:
    def __init__(self, nz, nf):
        self.nz = nz
        self.side = math.isqrt(nf // 2)
        assert 2 * self.side * self.side == nf
        self.chips = nz * self.side * self.side
        self.rows = D // self.chips
        self.dev_rows = self.rows // 2
        self.pad = -(-self.rows // 16) * 16

    def place(self):
        s = self.side
        self.z = lax.axis_index("dp")
        f = lax.axis_index("fsdp")
        self.core = lax.rem(f, 2)
        self.lo = lax.rem(f // 2, s)
        self.hi = f // (2 * s)
        self.beside = self.sib()

    def dev(self, z, hi, lo, core):
        return (z, (hi * self.side + lo) * 2 + core)

    def sib(self):
        return self.dev(self.z, self.hi, self.lo, 1 - self.core)

    def zs(self, d):
        return lax.rem(self.z + d, self.nz)

    def los(self, d):
        return lax.rem(self.lo + d, self.side)

    def his(self, d):
        return lax.rem(self.hi + d, self.side)

    def z_peer(self, d):
        return self.dev(self.zs(d), self.hi, self.lo, self.core)

    def lo_peer(self, d):
        return self.dev(self.z, self.hi, self.los(d), self.core)

    def hi_peer(self, d):
        return self.dev(self.z, self.his(d), self.lo, self.core)

    def chip(self, z, hi, lo):
        return (z * self.side + hi) * self.side + lo

    def peers(self):
        out = [self.sib()]
        out += [self.z_peer(d) for d in range(1, self.nz)]
        out += [self.lo_peer(d) for d in range(1, self.side)]
        out += [self.hi_peer(d) for d in range(1, self.side)]
        return out

    def barrier(self):
        sem = pltpu.get_barrier_semaphore()
        peers = self.peers()
        for peer in peers:
            pl.semaphore_signal(sem, inc=1, device_id=peer, device_id_type=MESH)
        pl.semaphore_wait(sem, len(peers))


class Sender:
    def __init__(self, sems):
        self.sems = sems
        self.started = []

    def start(self, src, dst, recv_sem, device):
        copy = pltpu.make_async_remote_copy(
            src_ref=src,
            dst_ref=dst,
            send_sem=self.sems.at[len(self.started)],
            recv_sem=recv_sem,
            device_id=device,
            device_id_type=MESH,
        )
        copy.start()
        self.started.append(copy)
        return copy

    def arrived(self, dst, recv_sem, grid):
        pltpu.make_async_remote_copy(
            src_ref=dst,
            dst_ref=dst,
            send_sem=self.sems.at[0],
            recv_sem=recv_sem,
            device_id=grid.beside,
            device_id_type=MESH,
        ).wait_recv()

    def finish(self):
        for copy in self.started:
            copy.wait_send()


class Gather:
    def __init__(self, grid, sender, at, sem, per_core=2):
        self.grid, self.sender, self.at, self.sem = grid, sender, at, sem
        self.per_core = per_core

    def mine(self, jj):
        return self.grid.core * self.per_core + jj

    def send(self, j, p, device):
        self.sender.start(self.at(j, p), self.at(j, p), self.sem(j, p), device)

    def wait(self, j, p):
        self.sender.arrived(self.at(j, p), self.sem(j, p), self.grid)

    def own(self):
        g = self.grid
        for jj in range(self.per_core):
            j, p = self.mine(jj), g.chip(g.z, g.hi, g.lo)
            for d in range(1, g.nz):
                self.send(j, p, g.z_peer(d))
            self.spread(j, p)

    def spread(self, j, p):
        g = self.grid
        for d in range(1, g.side):
            self.send(j, p, g.lo_peer(d))
        for d in range(1, g.side):
            self.send(j, p, g.hi_peer(d))
        self.send(j, p, g.sib())

    def along_z(self, d):
        g = self.grid
        for jj in range(self.per_core):
            j, p = self.mine(jj), g.chip(g.zs(d), g.hi, g.lo)
            self.wait(j, p)
            self.spread(j, p)

    def second(self, d):
        g = self.grid
        for jj in range(self.per_core):
            j = self.mine(jj)
            for e in range(1, g.side):
                if jj % 2 == 0:
                    p = g.chip(g.zs(d), g.hi, g.los(e))
                else:
                    p = g.chip(g.zs(d), g.his(e), g.lo)
                self.wait(j, p)
                for k in range(1, g.side):
                    self.send(j, p, g.hi_peer(k) if jj % 2 == 0 else g.lo_peer(k))
                self.send(j, p, g.sib())

    def third(self, d):
        g = self.grid
        for jj in range(self.per_core):
            j = self.mine(jj)
            for e in range(1, g.side):
                for k in range(g.side):
                    if jj % 2 == 0:
                        p = g.chip(g.zs(d), g.his(e), g.los(k))
                    else:
                        p = g.chip(g.zs(d), g.his(k), g.los(e))
                    self.wait(j, p)
                    self.send(j, p, g.sib())

    def sibling(self):
        g = self.grid
        for jj in range(self.per_core):
            j = (1 - g.core) * self.per_core + jj
            for d in range(g.nz):
                for e in range(g.side):
                    for k in range(g.side):
                        self.wait(j, g.chip(g.zs(d), g.his(e), g.los(k)))

    @staticmethod
    def sends(grid, per_core):
        n, s = grid.nz, grid.side
        return per_core * (n - 1 + n * (s - 1) + n * s * (s - 1) + grid.chips)


def join_rows(grid, low, high):
    parts = [low.astype(F32), high.astype(F32)]
    if grid.pad != grid.rows:
        parts.append(jnp.zeros((grid.pad - grid.rows, low.shape[1]), F32))
    return jnp.concatenate(parts, axis=0).astype(BF16)


def gather_kernel(grid, attn_ref, up_ref, down_ref, vec_ref, w_attn, w_up, w_down, w_vec,
                  pre_ref, pre_vec, stage, stage_vec, rsem, vsem, ssem, psem, lsem):
    grid.place()
    grid.barrier()
    sender = Sender(ssem)
    c = grid.core
    me = grid.chip(grid.z, grid.hi, grid.lo)
    raws = (attn_ref, up_ref)
    for g, raw in enumerate(raws):
        for jj in range(2):
            sender.start(raw.at[(1 - c) * 2 + jj], pre_ref.at[g, jj], psem.at[g, jj], grid.sib())
    sender.start(vec_ref.at[1 - c], pre_vec, psem.at[2, 0], grid.sib())

    groups = [
        Gather(grid, sender, lambda j, p: w_attn.at[j, p], lambda j, p: rsem.at[0, j, p]),
        Gather(grid, sender, lambda j, p: w_up.at[j, p], lambda j, p: rsem.at[1, j, p]),
        Gather(grid, sender, lambda j, p: w_down.at[p, j], lambda j, p: rsem.at[2, j, p]),
    ]
    vec = Gather(grid, sender, lambda j, p: w_vec.at[j, p], lambda j, p: vsem.at[j, p], per_core=1)

    def put(src, dst, k):
        copy = pltpu.make_async_copy(src, dst, lsem.at[k])
        copy.start()
        copy.wait()

    def assemble(g):
        for jj in range(2):
            if g < 2:
                sender.arrived(pre_ref.at[g, jj], psem.at[g, jj], grid)
                own, other = raws[g][c * 2 + jj], pre_ref[g, jj]
                first = jnp.where(c == 0, own.astype(F32), other.astype(F32))
                last = jnp.where(c == 0, other.astype(F32), own.astype(F32))
            else:
                first, last = down_ref[2 * jj], down_ref[2 * jj + 1]
            stage[jj] = join_rows(grid, first, last)
            put(stage.at[jj], groups[g].at(c * 2 + jj, me), 0)

    assemble(0)
    groups[0].own()
    sender.arrived(pre_vec, psem.at[2, 0], grid)
    stage_vec[...] = (vec_ref[c].astype(F32) + pre_vec[...].astype(F32)).astype(BF16)
    put(stage_vec, w_vec.at[c, me], 0)
    vec.own()
    def z_steps(g):
        for d in range(grid.nz - 1, 0, -1):
            g.along_z(d)

    def second_steps(g):
        for d in range(grid.nz, 0, -1):
            g.second(d)

    def third_steps(g):
        for d in range(grid.nz, 0, -1):
            g.third(d)

    z_steps(vec)
    z_steps(groups[0])
    assemble(1)
    groups[1].own()
    second_steps(vec)
    second_steps(groups[0])
    z_steps(groups[1])
    assemble(2)
    groups[2].own()
    third_steps(vec)
    third_steps(groups[0])
    second_steps(groups[1])
    z_steps(groups[2])
    third_steps(groups[1])
    second_steps(groups[2])
    third_steps(groups[2])
    for g in [vec] + groups:
        g.sibling()
    sender.finish()


def gather_all(grid, raw_attn, raw_up, raw_down, raw_vec):
    n, pad, dr = grid.chips, grid.pad, grid.dev_rows
    nsend = 5 + 3 * Gather.sends(grid, 2) + Gather.sends(grid, 1)
    any_spec = pl.BlockSpec(memory_space=pl.ANY)
    vmem = pl.BlockSpec(memory_space=pltpu.VMEM)
    return pl.pallas_call(
        functools.partial(gather_kernel, grid),
        out_shape=[
            jax.ShapeDtypeStruct((4, n, pad, D), BF16),
            jax.ShapeDtypeStruct((4, n, pad, D), BF16),
            jax.ShapeDtypeStruct((n, 4, pad, D), BF16),
            jax.ShapeDtypeStruct((2, n, 16, D), BF16),
        ],
        in_specs=[vmem] * 4,
        out_specs=[any_spec] * 4,
        scratch_shapes=[
            pltpu.VMEM((2, 2, dr, D), BF16),
            pltpu.VMEM((16, D), BF16),
            pltpu.VMEM((2, pad, D), BF16),
            pltpu.VMEM((16, D), BF16),
            pltpu.SemaphoreType.DMA((3, 4, n)),
            pltpu.SemaphoreType.DMA((2, n)),
            pltpu.SemaphoreType.DMA((nsend,)),
            pltpu.SemaphoreType.DMA((3, 2)),
            pltpu.SemaphoreType.DMA((1,)),
        ],
        compiler_params=pltpu.CompilerParams(collective_id=0, has_side_effects=True, vmem_limit_bytes=32 * 2**20),
    )(raw_attn, raw_up, raw_down, raw_vec)
class Reduce:
    def __init__(self, grid, sender, part, held, second, third, last, sems):
        self.grid, self.sender, self.part = grid, sender, part
        self.held, self.from_second, self.from_third, self.from_z = held, second, third, last
        self.sem_sib, self.sem_second, self.sem_third, self.sem_z = sems

    def to_sibling(self, d):
        g = self.grid
        z = g.zs(d)
        for jj in range(2):
            j = (1 - g.core) * 2 + jj
            self.sender.start(self.part(j, z), self.held.at[jj, z], self.sem_sib.at[jj, z], g.sib())

    def add_sibling(self, d):
        g, s = self.grid, self.grid.side
        z = g.zs(d)
        for jj in range(2):
            held = self.held.at[jj, z]
            self.sender.arrived(held, self.sem_sib.at[jj, z], g)
            own = self.part(g.core * 2 + jj, z)
            for h in range(s):
                def add(l, carry, h=h):
                    held[h, l] = (held[h, l].astype(F32) + own[h, l].astype(F32)).astype(BF16)
                    return carry
                lax.fori_loop(0, s, add, 0)
            for k in range(1, s):
                if jj % 2 == 0:
                    src, peer = held.at[g.his(k)], g.hi_peer(k)
                else:
                    src, peer = held.at[:, g.los(k)], g.lo_peer(k)
                self.sender.start(src, self.from_second.at[jj, s - k - 1, z], self.sem_second.at[jj, s - k - 1, z], peer)

    def add_second(self, d):
        g, s = self.grid, self.grid.side
        z = g.zs(d)
        for jj in range(2):
            for k in range(s - 1):
                self.sender.arrived(self.from_second.at[jj, k, z], self.sem_second.at[jj, k, z], g)
            for e in range(s):
                at = self.held.at[jj, z, g.hi, e] if jj % 2 == 0 else self.held.at[jj, z, e, g.lo]
                total = at[...].astype(F32)
                for k in range(s - 1):
                    total = total + self.from_second[jj, k, z, e].astype(F32)
                at[...] = total.astype(BF16)
            for k in range(1, s):
                if jj % 2 == 0:
                    src, peer = self.held.at[jj, z, g.hi, g.los(k)], g.lo_peer(k)
                else:
                    src, peer = self.held.at[jj, z, g.his(k), g.lo], g.hi_peer(k)
                self.sender.start(src, self.from_third.at[jj, s - k - 1, z], self.sem_third.at[jj, s - k - 1, z], peer)

    def own(self, jj, z):
        g, s = self.grid, self.grid.side
        for k in range(s - 1):
            self.sender.arrived(self.from_third.at[jj, k, z], self.sem_third.at[jj, k, z], g)
        total = self.held[jj, z, g.hi, g.lo].astype(F32)
        for k in range(s - 1):
            total = total + self.from_third[jj, k, z].astype(F32)
        return total

    def add_third(self, d):
        g = self.grid
        z = g.zs(d)
        for jj in range(2):
            at = self.held.at[jj, z, g.hi, g.lo]
            at[...] = self.own(jj, z).astype(BF16)
            self.sender.start(at, self.from_z.at[jj, g.nz - d - 1], self.sem_z.at[jj, g.nz - d - 1], g.z_peer(d))

    def result(self, jj):
        g = self.grid
        total = self.own(jj, g.z)
        for k in range(g.nz - 1):
            self.sender.arrived(self.from_z.at[jj, k], self.sem_z.at[jj, k], g)
            total = total + self.from_z[jj, k].astype(F32)
        return total

    @staticmethod
    def sends(grid):
        n, s = grid.nz, grid.side
        return 2 * (n + n * (s - 1) * 2 + n - 1)

    @staticmethod
    def scratch(grid, groups):
        n, s, pad = grid.nz, grid.side, grid.pad
        return [
            pltpu.VMEM((groups, 2, n, s, s, pad, D), BF16),
            pltpu.VMEM((groups, 2, s - 1, n, s, pad, D), BF16),
            pltpu.VMEM((groups, 2, s - 1, n, pad, D), BF16),
            pltpu.VMEM((groups, 2, n - 1, pad, D), BF16),
            pltpu.SemaphoreType.DMA((groups, 2, n)),
            pltpu.SemaphoreType.DMA((groups, 2, s - 1, n)),
            pltpu.SemaphoreType.DMA((groups, 2, s - 1, n)),
            pltpu.SemaphoreType.DMA((groups, 2, n - 1)),
        ]


def sum_everywhere(grid, sender, own, landing, sem):
    steps = [[grid.sib()],
             [grid.lo_peer(d) for d in range(1, grid.side)],
             [grid.hi_peer(d) for d in range(1, grid.side)],
             [grid.z_peer(d) for d in range(1, grid.nz)]]
    slot = 0
    for n, peers in enumerate(steps):
        for k, peer in enumerate(peers):
            sender.start(own.at[n], landing.at[slot + len(peers) - 1 - k], sem.at[slot + len(peers) - 1 - k], peer)
        total = own[n]
        for k in range(len(peers)):
            sender.arrived(landing.at[slot + k], sem.at[slot + k], grid)
            total = total + landing[slot + k]
        slot += len(peers)
        own[n + 1] = total


def peer_count(grid):
    return 1 + 2 * (grid.side - 1) + grid.nz - 1


def reduce_kernel(grid, g_attn, g_up, g_down, g_vec, o_attn, o_up, o_down, o_vec,
                  held, second, third, last, s1, s2, s3, s4, swap_out, swap_in, wsem, vec, vec_in, vsem, ssem):
    grid.place()
    grid.barrier()
    sender = Sender(ssem)
    c = grid.core
    parts = [lambda j, z: g_attn.at[j, z], lambda j, z: g_up.at[j, z], lambda j, z: g_down.at[z, :, :, j]]
    groups = [
        Reduce(grid, sender, parts[g], held.at[g], second.at[g], third.at[g], last.at[g],
               (s1.at[g], s2.at[g], s3.at[g], s4.at[g]))
        for g in range(3)
    ]
    order = [groups[2], groups[1], groups[0]]
    n = grid.nz
    for g in order:
        for d in range(n, 0, -1):
            g.to_sibling(d)
    vec[0] = g_vec[...]
    for g in order:
        for d in range(n, 0, -1):
            g.add_sibling(d)
    for g in order:
        for d in range(n, 0, -1):
            g.add_second(d)
    for g in order:
        for d in range(n - 1, 0, -1):
            g.add_third(d)
    sum_everywhere(grid, sender, vec, vec_in, vsem)
    o_vec[...] = vec[4]
    r, dr = grid.rows, grid.dev_rows
    for i, (g, out) in enumerate(((groups[1], o_up), (groups[0], o_attn))):
        for jj in range(2):
            total = g.result(jj)
            top, bottom = total[:dr], total[dr:r]
            out[c * 2 + jj] = jnp.where(c == 0, top, bottom)
            swap_out[i, jj] = jnp.where(c == 0, bottom, top)
            sender.start(swap_out.at[i, jj], swap_in.at[i, jj], wsem.at[i, jj], grid.sib())
    for jj in range(2):
        o_down[jj] = groups[2].result(jj)[:r]
    for i, out in enumerate((o_up, o_attn)):
        for jj in range(2):
            sender.arrived(swap_in.at[i, jj], wsem.at[i, jj], grid)
            out[(1 - c) * 2 + jj] = swap_in[i, jj]
    sender.finish()


def reduce_all(grid, g_attn, g_up, g_down, g_vec):
    n, s, pad, dr = grid.nz, grid.side, grid.pad, grid.dev_rows
    nsend = 3 * Reduce.sends(grid) + 4 + peer_count(grid)
    vmem = pl.BlockSpec(memory_space=pltpu.VMEM)
    return pl.pallas_call(
        functools.partial(reduce_kernel, grid),
        out_shape=[
            jax.ShapeDtypeStruct((4, dr, D), F32),
            jax.ShapeDtypeStruct((4, dr, D), F32),
            jax.ShapeDtypeStruct((2, grid.rows, D), F32),
            jax.ShapeDtypeStruct((16, D), F32),
        ],
        in_specs=[vmem] * 4,
        out_specs=[vmem] * 4,
        scratch_shapes=Reduce.scratch(grid, 3) + [
            pltpu.VMEM((2, 2, dr, D), F32),
            pltpu.VMEM((2, 2, dr, D), F32),
            pltpu.SemaphoreType.DMA((2, 2)),
            pltpu.VMEM((5, 16, D), F32),
            pltpu.VMEM((peer_count(grid), 16, D), F32),
            pltpu.SemaphoreType.DMA((peer_count(grid),)),
            pltpu.SemaphoreType.DMA((nsend,)),
        ],
        compiler_params=pltpu.CompilerParams(collective_id=1, has_side_effects=True, vmem_limit_bytes=56 * 2**20),
    )(g_attn, g_up, g_down, g_vec)
HEADS = 12
HD = 64
ROW = 512
BLOCK = 64
PER_ROW = ROW // BLOCK
NEG = -1e30
TM = 256


def mm(a, b):
    return jnp.dot(a, b, preferred_element_type=F32)


def mm_nt(a, b):
    return lax.dot_general(a, b, (((1,), (1,)), ((), ())), preferred_element_type=F32)


def mm_tn(a, b):
    return lax.dot_general(a, b, (((0,), (0,)), ((), ())), preferred_element_type=F32)


def tile(i, size):
    if isinstance(i, int):
        return pl.ds(i * size, size)
    return pl.ds(pl.multiple_of(i * size, size), size)


def loop(n, f, unroll=1):
    def step(i, carry):
        for k in range(unroll):
            f(i * unroll + k)
        return carry
    lax.fori_loop(0, n // unroll, step, 0)


def row_blocks(bucket_ref, length_ref, row):
    starts, lens = [], []
    for b in range(PER_ROW):
        stride = bucket_ref[row * PER_ROW + b] // BLOCK
        first = b // stride * stride
        starts.append(first)
        lens.append(length_ref[row * PER_ROW + first])
    return starts, lens


def pick(ids, values):
    out = jnp.zeros_like(ids)
    for b, value in enumerate(values):
        out = jnp.where(ids == b, value, out)
    return out


def write_mask(mask_ref, starts, lens):
    query = pick(lax.broadcasted_iota(jnp.int32, (BLOCK, ROW), 1) // BLOCK, starts)
    place = lax.broadcasted_iota(jnp.int32, (BLOCK, ROW), 0)
    for b in range(PER_ROW):
        limit = lens[b] - (b - starts[b]) * BLOCK
        allowed = (query == starts[b]) & (place < limit)
        mask_ref[b * BLOCK : (b + 1) * BLOCK, :] = jnp.where(allowed, 0.0, NEG)


def member_matrix(starts, lens):
    lane = lax.broadcasted_iota(jnp.int32, (PER_ROW, ROW), 1)
    token_start = pick(lane // BLOCK, starts)
    token_len = pick(lane // BLOCK, lens)
    valid = lane - token_start * BLOCK < token_len
    block = lax.broadcasted_iota(jnp.int32, (PER_ROW, ROW), 0)
    member = jnp.where((token_start == pick(block, starts)) & valid, 1.0, 0.0).astype(F32)
    lens_col = pick(lax.broadcasted_iota(jnp.int32, (PER_ROW, 1), 0), lens)
    return member, 1.0 / lens_col.astype(F32)


def layer_norm_parts(v):
    center = v - jnp.mean(v, axis=-1, keepdims=True)
    spread = jnp.mean(center * center, axis=-1, keepdims=True)
    scale = lax.rsqrt(spread + 1e-05)
    return center * scale, scale


def layer_norm_back(grad, normed, scale, gain):
    g = grad * gain
    return scale * (g - jnp.mean(g, axis=-1, keepdims=True) - normed * jnp.mean(g * normed, axis=-1, keepdims=True))


def gelu_both(x):
    t = 1.0 / (1.0 + 0.23164189 * jnp.abs(x))
    density = jnp.exp(x * x * -0.5 - 0.9189385332046727)
    poly = ((((1.330274429 * t - 1.821255978) * t + 1.781477937) * t - 0.356563782) * t + 0.319381530) * t
    tail = poly * density
    phi = jnp.where(x < 0, tail, 1.0 - tail)
    return x * phi, phi + x * density


def half(shape, axis, h):
    return lax.broadcasted_iota(jnp.int32, shape, axis) // HD == h


def attend_pair_back(queries, keys, values, context, logs, mask, grad_context, grad_q, grad_k, grad_v, row, pair, chunk=256):
    rows, cols = tile(row, ROW), tile(pair, 2 * HD)
    key_slab, value_slab = keys[rows, cols], values[rows, cols]
    key_turned = key_slab.astype(F32).T.astype(BF16)
    lane = [half((ROW, 2 * HD), 1, h) for h in range(2)]
    only_k = [jnp.where(lane[h], key_slab.astype(F32), 0.0).astype(BF16) for h in range(2)]
    only_v = [jnp.where(lane[h], value_slab.astype(F32), 0.0).astype(BF16) for h in range(2)]
    sums = []
    for c in range(ROW // chunk):
        part = tile(row * (ROW // chunk) + c, chunk)
        query_slab, grad_slab = queries[part, cols], grad_context[part, cols]
        dot = (grad_slab.astype(F32) * context[part, cols].astype(F32)).T
        gq, gk, gv = [], [], []
        for h in range(2):
            delta = jnp.sum(dot[h * HD : (h + 1) * HD], axis=0, keepdims=True)
            s = mm_nt(only_k[h], query_slab) + mask[rows, c * chunk : (c + 1) * chunk]
            p = jnp.exp(s - logs[row, pair, h : h + 1, c * chunk : (c + 1) * chunk])
            gp = mm_nt(only_v[h], grad_slab)
            gs = (p * (gp - delta)).astype(BF16)
            gv.append(mm(p.astype(BF16), grad_slab))
            gk.append(mm(gs, query_slab))
            gq.append(mm(key_turned, gs))
        turned = jnp.where(half((2 * HD, chunk), 0, 0), gq[0], gq[1]) * 0.125
        grad_q[part, cols] = turned.T.astype(BF16)
        now = (jnp.where(lane[0], gk[0], gk[1]), jnp.where(lane[0], gv[0], gv[1]))
        sums = now if c == 0 else tuple(a + b for a, b in zip(sums, now))
    grad_k[rows, cols] = sums[0].astype(BF16)
    grad_v[rows, cols] = sums[1].astype(BF16)


def attend_pair_rows(queries, keys, values, context, logs, mask, row, pair, chunk=256):
    rows, cols = tile(row, ROW), tile(pair, 2 * HD)
    key_slab, value_slab = keys[rows, cols], values[rows, cols]
    for c in range(ROW // chunk):
        part = tile(row * (ROW // chunk) + c, chunk)
        query_slab = queries[part, cols]
        parts, cols_log = [], []
        lane = [half((chunk, 2 * HD), 1, h) for h in range(2)]
        for h in range(2):
            only = jnp.where(lane[h], query_slab.astype(F32), 0.0).astype(BF16)
            s = mm_nt(only, key_slab) + mask[part, :ROW]
            peak = jnp.max(s, axis=1, keepdims=True)
            e = jnp.exp(s - peak)
            total = jnp.sum(e, axis=1, keepdims=True)
            cols_log.append(peak + jnp.log(total))
            parts.append(mm(e.astype(BF16), value_slab) * (1.0 / total))
        context[part, cols] = jnp.where(lane[0], parts[0], parts[1]).astype(BF16)
        both = jnp.where(lane[0], cols_log[0], cols_log[1]).T
        for h in range(2):
            logs[row, pair, h : h + 1, c * chunk : (c + 1) * chunk] = both[h * HD : h * HD + 1]


QB, VB, OB, G1, S1, DB, G2, S2 = range(8)
UB = 8


def after_attention(tokens, context, w_out, vec, normed, scale, hidden, i, tm):
    rows = tile(i, tm)
    first = tokens[rows, :].astype(F32) + mm(context[rows, :], w_out) + vec[OB : OB + 1, :]
    n, r = layer_norm_parts(first)
    normed[rows, :] = n
    scale[rows, :64] = jnp.broadcast_to(r, (tm, 64))
    hidden[rows, :] = (n * vec[G1 : G1 + 1, :] + vec[S1 : S1 + 1, :]).astype(BF16)


WIDTHS = (D, 2 * D // 3, D // 3, D // 6, D // 12)


def split_low(x):
    high = x.astype(BF16)
    return high, (x - high.astype(F32)).astype(BF16)


def pool_row(normed, vec, layer_out, pools, pool_grad, out_grad, total, starts, lens, row):
    rows = pl.ds(row * ROW, ROW)
    member, inverse = member_matrix(starts, lens)
    member = member.astype(BF16)
    outputs = normed[rows, :] * vec[G2 : G2 + 1, :] + vec[S2 : S2 + 1, :]
    layer_out[rows, :] = outputs.astype(BF16)
    high, low = split_low(outputs)
    avg = (mm(member, high) + mm(member, low)) * inverse
    square = avg * avg
    blocks = pl.ds(row * PER_ROW, PER_ROW)
    grad = None
    at = 0
    for width in WIDTHS:
        r = lax.rsqrt(jnp.sum(square[:, :width], axis=-1, keepdims=True) / width + 1e-06)
        lead = avg[:, :width]
        pools[blocks, at : at + width] = lead * r
        g = pool_grad[blocks, at : at + width]
        back = g * r - lead * (r * r * r * (jnp.sum(g * lead, axis=-1, keepdims=True) / width))
        if width % 128:
            wide = -(-width // 128) * 128
            back = jnp.concatenate([back, jnp.zeros((PER_ROW, wide - width), F32)], axis=1)
        if grad is None:
            grad = back
        else:
            grad = jnp.concatenate([grad[:, : back.shape[1]] + back, grad[:, back.shape[1] :]], axis=1)
        at += width
    high, low = split_low(grad * inverse)
    both = jnp.concatenate([high, low], axis=0)
    total[rows, :] = out_grad[rows, :].astype(F32) + mm_tn(jnp.concatenate([member, member], axis=0), both)


def add_row(vec_grad, k, values):
    vec_grad[k : k + 1, :] += jnp.sum(values, axis=0, keepdims=True)


def second_norm_back(total, normed, scale, vec, vec_grad, branch, i, tm):
    rows = tile(i, tm)
    g, n = total[rows, :], normed[rows, :]
    add_row(vec_grad, G2, g * n)
    add_row(vec_grad, S2, g)
    back = layer_norm_back(g, n, scale[rows, 64:65], vec[G2 : G2 + 1, :])
    total[rows, :] = back
    low = back.astype(BF16)
    branch[rows, :] = low
    add_row(vec_grad, DB, low.astype(F32))


def turn(x, out, tm=256):
    for i in range(x.shape[0] // tm):
        for j in range(x.shape[1] // tm):
            out[j * tm : (j + 1) * tm, i * tm : (i + 1) * tm] = x[i * tm : (i + 1) * tm, j * tm : (j + 1) * tm].T
class Memory:
    NAMES = ("attn", "up", "down", "spare", "act", "slope", "x", "ctx", "hidden", "norm", "total",
             "scale", "logs", "vec", "vec_grad", "lsem")

    def __init__(self, refs):
        for name, ref in zip(self.NAMES, refs):
            setattr(self, name, ref)

    @staticmethod
    def shapes(tokens):
        v = pltpu.VMEM
        weights = [v((4 * D, D), BF16)] * 4
        return weights + [
            v((4, tokens, D), BF16), v((4, tokens, D), BF16),
            v((tokens, D), BF16), v((tokens, D), BF16), v((tokens, D), BF16),
            v((tokens, D), F32), v((tokens, D), F32), v((tokens, 128), F32),
            v((tokens // ROW, HEADS // 2, 8, ROW), F32), v((16, D), F32), v((16, D), F32),
            pltpu.SemaphoreType.DMA((12,)),
        ]


def panel(ref, j):
    return ref.at[j * D : (j + 1) * D]


class NoNetwork:
    def __getattr__(self, name):
        return lambda *a: None


def layer_steps(m, net, bucket, length, tokens_in, out_grad_in, pool_grad, layer_out, pools, token_grad, keep_qkv, keep_norm, block=None):
    count = m.x.shape[0]
    tiles, rows_total = count // TM, count // ROW

    def copy(src, dst, k):
        return pltpu.make_async_copy(src, dst, m.lsem.at[k])

    queries, keys, values = (m.slope.at[j] for j in range(3))
    load_tokens = copy(tokens_in, m.x, 0)
    load_tokens.start()
    net.begin()
    m.vec_grad[...] = jnp.zeros_like(m.vec_grad)
    load_tokens.wait()
    net.need_attn()
    w_query, w_key, w_value, w_out = (panel(m.attn, j) for j in range(4))

    def qkv(i):
        rows = tile(i, TM)
        t = m.x[rows, :]
        q = (mm(t, w_query[...]) + m.vec[QB : QB + 1, :]).astype(BF16)
        queries[rows, :] = (q.astype(F32) * 0.125).astype(BF16)
        keys[rows, :] = mm(t, w_key[...]).astype(BF16)
        values[rows, :] = (mm(t, w_value[...]) + m.vec[VB : VB + 1, :]).astype(BF16)

    for i in range(tiles):
        qkv(i)
        net.during_qkv(i)
    for row in range(rows_total):
        starts, lens = row_blocks(bucket, length, row)
        mask = m.total.at[row * ROW : (row + 1) * ROW, :ROW]
        write_mask(mask, starts, lens)
        mask[...] = mask[...].T
        for part in range(2):
            net.during_attention(row * 2 + part)
            loop(3, lambda p: attend_pair_rows(queries, keys, values, m.ctx, m.logs, m.total, row, p + 3 * part, ROW), 3)
    stores = [copy(m.slope.at[j], keep_qkv.at[j], 1 + j) for j in range(3)]
    for s in stores:
        s.start()
    loop(tiles, lambda i: after_attention(m.x, m.ctx, w_out[...], m.vec, m.norm, m.scale, m.hidden, i, TM), 2)
    stores.append(copy(m.norm, keep_norm, 4))
    stores[-1].start()
    load_grad = copy(out_grad_in, m.x, 0)
    load_grad.start()
    net.need_up()
    for s in stores[:3]:
        s.wait()
    def feed(i):
        rows = tile(i, TM)
        for j in range(4):
            value, deriv = gelu_both(mm(m.hidden[rows, :], panel(m.up, j)[...]) + m.vec[UB + j : UB + j + 1, :])
            m.act[j, rows, :] = value.astype(BF16)
            m.slope[j, rows, :] = deriv.astype(BF16)

    for part in range(2):
        loop(tiles // 2, lambda i: feed(i + part * (tiles // 2)))
        net.during_up(part)
    stores[3].wait()
    net.need_down()

    def down(i):
        rows = tile(i, TM)
        second = m.hidden[rows, :].astype(F32) + m.vec[DB : DB + 1, :]
        for j in range(4):
            second = second + mm(m.act[j, rows, :], panel(m.down, j)[...])
        n, r = layer_norm_parts(second)
        m.norm[rows, :] = n
        m.scale[rows, 64:] = jnp.broadcast_to(r, (TM, 64))

    loop(tiles, down)
    load_grad.wait()
    out_low = m.spare.at[:count]
    for row in range(rows_total):
        starts, lens = row_blocks(bucket, length, row)
        pool_row(m.norm, m.vec, out_low, pools, pool_grad, m.x, m.total, starts, lens, row)
    store_out = copy(out_low, layer_out, 5)
    store_out.start()
    loop(tiles, lambda i: second_norm_back(m.total, m.norm, m.scale, m.vec, m.vec_grad, m.x, i, TM))
    load_norm = copy(keep_norm, m.norm, 6)
    load_norm.start()
    store_out.wait()
    net.gathered()
    group = D // 2

    def grad_down(i):
        for j in range(4):
            part = mm_tn(m.act[j, :, tile(i, group)], m.x[...]).astype(BF16)
            if block is None:
                m.spare[pl.ds(pl.multiple_of(i * group + j * D, group), group), :] = part
            else:
                for b in range(group // block):
                    chip = (i * group + j * D) // (4 * block) + b // 4
                    at = ((b % 4) * (D // block) + chip) * block
                    m.spare[pl.ds(pl.multiple_of(at, block), block), :] = part[b * block : (b + 1) * block]

    loop(D // group, grad_down)
    net.ready_down()
    def back(i):
        rows = tile(i, TM)
        for j in range(4):
            g = (mm_nt(m.x[rows, :], panel(m.down, j)[...]) * m.slope[j, rows, :].astype(F32)).astype(BF16)
            m.slope[j, rows, :] = g
            add_row(m.vec_grad, UB + j, g.astype(F32))

    for part in range(2):
        loop(tiles // 2, lambda i: back(i + part * (tiles // 2)))
        net.during_back(part)
    for j in range(4):
        def grad_up(i, j=j):
            at = pl.ds(pl.multiple_of(i * TM + j * D, TM), TM)
            m.down[at, :] = mm_tn(m.hidden[:, tile(i, TM)], m.slope[j]).astype(BF16)
        loop(D // TM, grad_up, D // TM)
        net.during_up_grad(j)
    load_norm.wait()

    def first_back(i):
        rows = tile(i, TM)
        g = m.total[rows, :]
        for j in range(4):
            g = g + mm_nt(m.slope[j, rows, :], panel(m.up, j)[...])
        n = m.norm[rows, :]
        add_row(m.vec_grad, G1, g * n)
        add_row(m.vec_grad, S1, g)
        back = layer_norm_back(g, n, m.scale[rows, :1], m.vec[G1 : G1 + 1, :])
        m.total[rows, :] = back
        low = back.astype(BF16)
        m.x[rows, :] = low
        add_row(m.vec_grad, OB, low.astype(F32))

    loop(tiles, first_back)
    net.after_first_back()
    loads = [copy(keep_qkv.at[j], m.slope.at[j], 7 + j) for j in range(3)]
    loads.append(copy(tokens_in, m.hidden, 10))
    for s in loads:
        s.start()
    grad_context = m.act.at[3]

    def context_back(i):
        grad_context[tile(i, TM), :] = mm_nt(m.x[tile(i, TM), :], w_out[...]).astype(BF16)

    loop(tiles, context_back)

    def grad_out(i):
        m.up[tile(i, TM), :] = mm_tn(m.ctx[:, tile(i, TM)], m.x[...]).astype(BF16)

    loop(D // TM, grad_out)
    net.after_out()
    for s in loads:
        s.wait()
    grads = [m.act.at[j] for j in range(3)]
    for row in range(rows_total):
        starts, lens = row_blocks(bucket, length, row)
        write_mask(m.norm.at[row * ROW : (row + 1) * ROW, :ROW], starts, lens)
    wide = D // 3
    for k in range(3):
        for part in range(2):
            net.after_chunk(k, part)
            loop(rows_total, lambda row: attend_pair_back(
                queries, keys, values, m.ctx, m.logs, m.norm, grad_context, *grads, row, 2 * k + part, 256), rows_total)
        cols = slice(k * wide, (k + 1) * wide)

        def grad_qkv(i):
            at = pl.ds(pl.multiple_of(i * TM + (k + 1) * D, TM), TM)
            for j in range(3):
                m.up[at, j * wide : (j + 1) * wide] = mm_tn(m.hidden[:, tile(i, TM)], m.act[j, :, cols]).astype(BF16)

        loop(D // TM, grad_qkv, D // TM)
        net.after_chunk(k, 2)
        for place, j in ((QB, 0), (VB, 2)):
            m.vec_grad[place : place + 1, cols] = jnp.sum(m.act[j, :, cols].astype(F32), axis=0, keepdims=True)
    net.ready_vec()
    for i in range(tiles):
        rows = slice(i * TM, (i + 1) * TM)
        g = m.total[rows, :]
        for j, w in enumerate((w_query, w_key, w_value)):
            g = g + mm_nt(m.act[j, rows, :], w[...])
        m.total[rows, :] = g
        net.during_finish(i)
    store_grad = copy(m.total, token_grad, 11)
    store_grad.start()
    net.end()
    store_grad.wait()


def local_kernel(bucket, length, tokens_in, out_grad_in, pool_grad, vec, w_attn, w_up, w_down,
                 layer_out, pools, token_grad, g_attn, g_up, g_down, g_vec, keep_qkv, keep_norm, *scratch):
    m = Memory(scratch)

    class Local(NoNetwork):
        def begin(self):
            m.vec[...] = vec[...]
            for src, dst in ((w_attn, m.attn), (w_up, m.up), (w_down, m.down)):
                c = pltpu.make_async_copy(src, dst, m.lsem.at[1])
                c.start()
                c.wait()

    layer_steps(m, Local(), bucket, length, tokens_in, out_grad_in, pool_grad, layer_out, pools, token_grad, keep_qkv, keep_norm)
    for src, dst in ((m.up, g_attn), (m.down, g_up), (m.spare, g_down)):
        c = pltpu.make_async_copy(src, dst, m.lsem.at[1])
        c.start()
        c.wait()
    g_vec[...] = m.vec_grad[...]


def layer_local(bucket, length, tokens, out_grad, pool_grad, vec, w_attn, w_up, w_down):
    count = tokens.shape[0]
    v, any_spec, smem = pl.BlockSpec(memory_space=pltpu.VMEM), pl.BlockSpec(memory_space=pl.ANY), pl.BlockSpec(memory_space=pltpu.SMEM)
    s = jax.ShapeDtypeStruct
    return pl.pallas_call(
        local_kernel,
        out_shape=[s((count, D), BF16), s(pool_grad.shape, F32), s((count, D), F32), s((4 * D, D), BF16), s((4 * D, D), BF16),
                   s((4 * D, D), BF16), s((16, D), F32), s((3, count, D), BF16), s((count, D), F32)],
        in_specs=[smem, smem, any_spec, any_spec, v, v, any_spec, any_spec, any_spec],
        out_specs=[any_spec, v, any_spec, any_spec, any_spec, any_spec, v, any_spec, any_spec],
        scratch_shapes=Memory.shapes(count),
        compiler_params=pltpu.CompilerParams(vmem_limit_bytes=63 * 2**20),
    )(bucket, length, tokens, out_grad, pool_grad, vec, w_attn, w_up, w_down)[:7]
def flip(x, d):
    bit = 1
    while bit <= d:
        if d & bit:
            x = x + bit - 2 * bit * lax.rem(x // bit, 2)
        bit *= 2
    return x


def near_first(n):
    return sorted(range(1, n), key=lambda d: (d == n // 2, d % 2 == 0, d))


class Place:
    def __init__(self, grid):
        self.grid = grid
        self.sizes = {"z": grid.nz, "hi": grid.side, "lo": grid.side}
        assert all(n & (n - 1) == 0 for n in self.sizes.values())

        self.on = {(name, d): flip(getattr(grid, name), d) for name, n in self.sizes.items() for d in range(n)}
        self.chips = {}
        for dz in range(grid.nz):
            for dh in range(grid.side):
                for dl in range(grid.side):
                    self.chips[dz, dh, dl] = grid.chip(self.on["z", dz], self.on["hi", dh], self.on["lo", dl])
        self.to = {key: self.device({key[0]: key[1]}) for key in self.on}
        self.sibling = grid.sib()

    def device(self, offsets):
        z, hi, lo = (self.on[name, offsets.get(name, 0)] for name in ("z", "hi", "lo"))
        return self.grid.dev(z, hi, lo, self.grid.core)

    def chip(self, offsets):
        return self.chips[tuple(offsets.get(name, 0) for name in ("z", "hi", "lo"))]

    def peer(self, name, d):
        return self.to[name, d]


class Spread:
    def __init__(self, place, sender, route, at, sem, unit, other):
        self.place, self.sender, self.route, self.at, self.sem = place, sender, route, at, sem
        self.unit, self.other = unit, other

    def send(self, offsets, device):
        p = self.place.chip(offsets)
        self.sender.start(self.at(self.unit, p), self.at(self.unit, p), self.sem(self.unit, p), device)

    def pass_on(self, offsets, axes):
        for name in axes:
            for d in near_first(self.place.sizes[name]):
                self.send(offsets, self.place.peer(name, d))

    def arrived(self, offsets):
        p = self.place.chip(offsets)
        self.sender.arrived(self.at(self.unit, p), self.sem(self.unit, p), self.place.grid)

    def to_sibling(self, offsets):
        self.send(offsets, self.place.sibling)

    def own(self, axes=None, sibling=True):
        self.pass_on({}, self.route if axes is None else axes)
        if sibling:
            self.to_sibling({})

    def first(self, d, axes=None, sibling=True):
        offsets = {self.route[0]: d}
        self.arrived(offsets)
        self.pass_on(offsets, self.route[1:])
        self.to_sibling(offsets)

    def second(self, a, d):
        offsets = {self.route[0]: a, self.route[1]: d}
        self.arrived(offsets)
        self.pass_on(offsets, self.route[2:])
        self.to_sibling(offsets)

    def third(self, a, b, d):
        offsets = {self.route[0]: a, self.route[1]: b, self.route[2]: d}
        self.arrived(offsets)
        self.to_sibling(offsets)

    def firsts(self):
        return [functools.partial(self.first, d) for d in near_first(self.place.sizes[self.route[0]])]

    def seconds(self):
        a_all = [0] + near_first(self.place.sizes[self.route[0]])
        return [functools.partial(self.second, a, d) for a in a_all for d in near_first(self.place.sizes[self.route[1]])]

    def thirds(self):
        a_all, b_all = ([0] + near_first(self.place.sizes[name]) for name in self.route[:2])
        return [functools.partial(self.third, a, b, d) for a in a_all for b in b_all for d in near_first(self.place.sizes[self.route[2]])]

    def from_sibling(self):
        offsets = [[0] + near_first(self.place.sizes[name]) for name in self.route]
        for a in offsets[0]:
            for b in offsets[1]:
                for c in offsets[2]:
                    p = self.place.chip({self.route[0]: a, self.route[1]: b, self.route[2]: c})
                    self.sender.arrived(self.at(self.other, p), self.sem(self.other, p), self.place.grid)

    @staticmethod
    def sends(grid):
        return 2 * grid.chips - 1


def mix(*lists):
    return [step for group in zip(*lists) for step in group]


class Stage:
    def __init__(self, place, sender, turn_over, z_early, source, held, second, third, last, sems):
        self.place, self.sender, self.source, self.z_early = place, sender, source, z_early
        self.held, self.from_second, self.from_third, self.from_z = held, second, third, last
        self.sem_sib, self.sem_second, self.sem_third, self.sem_z = sems
        g = place.grid
        self.grid = g
        self.which = lax.rem(g.core + turn_over, 2)
        s = g.side
        here = {n: [self.swap(place.on["hi", d], place.on["lo", d])[n] for d in range(s)] for n in range(2)}
        self.a_at, self.b_at = here[0], here[1]
        self.a, self.b = self.a_at[0], self.b_at[0]
        self.peers_a = [self.peer(self.a_at[k], self.b) for k in range(s)]
        self.peers_b = [self.peer(self.a, self.b_at[k]) for k in range(s)]
        self.blocks_a = [[self.block(self.a_at[k], b) for b in range(s)] for k in range(s)]
        self.blocks_b = [self.block(self.a, self.b_at[k]) for k in range(s)]

    def swap(self, x, y):
        return x * (1 - self.which) + y * self.which, y * (1 - self.which) + x * self.which

    def z(self, d):
        return self.place.on["z", d]

    def block(self, a, b):
        r, s = self.grid.rows, self.grid.side
        hi, lo = self.swap(a, b)
        index = hi * s + lo
        return pl.ds(pl.multiple_of(index * r, r), r)

    def peer(self, a, b):
        hi, lo = self.swap(a, b)
        return self.grid.dev(self.grid.z, hi, lo, self.grid.core)

    def to_sibling(self):
        for d in self.z_order():
            z = self.z(d)
            self.sender.start(self.source(1 - self.grid.core, z), self.held.at[z], self.sem_sib.at[z], self.place.sibling)

    def z_order(self):
        return near_first(self.grid.nz)[::-1] + [0]

    def add_sibling(self, d):
        s, r, z = self.grid.side, self.grid.rows, self.z(d)
        held, own = self.held.at[z], self.source(self.grid.core, z)
        self.sender.arrived(held, self.sem_sib.at[z], self.grid)

        def add(i):
            at = pl.ds(pl.multiple_of(i * r, r), r)
            held[at, :] = (held[at, :].astype(F32) + own[at, :].astype(F32)).astype(BF16)

        loop(s * s, add)
        for k in range(1, s):
            for b in range(s):
                self.sender.start(held.at[self.blocks_a[k][b]], self.from_second.at[k - 1, z, b * r : (b + 1) * r],
                                  self.sem_second.at[k - 1, z, b], self.peers_a[k])

    def add_second(self, d):
        s, r, z = self.grid.side, self.grid.rows, self.z(d)
        for k in range(s - 1):
            for b in range(s):
                self.sender.arrived(self.from_second.at[k, z, b * r : (b + 1) * r], self.sem_second.at[k, z, b], self.grid)
        for b in range(s):
            at = self.held.at[z, self.blocks_a[0][b]]
            total = at[...].astype(F32)
            for k in range(s - 1):
                total = total + self.from_second[k, z, b * r : (b + 1) * r].astype(F32)
            at[...] = total.astype(BF16)
        if self.z_early:
            if d:
                for k in range(s):
                    landing, sem = self.z_slot(d, k)
                    self.sender.start(self.held.at[z, self.blocks_b[k]], landing, sem, self.place.peer("z", d))
            return
        for k in range(1, s):
            self.sender.start(self.held.at[z, self.blocks_b[k]], self.from_third.at[k - 1, z],
                              self.sem_third.at[k - 1, z], self.peers_b[k])

    def z_slot(self, d, k):
        if k == 0:
            return self.from_z.at[d - 1], self.sem_z.at[d - 1]
        return self.from_third.at[k - 1, d], self.sem_third.at[k - 1, d]

    def z_total(self, k):
        total = self.held[self.grid.z, self.blocks_b[k]].astype(F32)
        for d in range(1, self.grid.nz):
            landing, sem = self.z_slot(d, k)
            self.sender.arrived(landing, sem, self.grid)
            total = total + landing[...].astype(F32)
        return total

    def own(self, z):
        s = self.grid.side
        for k in range(s - 1):
            self.sender.arrived(self.from_third.at[k, z], self.sem_third.at[k, z], self.grid)
        total = self.held[z, self.blocks_b[0]].astype(F32)
        for k in range(s - 1):
            total = total + self.from_third[k, z].astype(F32)
        return total

    def add_third(self, d):
        z = self.z(d)
        at = self.held.at[z, self.blocks_b[0]]
        at[...] = self.own(z).astype(BF16)
        self.sender.start(at, self.from_z.at[d - 1], self.sem_z.at[d - 1], self.place.peer("z", d))

    def result(self):
        if self.z_early:
            total = self.z_total(0)
            for k in range(1, self.grid.side):
                self.sender.arrived(self.from_third.at[k - 1, 0], self.sem_third.at[k - 1, 0], self.grid)
                total = total + self.from_third[k - 1, 0].astype(F32)
            return total
        total = self.own(self.grid.z)
        for k in range(self.grid.nz - 1):
            self.sender.arrived(self.from_z.at[k], self.sem_z.at[k], self.grid)
            total = total + self.from_z[k].astype(F32)
        return total

    def add_siblings(self):
        for d in self.z_order():
            self.add_sibling(d)

    def add_seconds(self):
        for d in self.z_order():
            self.add_second(d)

    def add_thirds(self):
        if self.z_early:
            for k in range(1, self.grid.side):
                at = self.held.at[self.grid.z, self.blocks_b[k]]
                at[...] = self.z_total(k).astype(BF16)
                self.sender.start(at, self.from_third.at[k - 1, 0], self.sem_third.at[k - 1, 0], self.peers_b[k])
            return
        for d in self.z_order()[:-1]:
            self.add_third(d)

    @staticmethod
    def sends(grid):
        n, s = grid.nz, grid.side
        return n + n * (s - 1) * s + n * (s - 1) + n - 1

    @staticmethod
    def scratch(grid, stages, width):
        n, s, r = grid.nz, grid.side, grid.rows
        return [
            pltpu.VMEM((stages, n, s * s * r, width), BF16),
            pltpu.VMEM((stages, s - 1, n, s * r, width), BF16),
            pltpu.VMEM((stages, s - 1, n, r, width), BF16),
            pltpu.VMEM((stages, n - 1, r, width), BF16),
            pltpu.SemaphoreType.DMA((stages, n)),
            pltpu.SemaphoreType.DMA((stages, s - 1, n, s)),
            pltpu.SemaphoreType.DMA((stages, s - 1, n)),
            pltpu.SemaphoreType.DMA((stages, n - 1)),
        ]


class SumAll:
    def __init__(self, place, sender, held, landing, sem):
        g = place.grid
        self.grid, self.sender, self.held, self.landing, self.sem = g, sender, held, landing, sem
        self.peers = [[g.sib()]] + [[place.peer(name, d) for d in range(1, place.sizes[name])] for name in ("lo", "hi", "z")]
        self.slots = [sum(len(p) for p in self.peers[:n]) for n in range(4)]

    def send(self, n):
        for k, peer in enumerate(self.peers[n]):
            slot = self.slots[n] + k
            self.sender.start(self.held.at[n], self.landing.at[slot], self.sem.at[slot], peer)

    def add(self, n):
        total = self.held[n]
        for k in range(len(self.peers[n])):
            slot = self.slots[n] + k
            self.sender.arrived(self.landing.at[slot], self.sem.at[slot], self.grid)
            total = total + self.landing[slot]
        self.held[n + 1] = total


def lane_places(grid, width):
    rank = grid.chip(grid.z, grid.hi, grid.lo) * 2 + grid.core
    first = lax.rem(rank * width, D)
    entry = lax.broadcasted_iota(jnp.int32, (128, D), 0)
    lane = lax.broadcasted_iota(jnp.int32, (128, D), 1)
    return jnp.where((lane == first + entry) & (entry < width), 1.0, 0.0).astype(BF16), rank * width // D


SHARES = (6, 6, 6, 6, 12, 14, 14, 14, 14, 8)


class Network:
    FFN, ATTN = 4, 4

    def __init__(self, grid, m, raws, outs, scratch):
        self.grid, self.m, self.raws, self.outs = grid, m, raws, outs
        (self.pre_out, self.pre_in, self.vec_out, self.vec_in, rsem, vsem, self.psem, ssem) = scratch[:8]
        ffn, attn = scratch[8:16], scratch[16:24]
        (self.swap_out, self.swap_in, self.wsem, self.swap_up_out, self.swap_up_in, self.wsem_up, sums, sums_in, sums_sem) = scratch[24:]
        self.sender = Sender(ssem)
        self.place = place = Place(grid)
        r, chips, c = grid.rows, grid.chips, grid.core

        def rows(ref, index):
            return ref.at[pl.ds(pl.multiple_of(index * r, r), r)]

        def spread(g, ref, jj, route, by_chip):
            def at(j, p):
                return rows(ref, p * 4 + j) if by_chip else rows(ref, j * chips + p)
            return Spread(place, self.sender, route, at, lambda j, p: rsem.at[g, j, p], c * 2 + jj, (1 - c) * 2 + jj)

        even, odd = ("z", "lo", "hi"), ("z", "hi", "lo")
        self.attn = [spread(0, m.attn, 0, even, False), spread(0, m.attn, 1, odd, False)]
        self.up = [spread(1, m.up, 0, even, False), spread(1, m.up, 1, odd, False)]
        self.down = [spread(2, m.down, 0, ("lo", "z", "hi"), True), spread(2, m.down, 1, ("hi", "z", "lo"), True)]
        self.vec = Spread(place, self.sender, even, self.vec_at, lambda j, p: vsem.at[j, p], c, 1 - c)

        z_rows = grid.side * grid.side * r

        def ffn_source(ref, quarter):
            def source(core, z):
                at = (quarter(core) * grid.nz + z) * z_rows
                return ref.at[pl.ds(pl.multiple_of(at, z_rows), z_rows)]
            return source

        def attn_source(t):
            def source(core, z):
                at = (t * grid.nz + z) * z_rows
                return m.up.at[pl.ds(pl.multiple_of(at, z_rows), z_rows), pl.ds(pl.multiple_of(core * (D // 2), D // 2), D // 2)]
            return source

        def stage(source, refs, slot, t, z_early=False):
            return Stage(place, self.sender, t, z_early, source, *(x.at[slot] for x in refs[:4]), tuple(x.at[slot] for x in refs[4:]))

        self.r_down = [stage(ffn_source(m.spare, lambda core, t=t: 2 * core + t), ffn, t, t, True) for t in range(2)]
        self.r_up = [stage(ffn_source(m.down, lambda core, t=t: 2 * t + core), ffn, 2 + t, t) for t in range(2)]
        self.r_attn = [stage(attn_source(t), attn, t, t) for t in range(4)]
        self.sums, self.sum_all = sums, SumAll(place, self.sender, sums, sums_in, sums_sem)


    def vec_at(self, j, p):
        base = self.m.x.shape[0]
        half_width = D // 2
        return self.m.spare.at[pl.ds(pl.multiple_of(base + p * 16, 16), 16), pl.ds(pl.multiple_of(j * half_width, half_width), half_width)]

    def mine(self, first, second):
        return jnp.where(self.grid.core == 0, first.astype(F32), second.astype(F32))

    def begin(self):
        grid, c = self.grid, self.grid.core
        greeting = pltpu.get_barrier_semaphore()
        peers = grid.peers()
        for peer in peers:
            pl.semaphore_signal(greeting, inc=1, device_id=peer, device_id_type=MESH)
        query, key, value, out, up, down, small = self.raws
        pairs = [[(query[...], value[...]), (key[...], out[...])],
                 [(up[:, j * D : (j + 1) * D], up[:, (2 + j) * D : (3 + j) * D]) for j in range(2)]]
        for g in range(2):
            for jj in range(2):
                first, second = pairs[g][jj]
                self.pre_out[g, jj] = self.mine(second, first).astype(BF16)
        matrix, _ = lane_places(grid, grid.dev_rows)
        matrix_up, row_up = lane_places(grid, 4 * grid.dev_rows)
        here = mm(small[...], matrix)
        up_row = mm(small[...], matrix_up)[8:9]
        sub = lax.broadcasted_iota(jnp.int32, (16, D), 0)
        placed = jnp.where(sub < 8, here, jnp.where(sub == UB + row_up, jnp.broadcast_to(up_row, (16, D)), 0.0))
        width = D // 2
        self.vec_out[...] = self.mine(placed[:, width:], placed[:, :width]).astype(BF16)
        pl.semaphore_wait(greeting, len(peers))
        for jj in range(2):
            self.sender.start(self.pre_out.at[0, jj], self.pre_in.at[0, jj], self.psem.at[0, jj], grid.sib())
        self.sender.start(self.vec_out, self.vec_in, self.psem.at[2, 0], grid.sib())
        for jj in range(2):
            self.sender.start(self.pre_out.at[1, jj], self.pre_in.at[1, jj], self.psem.at[1, jj], grid.sib())
        chip = self.place.chip({})
        for g, units in enumerate((self.attn, self.up)):
            for jj, unit in enumerate(units):
                self.sender.arrived(self.pre_in.at[g, jj], self.psem.at[g, jj], grid)
                own, other = self.mine(*pairs[g][jj]), self.pre_in[g, jj].astype(F32)
                both = jnp.concatenate([self.mine(own, other), self.mine(other, own)], axis=0)
                unit.at(unit.unit, chip)[...] = both.astype(BF16)
                if g == 0:
                    unit.own(("z",), sibling=False)
            if g == 0:
                self.sender.arrived(self.vec_in, self.psem.at[2, 0], grid)
                total = self.mine(placed[:, :width], placed[:, width:]) + self.vec_in[...].astype(F32)
                self.vec.at(self.vec.unit, chip)[...] = total.astype(BF16)
                self.vec.own()
                for unit in units:
                    unit.own(("lo", "hi"))
        for jj, unit in enumerate(self.down):
            r = grid.rows
            unit.at(unit.unit, chip)[...] = down[jj * r : (jj + 1) * r, :]
            unit.own(unit.route[:1])
        for unit in self.up:
            unit.own(("lo", "hi"))

    def run(self, steps):
        for step in steps:
            step()

    def need_attn(self):
        a, up = self.attn, self.up
        firsts = mix(a[0].firsts(), a[1].firsts(), self.vec.firsts())
        self.run(firsts[:6])
        for unit in up:
            unit.own(("z",), sibling=False)
        self.run(firsts[6:])
        self.run(mix(a[0].seconds(), a[1].seconds(), self.vec.seconds()))
        self.run(mix(a[0].thirds(), a[1].thirds(), self.vec.thirds()))
        for unit in a + [self.vec]:
            unit.from_sibling()
        base = self.m.x.shape[0]
        total = self.m.spare[base : base + 16, :].astype(F32)
        for p in range(1, self.grid.chips):
            total = total + self.m.spare[base + p * 16 : base + (p + 1) * 16, :].astype(F32)
        self.m.vec[...] = total
        up_firsts, down_firsts = mix(up[0].firsts(), up[1].firsts()), mix(self.down[0].firsts(), self.down[1].firsts())
        up_seconds, up_thirds = mix(up[0].seconds(), up[1].seconds()), mix(up[0].thirds(), up[1].thirds())
        down_seconds, down_thirds = mix(self.down[0].seconds(), self.down[1].seconds()), mix(self.down[0].thirds(), self.down[1].thirds())

        def own_down_z():
            for unit in self.down:
                unit.own(("z",), sibling=False)

        def own_down_last():
            for unit in self.down:
                unit.own(unit.route[2:], sibling=False)

        self.run(up_firsts)
        own_down_z()
        self.run(down_firsts)
        own_down_last()
        self.plan = up_seconds + up_thirds[: len(up_thirds) // 2] + down_seconds + up_thirds[len(up_thirds) // 2 :] + down_thirds
        total = len(self.plan)
        self.shares = [total * k // 100 for k in SHARES]

    def next(self):
        if self.shares:
            for _ in range(self.shares.pop(0)):
                if self.plan:
                    self.plan.pop(0)()

    def during_qkv(self, i):
        self.next()

    def during_attention(self, k):
        self.next()

    def need_up(self):
        while any(step.func.__self__ in self.up for step in self.plan):
            self.plan.pop(0)()
        for unit in self.up:
            unit.from_sibling()

    def during_up(self, j):
        self.next()

    def need_down(self):
        while self.plan:
            self.plan.pop(0)()
        for unit in self.down:
            unit.from_sibling()

    def gathered(self):
        self.sender.finish()
        self.sender.started = Started(len(self.sender.started))


    def ready_down(self):
        for stage in self.r_down:
            stage.to_sibling()

    def during_back(self, j):
        if j < 2:
            self.r_down[j].add_siblings()

    def during_up_grad(self, j):
        if j % 2 == 1:
            self.r_up[j // 2].to_sibling()
        if j == 2:
            self.r_down[0].add_seconds()
        if j == 3:
            self.r_up[0].add_siblings()

    def after_first_back(self):
        self.r_up[1].add_siblings()
        self.r_down[1].add_seconds()

    def after_out(self):
        self.r_attn[0].to_sibling()
        self.r_up[0].add_seconds()

    def after_chunk(self, k, middle):
        attn, up, down = self.r_attn, self.r_up, self.r_down
        if middle == 1:
            attn[k].add_siblings()
        if middle == 2:
            attn[1 + k].to_sibling()
        if (k, middle) == (0, 1):
            down[0].add_thirds()
        if (k, middle) == (1, 0):
            up[1].add_seconds()
            up[0].add_thirds()
        if (k, middle) == (1, 1):
            down[1].add_thirds()
            attn[0].add_seconds()
        if (k, middle) == (2, 0):
            up[1].add_thirds()
        if (k, middle) == (2, 1):
            attn[1].add_seconds()
            attn[0].add_thirds()

    def ready_vec(self):
        self.sums[0] = self.m.vec_grad[...]
        self.sum_all.send(0)

    def during_finish(self, i):
        attn = self.r_attn
        if i == 0:
            self.sum_all.add(0)
            self.sum_all.send(1)
        if i == 1:
            attn[3].add_siblings()
            attn[2].add_seconds()
        if i == 2:
            attn[1].add_thirds()
            self.down_result()
        if i == 3:
            self.sum_all.add(1)
            self.sum_all.send(2)

    def end(self):
        attn = self.r_attn
        attn[3].add_seconds()
        attn[2].add_thirds()
        self.up_result()
        self.sum_all.add(2)
        self.sum_all.send(3)
        self.attn_result(0)
        attn[3].add_thirds()
        self.attn_result(1)
        self.sum_all.add(3)
        self.small_result()
        self.attn_result(2)
        self.attn_result(3)
        self.finish_results()
        self.sender.finish()

    def down_result(self):
        r, down = self.grid.rows, self.outs[5]
        for t in range(2):
            down[t * r : (t + 1) * r, :] = self.r_down[t].result()

    def trade(self, total, out, landing, sem):
        c, dr = self.grid.core, self.grid.dev_rows
        top, bottom = total[:dr], total[dr:]
        out[...] = jnp.where(c == 0, bottom, top)
        self.sender.start(out, landing, sem, self.grid.sib())
        return jnp.where(c == 0, top, bottom)

    def by_core(self, put, own, landing=None):
        for core in range(2):
            @pl.when(self.grid.core == core)
            def _(core=core):
                put(core, own)

    def put_up(self, t):
        def put(core, value):
            at = (2 * t + core) * D
            self.outs[4][:, at : at + D] = value
        return put

    def put_attn(self, t):
        query, key, value, out = self.outs[:4]

        def put(core, v):
            if t == 0:
                out[:, core * (D // 2) : (core + 1) * (D // 2)] = v
                return
            at, wide = (t - 1) * (D // 3), D // 3
            if core == 0:
                query[:, at : at + wide] = v[:, :wide]
                key[:, at : at + wide // 2] = v[:, wide:]
            else:
                key[:, at + wide // 2 : at + wide] = v[:, : wide // 2]
                value[:, at : at + wide] = v[:, wide // 2 :]
        return put

    def up_result(self):
        for t in range(2):
            mine = self.trade(self.r_up[t].result(), self.swap_up_out.at[t], self.swap_up_in.at[t], self.wsem_up.at[t])
            self.by_core(self.put_up(t), mine)

    def attn_result(self, t):
        mine = self.trade(self.r_attn[t].result(), self.swap_out.at[t], self.swap_in.at[t], self.wsem.at[t])
        self.by_core(self.put_attn(t), mine)

    def finish_results(self):
        for n, put, landing, sems in ((2, self.put_up, self.swap_up_in, self.wsem_up), (4, self.put_attn, self.swap_in, self.wsem)):
            for t in range(n):
                self.sender.arrived(landing.at[t], sems.at[t], self.grid)
                for core in range(2):
                    @pl.when(self.grid.core == 1 - core)
                    def _(core=core):
                        put(t)(core, landing[t])

    def small_result(self):
        x = self.sums[4]
        high = x.astype(BF16)
        rest = x - high.astype(F32)
        middle = rest.astype(BF16)
        low = (rest - middle.astype(F32)).astype(BF16)
        matrix, _ = lane_places(self.grid, self.grid.dev_rows)
        matrix_up, row_up = lane_places(self.grid, 4 * self.grid.dev_rows)
        narrow, wide = (mm_nt(high, k) + mm_nt(middle, k) + mm_nt(low, k) for k in (matrix, matrix_up))
        sub = lax.broadcasted_iota(jnp.int32, (16, 128), 0)
        up = jnp.sum(jnp.where(sub == UB + row_up, wide, 0.0), axis=0, keepdims=True)
        self.outs[6][...] = jnp.where(sub < 8, narrow, jnp.broadcast_to(up, (16, 128)))

    @staticmethod
    def sends(grid):
        return 5 + 7 * Spread.sends(grid) + 8 * Stage.sends(grid) + 6 + peer_count(grid)

    @staticmethod
    def scratch(grid):
        chips, dr = grid.chips, grid.dev_rows
        dma = pltpu.SemaphoreType.DMA
        return [
            pltpu.VMEM((2, 2, dr, D), BF16),
            pltpu.VMEM((2, 2, dr, D), BF16),
            pltpu.VMEM((16, D // 2), BF16),
            pltpu.VMEM((16, D // 2), BF16),
            dma((3, 4, chips)),
            dma((2, chips)),
            dma((3, 2)),
            dma((Network.sends(grid),)),
        ] + Stage.scratch(grid, 4, D) + Stage.scratch(grid, 4, D // 2) + [
            pltpu.VMEM((4, dr, D // 2), F32),
            pltpu.VMEM((4, dr, D // 2), F32),
            dma((4,)),
            pltpu.VMEM((2, dr, D), F32),
            pltpu.VMEM((2, dr, D), F32),
            dma((2,)),
            pltpu.VMEM((5, 16, D), F32),
            pltpu.VMEM((peer_count(grid), 16, D), F32),
            dma((peer_count(grid),)),
        ]


class Started(list):
    def __init__(self, offset):
        super().__init__()
        self.offset = offset

    def __len__(self):
        return self.offset + super().__len__()


def fused_kernel(grid, memory, bucket, length, tokens_in, out_grad_in, pool_grad, *refs):
    raws, (layer_out, pools, token_grad), outs, (keep_qkv, keep_norm), scratch = refs[:7], refs[7:10], refs[10:17], refs[17:19], refs[19:]
    grid.place()
    m = Memory(scratch[:memory])
    net = Network(grid, m, raws, outs, scratch[memory:])
    layer_steps(m, net, bucket, length, tokens_in, out_grad_in, pool_grad, layer_out, pools, token_grad, keep_qkv, keep_norm, grid.rows)


def layer_fused(grid, bucket, length, tokens, out_grad, pool_grad, query, key, value, out, up, down, small):
    count, dr = tokens.shape[0], grid.dev_rows
    v, any_spec, smem = pl.BlockSpec(memory_space=pltpu.VMEM), pl.BlockSpec(memory_space=pl.ANY), pl.BlockSpec(memory_space=pltpu.SMEM)
    s = jax.ShapeDtypeStruct
    memory = Memory.shapes(count)
    return pl.pallas_call(
        functools.partial(fused_kernel, grid, len(memory)),
        out_shape=[s((count, D), BF16), s(pool_grad.shape, F32), s((count, D), F32)] + [s((dr, D), F32)] * 4
        + [s((dr, 4 * D), F32), s((4 * dr, D), F32), s((16, 128), F32), s((3, count, D), BF16), s((count, D), F32)],
        in_specs=[smem, smem, any_spec, any_spec] + [v] * 8,
        out_specs=[any_spec, v, any_spec] + [v] * 7 + [any_spec, any_spec],
        scratch_shapes=memory + Network.scratch(grid),
        compiler_params=pltpu.CompilerParams(collective_id=2, has_side_effects=True, vmem_limit_bytes=255 * 2**18),
    )(bucket, length, tokens, out_grad, pool_grad, query, key, value, out, up, down, small)[:10]
def hand_out_kernel(parts, *refs):
    count = len(parts)
    srcs, small, dsts, vectors = refs[:count], refs[count], refs[count + 1 : 2 * count + 1], refs[2 * count + 1 : 2 * count + 10]
    held, sem_in, sem_out = refs[2 * count + 10 : -2], refs[-2], refs[-1]
    loads, stores = [], []
    for src, dst, kept, n in zip(srcs, dsts, held, parts):
        rows = src.shape[0] // n
        for k in range(n):
            at = slice(k * rows, (k + 1) * rows)
            loads.append(pltpu.make_async_copy(src.at[at], kept.at[at], sem_in.at[len(loads)]))
            stores.append(pltpu.make_async_copy(kept.at[at], dst.at[at], sem_out.at[len(stores)]))
    for c in loads:
        c.start()
    for k, out in enumerate(vectors):
        out[...] = small[k, : out.shape[0]]
    for load, store in zip(loads, stores):
        load.wait()
        store.start()
    for c in stores:
        c.wait()


def hand_out(grid, results):
    arrays, small = results[:9], results[9]
    parts = [4 if x.shape[0] % 64 == 0 and x.shape[1] == D else 1 for x in arrays]
    dr = grid.dev_rows
    v, any_spec = pl.BlockSpec(memory_space=pltpu.VMEM), pl.BlockSpec(memory_space=pl.ANY)
    lengths = [dr] * 8 + [4 * dr]
    out = pl.pallas_call(
        functools.partial(hand_out_kernel, parts),
        out_shape=[jax.ShapeDtypeStruct(x.shape, x.dtype) for x in arrays] + [jax.ShapeDtypeStruct((k,), F32) for k in lengths],
        in_specs=[any_spec] * 9 + [v],
        out_specs=[any_spec] * 9 + [v] * 9,
        scratch_shapes=[pltpu.VMEM(x.shape, x.dtype) for x in arrays] + [pltpu.SemaphoreType.DMA((sum(parts),))] * 2,
        compiler_params=pltpu.CompilerParams(vmem_limit_bytes=60 * 2**20),
    )(*arrays, small)
    layer_out, pools, token_grad, g_query, g_key, g_value, g_out, g_up, g_down = out[:9]
    vec = out[9:]
    return (
        layer_out, pools, token_grad, g_query, vec[QB], g_key, g_value, vec[VB], g_out, vec[OB], vec[G1], vec[S1],
        g_up, vec[UB], g_down, vec[DB], vec[G2], vec[S2],
    )


def body(
    grid,
    tokens,
    block_bucket,
    lengths,
    query_weight,
    query_bias,
    key_weight,
    value_weight,
    value_bias,
    out_weight,
    out_bias,
    first_gain,
    first_shift,
    up_weight,
    up_bias,
    down_weight,
    down_bias,
    second_gain,
    second_shift,
    out_grad,
    pool_grad,
):
    rank = lax.axis_index("dp") * lax.axis_size("fsdp") + lax.axis_index("fsdp")
    dr, n, s, pad, r = grid.dev_rows, grid.nz, grid.side, grid.pad, grid.rows
    if pad == r:
        vectors = (query_bias, value_bias, out_bias, first_gain, first_shift, down_bias, second_gain, second_shift)
        small = jnp.concatenate([
            jnp.pad(jnp.stack(vectors), ((0, 0), (0, 128 - dr))),
            jnp.pad(up_bias[None], ((0, 7), (0, 128 - 4 * dr)))])
        results = layer_fused(
            grid, block_bucket, lengths, tokens, out_grad, pool_grad, query_weight, key_weight, value_weight, out_weight,
            up_weight, down_weight, small)
        return hand_out(grid, results)
    raw_attn = jnp.stack([query_weight, key_weight, value_weight, out_weight])
    raw_up = up_weight.reshape(dr, 4, D).transpose(1, 0, 2)
    raw_down = down_weight.reshape(4, dr, D)
    small = jnp.stack([query_bias, value_bias, out_bias, first_gain, first_shift, down_bias, second_gain, second_shift])
    small = lax.dynamic_update_slice(jnp.zeros((16, D), BF16), small, (0, rank * dr))
    wide = lax.dynamic_update_slice(jnp.zeros((16 * D,), BF16), up_bias, (rank * 4 * dr,)).reshape(16, D)
    raw_vec = jnp.stack([small, wide])
    w_attn, w_up, w_down, w_vec = gather_all(grid, raw_attn, raw_up, raw_down, raw_vec)
    w_attn, w_up, w_down = (w[:, :, :r].reshape(4 * D, D) for w in (w_attn, w_up, w_down))
    vec = jnp.sum(w_vec.astype(F32), axis=1)
    vec = jnp.concatenate([vec[0, :8], vec[1, :8]])
    layer_out, pools, token_grad, g_attn, g_up, g_down, g_vec = layer_local(
        block_bucket, lengths, tokens, out_grad, pool_grad, vec, w_attn, w_up, w_down)
    panels = g_attn[D:].reshape(3, D, 3, D // 3).transpose(2, 1, 0, 3).reshape(3 * D, D)
    g_attn = jnp.concatenate([panels, g_attn[:D]])

    def blocks(grad):
        return jnp.pad(grad.reshape(-1, r, D), ((0, 0), (0, pad - r), (0, 0)))

    g_attn, g_up = (blocks(g).reshape(4, n, s, s, pad, D) for g in (g_attn, g_up))
    g_down = blocks(g_down).reshape(n, s, s, 4, pad, D)
    o_attn, o_up, o_down, o_vec = reduce_all(grid, g_attn, g_up, g_down, g_vec)
    small = lax.dynamic_slice(o_vec, (0, rank * dr), (8, dr))
    wide = lax.dynamic_slice(o_vec[8:12].reshape(4 * D), (rank * 4 * dr,), (4 * dr,))
    return (
        layer_out,
        pools,
        token_grad,
        o_attn[0],
        small[QB],
        o_attn[1],
        o_attn[2],
        small[VB],
        o_attn[3],
        small[OB],
        small[G1],
        small[S1],
        o_up.transpose(1, 0, 2).reshape(dr, 4 * D),
        wide,
        o_down.reshape(4 * dr, D),
        small[DB],
        small[G2],
        small[S2],
    )


def solution(mesh):
    whole, line = P(("dp", "fsdp"), None), P(("dp", "fsdp"))
    grid = Grid(mesh.shape["dp"], mesh.shape["fsdp"])
    return jax.shard_map(
        functools.partial(body, grid),
        mesh=mesh,
        in_specs=(
            whole, line, line, whole, line, whole, whole, line, whole, line,
            line, line, whole, line, whole, line, line, line, whole, whole,
        ),
        out_specs=(
            whole, whole, whole, whole, line, whole, whole, line, whole, line,
            line, line, whole, line, whole, line, line, line,
        ),
        check_vma=False,
    )
```

```python
import functools
import math

import jax
import jax.numpy as jnp
from jax import lax
from jax.experimental import pallas as pl
from jax.experimental.pallas import tpu as pltpu
from jax.sharding import PartitionSpec as P

MESH = pl.DeviceIdType.MESH
D = 768
F32 = jnp.float32
BF16 = jnp.bfloat16


class Grid:
    def __init__(self, nz, nf):
        self.nz = nz
        self.side = math.isqrt(nf // 2)
        assert 2 * self.side * self.side == nf
        self.chips = nz * self.side * self.side
        self.rows = D // self.chips
        self.dev_rows = self.rows // 2
        self.pad = -(-self.rows // 16) * 16

    def place(self):
        s = self.side
        self.z = lax.axis_index("dp")
        f = lax.axis_index("fsdp")
        self.core = lax.rem(f, 2)
        self.lo = lax.rem(f // 2, s)
        self.hi = f // (2 * s)
        self.beside = self.sib()

    def dev(self, z, hi, lo, core):
        return (z, (hi * self.side + lo) * 2 + core)

    def sib(self):
        return self.dev(self.z, self.hi, self.lo, 1 - self.core)

    def zs(self, d):
        return lax.rem(self.z + d, self.nz)

    def los(self, d):
        return lax.rem(self.lo + d, self.side)

    def his(self, d):
        return lax.rem(self.hi + d, self.side)

    def z_peer(self, d):
        return self.dev(self.zs(d), self.hi, self.lo, self.core)

    def lo_peer(self, d):
        return self.dev(self.z, self.hi, self.los(d), self.core)

    def hi_peer(self, d):
        return self.dev(self.z, self.his(d), self.lo, self.core)

    def chip(self, z, hi, lo):
        return (z * self.side + hi) * self.side + lo

    def peers(self):
        out = [self.sib()]
        out += [self.z_peer(d) for d in range(1, self.nz)]
        out += [self.lo_peer(d) for d in range(1, self.side)]
        out += [self.hi_peer(d) for d in range(1, self.side)]
        return out

    def barrier(self):
        sem = pltpu.get_barrier_semaphore()
        peers = self.peers()
        for peer in peers:
            pl.semaphore_signal(sem, inc=1, device_id=peer, device_id_type=MESH)
        pl.semaphore_wait(sem, len(peers))


class Sender:
    def __init__(self, sems):
        self.sems = sems
        self.started = []

    def start(self, src, dst, recv_sem, device):
        copy = pltpu.make_async_remote_copy(
            src_ref=src,
            dst_ref=dst,
            send_sem=self.sems.at[len(self.started)],
            recv_sem=recv_sem,
            device_id=device,
            device_id_type=MESH,
        )
        copy.start()
        self.started.append(copy)
        return copy

    def arrived(self, dst, recv_sem, grid):
        pltpu.make_async_remote_copy(
            src_ref=dst,
            dst_ref=dst,
            send_sem=self.sems.at[0],
            recv_sem=recv_sem,
            device_id=grid.beside,
            device_id_type=MESH,
        ).wait_recv()

    def finish(self):
        for copy in self.started:
            copy.wait_send()


class Gather:
    def __init__(self, grid, sender, at, sem, per_core=2):
        self.grid, self.sender, self.at, self.sem = grid, sender, at, sem
        self.per_core = per_core

    def mine(self, jj):
        return self.grid.core * self.per_core + jj

    def send(self, j, p, device):
        self.sender.start(self.at(j, p), self.at(j, p), self.sem(j, p), device)

    def wait(self, j, p):
        self.sender.arrived(self.at(j, p), self.sem(j, p), self.grid)

    def own(self):
        g = self.grid
        for jj in range(self.per_core):
            j, p = self.mine(jj), g.chip(g.z, g.hi, g.lo)
            for d in range(1, g.nz):
                self.send(j, p, g.z_peer(d))
            self.spread(j, p)

    def spread(self, j, p):
        g = self.grid
        for d in range(1, g.side):
            self.send(j, p, g.lo_peer(d))
        for d in range(1, g.side):
            self.send(j, p, g.hi_peer(d))
        self.send(j, p, g.sib())

    def along_z(self, d):
        g = self.grid
        for jj in range(self.per_core):
            j, p = self.mine(jj), g.chip(g.zs(d), g.hi, g.lo)
            self.wait(j, p)
            self.spread(j, p)

    def second(self, d):
        g = self.grid
        for jj in range(self.per_core):
            j = self.mine(jj)
            for e in range(1, g.side):
                if jj % 2 == 0:
                    p = g.chip(g.zs(d), g.hi, g.los(e))
                else:
                    p = g.chip(g.zs(d), g.his(e), g.lo)
                self.wait(j, p)
                for k in range(1, g.side):
                    self.send(j, p, g.hi_peer(k) if jj % 2 == 0 else g.lo_peer(k))
                self.send(j, p, g.sib())

    def third(self, d):
        g = self.grid
        for jj in range(self.per_core):
            j = self.mine(jj)
            for e in range(1, g.side):
                for k in range(g.side):
                    if jj % 2 == 0:
                        p = g.chip(g.zs(d), g.his(e), g.los(k))
                    else:
                        p = g.chip(g.zs(d), g.his(k), g.los(e))
                    self.wait(j, p)
                    self.send(j, p, g.sib())

    def sibling(self):
        g = self.grid
        for jj in range(self.per_core):
            j = (1 - g.core) * self.per_core + jj
            for d in range(g.nz):
                for e in range(g.side):
                    for k in range(g.side):
                        self.wait(j, g.chip(g.zs(d), g.his(e), g.los(k)))

    @staticmethod
    def sends(grid, per_core):
        n, s = grid.nz, grid.side
        return per_core * (n - 1 + n * (s - 1) + n * s * (s - 1) + grid.chips)


def join_rows(grid, low, high):
    parts = [low.astype(F32), high.astype(F32)]
    if grid.pad != grid.rows:
        parts.append(jnp.zeros((grid.pad - grid.rows, low.shape[1]), F32))
    return jnp.concatenate(parts, axis=0).astype(BF16)


def gather_kernel(grid, attn_ref, up_ref, down_ref, vec_ref, w_attn, w_up, w_down, w_vec,
                  pre_ref, pre_vec, stage, stage_vec, rsem, vsem, ssem, psem, lsem):
    grid.place()
    grid.barrier()
    sender = Sender(ssem)
    c = grid.core
    me = grid.chip(grid.z, grid.hi, grid.lo)
    raws = (attn_ref, up_ref)
    for g, raw in enumerate(raws):
        for jj in range(2):
            sender.start(raw.at[(1 - c) * 2 + jj], pre_ref.at[g, jj], psem.at[g, jj], grid.sib())
    sender.start(vec_ref.at[1 - c], pre_vec, psem.at[2, 0], grid.sib())

    groups = [
        Gather(grid, sender, lambda j, p: w_attn.at[j, p], lambda j, p: rsem.at[0, j, p]),
        Gather(grid, sender, lambda j, p: w_up.at[j, p], lambda j, p: rsem.at[1, j, p]),
        Gather(grid, sender, lambda j, p: w_down.at[p, j], lambda j, p: rsem.at[2, j, p]),
    ]
    vec = Gather(grid, sender, lambda j, p: w_vec.at[j, p], lambda j, p: vsem.at[j, p], per_core=1)

    def put(src, dst, k):
        copy = pltpu.make_async_copy(src, dst, lsem.at[k])
        copy.start()
        copy.wait()

    def assemble(g):
        for jj in range(2):
            if g < 2:
                sender.arrived(pre_ref.at[g, jj], psem.at[g, jj], grid)
                own, other = raws[g][c * 2 + jj], pre_ref[g, jj]
                first = jnp.where(c == 0, own.astype(F32), other.astype(F32))
                last = jnp.where(c == 0, other.astype(F32), own.astype(F32))
            else:
                first, last = down_ref[2 * jj], down_ref[2 * jj + 1]
            stage[jj] = join_rows(grid, first, last)
            put(stage.at[jj], groups[g].at(c * 2 + jj, me), 0)

    assemble(0)
    groups[0].own()
    sender.arrived(pre_vec, psem.at[2, 0], grid)
    stage_vec[...] = (vec_ref[c].astype(F32) + pre_vec[...].astype(F32)).astype(BF16)
    put(stage_vec, w_vec.at[c, me], 0)
    vec.own()
    def z_steps(g):
        for d in range(grid.nz - 1, 0, -1):
            g.along_z(d)

    def second_steps(g):
        for d in range(grid.nz, 0, -1):
            g.second(d)

    def third_steps(g):
        for d in range(grid.nz, 0, -1):
            g.third(d)

    z_steps(vec)
    z_steps(groups[0])
    assemble(1)
    groups[1].own()
    second_steps(vec)
    second_steps(groups[0])
    z_steps(groups[1])
    assemble(2)
    groups[2].own()
    third_steps(vec)
    third_steps(groups[0])
    second_steps(groups[1])
    z_steps(groups[2])
    third_steps(groups[1])
    second_steps(groups[2])
    third_steps(groups[2])
    for g in [vec] + groups:
        g.sibling()
    sender.finish()


def gather_all(grid, raw_attn, raw_up, raw_down, raw_vec):
    n, pad, dr = grid.chips, grid.pad, grid.dev_rows
    nsend = 5 + 3 * Gather.sends(grid, 2) + Gather.sends(grid, 1)
    any_spec = pl.BlockSpec(memory_space=pl.ANY)
    vmem = pl.BlockSpec(memory_space=pltpu.VMEM)
    return pl.pallas_call(
        functools.partial(gather_kernel, grid),
        out_shape=[
            jax.ShapeDtypeStruct((4, n, pad, D), BF16),
            jax.ShapeDtypeStruct((4, n, pad, D), BF16),
            jax.ShapeDtypeStruct((n, 4, pad, D), BF16),
            jax.ShapeDtypeStruct((2, n, 16, D), BF16),
        ],
        in_specs=[vmem] * 4,
        out_specs=[any_spec] * 4,
        scratch_shapes=[
            pltpu.VMEM((2, 2, dr, D), BF16),
            pltpu.VMEM((16, D), BF16),
            pltpu.VMEM((2, pad, D), BF16),
            pltpu.VMEM((16, D), BF16),
            pltpu.SemaphoreType.DMA((3, 4, n)),
            pltpu.SemaphoreType.DMA((2, n)),
            pltpu.SemaphoreType.DMA((nsend,)),
            pltpu.SemaphoreType.DMA((3, 2)),
            pltpu.SemaphoreType.DMA((1,)),
        ],
        compiler_params=pltpu.CompilerParams(collective_id=0, has_side_effects=True, vmem_limit_bytes=32 * 2**20),
    )(raw_attn, raw_up, raw_down, raw_vec)
class Reduce:
    def __init__(self, grid, sender, part, held, second, third, last, sems):
        self.grid, self.sender, self.part = grid, sender, part
        self.held, self.from_second, self.from_third, self.from_z = held, second, third, last
        self.sem_sib, self.sem_second, self.sem_third, self.sem_z = sems

    def to_sibling(self, d):
        g = self.grid
        z = g.zs(d)
        for jj in range(2):
            j = (1 - g.core) * 2 + jj
            self.sender.start(self.part(j, z), self.held.at[jj, z], self.sem_sib.at[jj, z], g.sib())

    def add_sibling(self, d):
        g, s = self.grid, self.grid.side
        z = g.zs(d)
        for jj in range(2):
            held = self.held.at[jj, z]
            self.sender.arrived(held, self.sem_sib.at[jj, z], g)
            own = self.part(g.core * 2 + jj, z)
            for h in range(s):
                def add(l, carry, h=h):
                    held[h, l] = (held[h, l].astype(F32) + own[h, l].astype(F32)).astype(BF16)
                    return carry
                lax.fori_loop(0, s, add, 0)
            for k in range(1, s):
                if jj % 2 == 0:
                    src, peer = held.at[g.his(k)], g.hi_peer(k)
                else:
                    src, peer = held.at[:, g.los(k)], g.lo_peer(k)
                self.sender.start(src, self.from_second.at[jj, s - k - 1, z], self.sem_second.at[jj, s - k - 1, z], peer)

    def add_second(self, d):
        g, s = self.grid, self.grid.side
        z = g.zs(d)
        for jj in range(2):
            for k in range(s - 1):
                self.sender.arrived(self.from_second.at[jj, k, z], self.sem_second.at[jj, k, z], g)
            for e in range(s):
                at = self.held.at[jj, z, g.hi, e] if jj % 2 == 0 else self.held.at[jj, z, e, g.lo]
                total = at[...].astype(F32)
                for k in range(s - 1):
                    total = total + self.from_second[jj, k, z, e].astype(F32)
                at[...] = total.astype(BF16)
            for k in range(1, s):
                if jj % 2 == 0:
                    src, peer = self.held.at[jj, z, g.hi, g.los(k)], g.lo_peer(k)
                else:
                    src, peer = self.held.at[jj, z, g.his(k), g.lo], g.hi_peer(k)
                self.sender.start(src, self.from_third.at[jj, s - k - 1, z], self.sem_third.at[jj, s - k - 1, z], peer)

    def own(self, jj, z):
        g, s = self.grid, self.grid.side
        for k in range(s - 1):
            self.sender.arrived(self.from_third.at[jj, k, z], self.sem_third.at[jj, k, z], g)
        total = self.held[jj, z, g.hi, g.lo].astype(F32)
        for k in range(s - 1):
            total = total + self.from_third[jj, k, z].astype(F32)
        return total

    def add_third(self, d):
        g = self.grid
        z = g.zs(d)
        for jj in range(2):
            at = self.held.at[jj, z, g.hi, g.lo]
            at[...] = self.own(jj, z).astype(BF16)
            self.sender.start(at, self.from_z.at[jj, g.nz - d - 1], self.sem_z.at[jj, g.nz - d - 1], g.z_peer(d))

    def result(self, jj):
        g = self.grid
        total = self.own(jj, g.z)
        for k in range(g.nz - 1):
            self.sender.arrived(self.from_z.at[jj, k], self.sem_z.at[jj, k], g)
            total = total + self.from_z[jj, k].astype(F32)
        return total

    @staticmethod
    def sends(grid):
        n, s = grid.nz, grid.side
        return 2 * (n + n * (s - 1) * 2 + n - 1)

    @staticmethod
    def scratch(grid, groups):
        n, s, pad = grid.nz, grid.side, grid.pad
        return [
            pltpu.VMEM((groups, 2, n, s, s, pad, D), BF16),
            pltpu.VMEM((groups, 2, s - 1, n, s, pad, D), BF16),
            pltpu.VMEM((groups, 2, s - 1, n, pad, D), BF16),
            pltpu.VMEM((groups, 2, n - 1, pad, D), BF16),
            pltpu.SemaphoreType.DMA((groups, 2, n)),
            pltpu.SemaphoreType.DMA((groups, 2, s - 1, n)),
            pltpu.SemaphoreType.DMA((groups, 2, s - 1, n)),
            pltpu.SemaphoreType.DMA((groups, 2, n - 1)),
        ]


def sum_everywhere(grid, sender, own, landing, sem):
    steps = [[grid.sib()],
             [grid.lo_peer(d) for d in range(1, grid.side)],
             [grid.hi_peer(d) for d in range(1, grid.side)],
             [grid.z_peer(d) for d in range(1, grid.nz)]]
    slot = 0
    for n, peers in enumerate(steps):
        for k, peer in enumerate(peers):
            sender.start(own.at[n], landing.at[slot + len(peers) - 1 - k], sem.at[slot + len(peers) - 1 - k], peer)
        total = own[n]
        for k in range(len(peers)):
            sender.arrived(landing.at[slot + k], sem.at[slot + k], grid)
            total = total + landing[slot + k]
        slot += len(peers)
        own[n + 1] = total


def peer_count(grid):
    return 1 + 2 * (grid.side - 1) + grid.nz - 1


def reduce_kernel(grid, g_attn, g_up, g_down, g_vec, o_attn, o_up, o_down, o_vec,
                  held, second, third, last, s1, s2, s3, s4, swap_out, swap_in, wsem, vec, vec_in, vsem, ssem):
    grid.place()
    grid.barrier()
    sender = Sender(ssem)
    c = grid.core
    parts = [lambda j, z: g_attn.at[j, z], lambda j, z: g_up.at[j, z], lambda j, z: g_down.at[z, :, :, j]]
    groups = [
        Reduce(grid, sender, parts[g], held.at[g], second.at[g], third.at[g], last.at[g],
               (s1.at[g], s2.at[g], s3.at[g], s4.at[g]))
        for g in range(3)
    ]
    order = [groups[2], groups[1], groups[0]]
    n = grid.nz
    for g in order:
        for d in range(n, 0, -1):
            g.to_sibling(d)
    vec[0] = g_vec[...]
    for g in order:
        for d in range(n, 0, -1):
            g.add_sibling(d)
    for g in order:
        for d in range(n, 0, -1):
            g.add_second(d)
    for g in order:
        for d in range(n - 1, 0, -1):
            g.add_third(d)
    sum_everywhere(grid, sender, vec, vec_in, vsem)
    o_vec[...] = vec[4]
    r, dr = grid.rows, grid.dev_rows
    for i, (g, out) in enumerate(((groups[1], o_up), (groups[0], o_attn))):
        for jj in range(2):
            total = g.result(jj)
            top, bottom = total[:dr], total[dr:r]
            out[c * 2 + jj] = jnp.where(c == 0, top, bottom)
            swap_out[i, jj] = jnp.where(c == 0, bottom, top)
            sender.start(swap_out.at[i, jj], swap_in.at[i, jj], wsem.at[i, jj], grid.sib())
    for jj in range(2):
        o_down[jj] = groups[2].result(jj)[:r]
    for i, out in enumerate((o_up, o_attn)):
        for jj in range(2):
            sender.arrived(swap_in.at[i, jj], wsem.at[i, jj], grid)
            out[(1 - c) * 2 + jj] = swap_in[i, jj]
    sender.finish()


def reduce_all(grid, g_attn, g_up, g_down, g_vec):
    n, s, pad, dr = grid.nz, grid.side, grid.pad, grid.dev_rows
    nsend = 3 * Reduce.sends(grid) + 4 + peer_count(grid)
    vmem = pl.BlockSpec(memory_space=pltpu.VMEM)
    return pl.pallas_call(
        functools.partial(reduce_kernel, grid),
        out_shape=[
            jax.ShapeDtypeStruct((4, dr, D), F32),
            jax.ShapeDtypeStruct((4, dr, D), F32),
            jax.ShapeDtypeStruct((2, grid.rows, D), F32),
            jax.ShapeDtypeStruct((16, D), F32),
        ],
        in_specs=[vmem] * 4,
        out_specs=[vmem] * 4,
        scratch_shapes=Reduce.scratch(grid, 3) + [
            pltpu.VMEM((2, 2, dr, D), F32),
            pltpu.VMEM((2, 2, dr, D), F32),
            pltpu.SemaphoreType.DMA((2, 2)),
            pltpu.VMEM((5, 16, D), F32),
            pltpu.VMEM((peer_count(grid), 16, D), F32),
            pltpu.SemaphoreType.DMA((peer_count(grid),)),
            pltpu.SemaphoreType.DMA((nsend,)),
        ],
        compiler_params=pltpu.CompilerParams(collective_id=1, has_side_effects=True, vmem_limit_bytes=56 * 2**20),
    )(g_attn, g_up, g_down, g_vec)
HEADS = 12
HD = 64
ROW = 512
BLOCK = 64
PER_ROW = ROW // BLOCK
NEG = -1e30
TM = 256


def mm(a, b):
    return jnp.dot(a, b, preferred_element_type=F32)


def mm_nt(a, b):
    return lax.dot_general(a, b, (((1,), (1,)), ((), ())), preferred_element_type=F32)


def mm_tn(a, b):
    return lax.dot_general(a, b, (((0,), (0,)), ((), ())), preferred_element_type=F32)


def tile(i, size):
    if isinstance(i, int):
        return pl.ds(i * size, size)
    return pl.ds(pl.multiple_of(i * size, size), size)


def loop(n, f, unroll=1):
    def step(i, carry):
        for k in range(unroll):
            f(i * unroll + k)
        return carry
    lax.fori_loop(0, n // unroll, step, 0)


def row_blocks(bucket_ref, length_ref, row):
    starts, lens = [], []
    for b in range(PER_ROW):
        stride = bucket_ref[row * PER_ROW + b] // BLOCK
        first = b // stride * stride
        starts.append(first)
        lens.append(length_ref[row * PER_ROW + first])
    return starts, lens


def pick(ids, values):
    out = jnp.zeros_like(ids)
    for b, value in enumerate(values):
        out = jnp.where(ids == b, value, out)
    return out


def write_mask(mask_ref, starts, lens):
    query = pick(lax.broadcasted_iota(jnp.int32, (BLOCK, ROW), 1) // BLOCK, starts)
    place = lax.broadcasted_iota(jnp.int32, (BLOCK, ROW), 0)
    for b in range(PER_ROW):
        limit = lens[b] - (b - starts[b]) * BLOCK
        allowed = (query == starts[b]) & (place < limit)
        mask_ref[b * BLOCK : (b + 1) * BLOCK, :] = jnp.where(allowed, 0.0, NEG)


def member_matrix(starts, lens):
    lane = lax.broadcasted_iota(jnp.int32, (PER_ROW, ROW), 1)
    token_start = pick(lane // BLOCK, starts)
    token_len = pick(lane // BLOCK, lens)
    valid = lane - token_start * BLOCK < token_len
    block = lax.broadcasted_iota(jnp.int32, (PER_ROW, ROW), 0)
    member = jnp.where((token_start == pick(block, starts)) & valid, 1.0, 0.0).astype(F32)
    lens_col = pick(lax.broadcasted_iota(jnp.int32, (PER_ROW, 1), 0), lens)
    return member, 1.0 / lens_col.astype(F32)


def layer_norm_parts(v):
    center = v - jnp.mean(v, axis=-1, keepdims=True)
    spread = jnp.mean(center * center, axis=-1, keepdims=True)
    scale = lax.rsqrt(spread + 1e-05)
    return center * scale, scale


def layer_norm_back(grad, normed, scale, gain):
    g = grad * gain
    return scale * (g - jnp.mean(g, axis=-1, keepdims=True) - normed * jnp.mean(g * normed, axis=-1, keepdims=True))


def gelu_both(x):
    t = 1.0 / (1.0 + 0.23164189 * jnp.abs(x))
    density = jnp.exp(x * x * -0.5 - 0.9189385332046727)
    poly = ((((1.330274429 * t - 1.821255978) * t + 1.781477937) * t - 0.356563782) * t + 0.319381530) * t
    tail = poly * density
    phi = jnp.where(x < 0, tail, 1.0 - tail)
    return x * phi, phi + x * density


def half(shape, axis, h):
    return lax.broadcasted_iota(jnp.int32, shape, axis) // HD == h


def attend_pair_back(queries, keys, values, context, logs, mask, grad_context, grad_q, grad_k, grad_v, row, pair, chunk=256):
    rows, cols = tile(row, ROW), tile(pair, 2 * HD)
    key_slab, value_slab = keys[rows, cols], values[rows, cols]
    key_turned = key_slab.astype(F32).T.astype(BF16)
    lane = [half((ROW, 2 * HD), 1, h) for h in range(2)]
    only_k = [jnp.where(lane[h], key_slab.astype(F32), 0.0).astype(BF16) for h in range(2)]
    only_v = [jnp.where(lane[h], value_slab.astype(F32), 0.0).astype(BF16) for h in range(2)]
    sums = []
    for c in range(ROW // chunk):
        part = tile(row * (ROW // chunk) + c, chunk)
        query_slab, grad_slab = queries[part, cols], grad_context[part, cols]
        dot = (grad_slab.astype(F32) * context[part, cols].astype(F32)).T
        gq, gk, gv = [], [], []
        for h in range(2):
            delta = jnp.sum(dot[h * HD : (h + 1) * HD], axis=0, keepdims=True)
            s = mm_nt(only_k[h], query_slab) + mask[rows, c * chunk : (c + 1) * chunk]
            p = jnp.exp(s - logs[row, pair, h : h + 1, c * chunk : (c + 1) * chunk])
            gp = mm_nt(only_v[h], grad_slab)
            gs = (p * (gp - delta)).astype(BF16)
            gv.append(mm(p.astype(BF16), grad_slab))
            gk.append(mm(gs, query_slab))
            gq.append(mm(key_turned, gs))
        turned = jnp.where(half((2 * HD, chunk), 0, 0), gq[0], gq[1]) * 0.125
        grad_q[part, cols] = turned.T.astype(BF16)
        now = (jnp.where(lane[0], gk[0], gk[1]), jnp.where(lane[0], gv[0], gv[1]))
        sums = now if c == 0 else tuple(a + b for a, b in zip(sums, now))
    grad_k[rows, cols] = sums[0].astype(BF16)
    grad_v[rows, cols] = sums[1].astype(BF16)


def attend_pair_rows(queries, keys, values, context, logs, mask, row, pair, chunk=256):
    rows, cols = tile(row, ROW), tile(pair, 2 * HD)
    key_slab, value_slab = keys[rows, cols], values[rows, cols]
    for c in range(ROW // chunk):
        part = tile(row * (ROW // chunk) + c, chunk)
        query_slab = queries[part, cols]
        parts, cols_log = [], []
        lane = [half((chunk, 2 * HD), 1, h) for h in range(2)]
        for h in range(2):
            only = jnp.where(lane[h], query_slab.astype(F32), 0.0).astype(BF16)
            s = mm_nt(only, key_slab) + mask[part, :ROW]
            peak = jnp.max(s, axis=1, keepdims=True)
            e = jnp.exp(s - peak)
            total = jnp.sum(e, axis=1, keepdims=True)
            cols_log.append(peak + jnp.log(total))
            parts.append(mm(e.astype(BF16), value_slab) * (1.0 / total))
        context[part, cols] = jnp.where(lane[0], parts[0], parts[1]).astype(BF16)
        both = jnp.where(lane[0], cols_log[0], cols_log[1]).T
        for h in range(2):
            logs[row, pair, h : h + 1, c * chunk : (c + 1) * chunk] = both[h * HD : h * HD + 1]


QB, VB, OB, G1, S1, DB, G2, S2 = range(8)
UB = 8


def after_attention(tokens, context, w_out, vec, normed, scale, hidden, i, tm):
    rows = tile(i, tm)
    first = tokens[rows, :].astype(F32) + mm(context[rows, :], w_out) + vec[OB : OB + 1, :]
    n, r = layer_norm_parts(first)
    normed[rows, :] = n
    scale[rows, :64] = jnp.broadcast_to(r, (tm, 64))
    hidden[rows, :] = (n * vec[G1 : G1 + 1, :] + vec[S1 : S1 + 1, :]).astype(BF16)


WIDTHS = (D, 2 * D // 3, D // 3, D // 6, D // 12)


def split_low(x):
    high = x.astype(BF16)
    return high, (x - high.astype(F32)).astype(BF16)


def pool_row(normed, vec, layer_out, pools, pool_grad, out_grad, total, starts, lens, row):
    rows = pl.ds(row * ROW, ROW)
    member, inverse = member_matrix(starts, lens)
    member = member.astype(BF16)
    outputs = normed[rows, :] * vec[G2 : G2 + 1, :] + vec[S2 : S2 + 1, :]
    layer_out[rows, :] = outputs.astype(BF16)
    high, low = split_low(outputs)
    avg = (mm(member, high) + mm(member, low)) * inverse
    square = avg * avg
    blocks = pl.ds(row * PER_ROW, PER_ROW)
    grad = None
    at = 0
    for width in WIDTHS:
        r = lax.rsqrt(jnp.sum(square[:, :width], axis=-1, keepdims=True) / width + 1e-06)
        lead = avg[:, :width]
        pools[blocks, at : at + width] = lead * r
        g = pool_grad[blocks, at : at + width]
        back = g * r - lead * (r * r * r * (jnp.sum(g * lead, axis=-1, keepdims=True) / width))
        if width % 128:
            wide = -(-width // 128) * 128
            back = jnp.concatenate([back, jnp.zeros((PER_ROW, wide - width), F32)], axis=1)
        if grad is None:
            grad = back
        else:
            grad = jnp.concatenate([grad[:, : back.shape[1]] + back, grad[:, back.shape[1] :]], axis=1)
        at += width
    high, low = split_low(grad * inverse)
    both = jnp.concatenate([high, low], axis=0)
    total[rows, :] = out_grad[rows, :].astype(F32) + mm_tn(jnp.concatenate([member, member], axis=0), both)


def add_row(vec_grad, k, values):
    vec_grad[k : k + 1, :] += jnp.sum(values, axis=0, keepdims=True)


def second_norm_back(total, normed, scale, vec, vec_grad, branch, i, tm):
    rows = tile(i, tm)
    g, n = total[rows, :], normed[rows, :]
    add_row(vec_grad, G2, g * n)
    add_row(vec_grad, S2, g)
    back = layer_norm_back(g, n, scale[rows, 64:65], vec[G2 : G2 + 1, :])
    total[rows, :] = back
    low = back.astype(BF16)
    branch[rows, :] = low
    add_row(vec_grad, DB, low.astype(F32))


def turn(x, out, tm=256):
    for i in range(x.shape[0] // tm):
        for j in range(x.shape[1] // tm):
            out[j * tm : (j + 1) * tm, i * tm : (i + 1) * tm] = x[i * tm : (i + 1) * tm, j * tm : (j + 1) * tm].T
class Memory:
    NAMES = ("attn", "up", "down", "spare", "act", "slope", "x", "ctx", "hidden", "norm", "total",
             "scale", "logs", "vec", "vec_grad", "lsem")

    def __init__(self, refs):
        for name, ref in zip(self.NAMES, refs):
            setattr(self, name, ref)

    @staticmethod
    def shapes(tokens):
        v = pltpu.VMEM
        weights = [v((4 * D, D), BF16)] * 4
        return weights + [
            v((4, tokens, D), BF16), v((4, tokens, D), BF16),
            v((tokens, D), BF16), v((tokens, D), BF16), v((tokens, D), BF16),
            v((tokens, D), F32), v((tokens, D), F32), v((tokens, 128), F32),
            v((tokens // ROW, HEADS // 2, 8, ROW), F32), v((16, D), F32), v((16, D), F32),
            pltpu.SemaphoreType.DMA((12,)),
        ]


def panel(ref, j):
    return ref.at[j * D : (j + 1) * D]


class NoNetwork:
    def __getattr__(self, name):
        return lambda *a: None


def layer_steps(m, net, bucket, length, tokens_in, out_grad_in, pool_grad, layer_out, pools, token_grad, keep_qkv, keep_norm, block=None):
    count = m.x.shape[0]
    tiles, rows_total = count // TM, count // ROW

    def copy(src, dst, k):
        return pltpu.make_async_copy(src, dst, m.lsem.at[k])

    queries, keys, values = (m.slope.at[j] for j in range(3))
    load_tokens = copy(tokens_in, m.x, 0)
    load_tokens.start()
    net.begin()
    m.vec_grad[...] = jnp.zeros_like(m.vec_grad)
    load_tokens.wait()
    net.need_attn()
    w_query, w_key, w_value, w_out = (panel(m.attn, j) for j in range(4))

    def qkv(i):
        rows = tile(i, TM)
        t = m.x[rows, :]
        q = (mm(t, w_query[...]) + m.vec[QB : QB + 1, :]).astype(BF16)
        queries[rows, :] = (q.astype(F32) * 0.125).astype(BF16)
        keys[rows, :] = mm(t, w_key[...]).astype(BF16)
        values[rows, :] = (mm(t, w_value[...]) + m.vec[VB : VB + 1, :]).astype(BF16)

    for i in range(tiles):
        qkv(i)
        net.during_qkv(i)
    for row in range(rows_total):
        starts, lens = row_blocks(bucket, length, row)
        mask = m.total.at[row * ROW : (row + 1) * ROW, :ROW]
        write_mask(mask, starts, lens)
        mask[...] = mask[...].T
        for part in range(2):
            net.during_attention(row * 2 + part)
            loop(3, lambda p: attend_pair_rows(queries, keys, values, m.ctx, m.logs, m.total, row, p + 3 * part, ROW), 3)
    stores = [copy(m.slope.at[j], keep_qkv.at[j], 1 + j) for j in range(3)]
    for s in stores:
        s.start()
    loop(tiles, lambda i: after_attention(m.x, m.ctx, w_out[...], m.vec, m.norm, m.scale, m.hidden, i, TM), 2)
    stores.append(copy(m.norm, keep_norm, 4))
    stores[-1].start()
    load_grad = copy(out_grad_in, m.x, 0)
    load_grad.start()
    net.need_up()
    for s in stores[:3]:
        s.wait()
    def feed(i):
        rows = tile(i, TM)
        for j in range(4):
            value, deriv = gelu_both(mm(m.hidden[rows, :], panel(m.up, j)[...]) + m.vec[UB + j : UB + j + 1, :])
            m.act[j, rows, :] = value.astype(BF16)
            m.slope[j, rows, :] = deriv.astype(BF16)

    for part in range(2):
        loop(tiles // 2, lambda i: feed(i + part * (tiles // 2)))
        net.during_up(part)
    stores[3].wait()
    net.need_down()

    def down(i):
        rows = tile(i, TM)
        second = m.hidden[rows, :].astype(F32) + m.vec[DB : DB + 1, :]
        for j in range(4):
            second = second + mm(m.act[j, rows, :], panel(m.down, j)[...])
        n, r = layer_norm_parts(second)
        m.norm[rows, :] = n
        m.scale[rows, 64:] = jnp.broadcast_to(r, (TM, 64))

    loop(tiles, down)
    load_grad.wait()
    out_low = m.spare.at[:count]
    for row in range(rows_total):
        starts, lens = row_blocks(bucket, length, row)
        pool_row(m.norm, m.vec, out_low, pools, pool_grad, m.x, m.total, starts, lens, row)
    store_out = copy(out_low, layer_out, 5)
    store_out.start()
    loop(tiles, lambda i: second_norm_back(m.total, m.norm, m.scale, m.vec, m.vec_grad, m.x, i, TM))
    load_norm = copy(keep_norm, m.norm, 6)
    load_norm.start()
    store_out.wait()
    net.gathered()
    group = D // 2

    def grad_down(i):
        for j in range(4):
            part = mm_tn(m.act[j, :, tile(i, group)], m.x[...]).astype(BF16)
            if block is None:
                m.spare[pl.ds(pl.multiple_of(i * group + j * D, group), group), :] = part
            else:
                for b in range(group // block):
                    chip = (i * group + j * D) // (4 * block) + b // 4
                    at = ((b % 4) * (D // block) + chip) * block
                    m.spare[pl.ds(pl.multiple_of(at, block), block), :] = part[b * block : (b + 1) * block]

    loop(D // group, grad_down)
    net.ready_down()
    def back(i):
        rows = tile(i, TM)
        for j in range(4):
            g = (mm_nt(m.x[rows, :], panel(m.down, j)[...]) * m.slope[j, rows, :].astype(F32)).astype(BF16)
            m.slope[j, rows, :] = g
            add_row(m.vec_grad, UB + j, g.astype(F32))

    for part in range(2):
        loop(tiles // 2, lambda i: back(i + part * (tiles // 2)))
        net.during_back(part)
    for j in range(4):
        def grad_up(i, j=j):
            at = pl.ds(pl.multiple_of(i * TM + j * D, TM), TM)
            m.down[at, :] = mm_tn(m.hidden[:, tile(i, TM)], m.slope[j]).astype(BF16)
        loop(D // TM, grad_up, D // TM)
        net.during_up_grad(j)
    load_norm.wait()

    def first_back(i):
        rows = tile(i, TM)
        g = m.total[rows, :]
        for j in range(4):
            g = g + mm_nt(m.slope[j, rows, :], panel(m.up, j)[...])
        n = m.norm[rows, :]
        add_row(m.vec_grad, G1, g * n)
        add_row(m.vec_grad, S1, g)
        back = layer_norm_back(g, n, m.scale[rows, :1], m.vec[G1 : G1 + 1, :])
        m.total[rows, :] = back
        low = back.astype(BF16)
        m.x[rows, :] = low
        add_row(m.vec_grad, OB, low.astype(F32))

    loop(tiles, first_back)
    net.after_first_back()
    loads = [copy(keep_qkv.at[j], m.slope.at[j], 7 + j) for j in range(3)]
    loads.append(copy(tokens_in, m.hidden, 10))
    for s in loads:
        s.start()
    grad_context = m.act.at[3]

    def context_back(i):
        grad_context[tile(i, TM), :] = mm_nt(m.x[tile(i, TM), :], w_out[...]).astype(BF16)

    loop(tiles, context_back)

    def grad_out(i):
        m.up[tile(i, TM), :] = mm_tn(m.ctx[:, tile(i, TM)], m.x[...]).astype(BF16)

    loop(D // TM, grad_out)
    net.after_out()
    for s in loads:
        s.wait()
    grads = [m.act.at[j] for j in range(3)]
    for row in range(rows_total):
        starts, lens = row_blocks(bucket, length, row)
        write_mask(m.norm.at[row * ROW : (row + 1) * ROW, :ROW], starts, lens)
    wide = D // 3
    for k in range(3):
        for part in range(2):
            net.after_chunk(k, part)
            loop(rows_total, lambda row: attend_pair_back(
                queries, keys, values, m.ctx, m.logs, m.norm, grad_context, *grads, row, 2 * k + part, 256), rows_total)
        cols = slice(k * wide, (k + 1) * wide)

        def grad_qkv(i):
            at = pl.ds(pl.multiple_of(i * TM + (k + 1) * D, TM), TM)
            for j in range(3):
                m.up[at, j * wide : (j + 1) * wide] = mm_tn(m.hidden[:, tile(i, TM)], m.act[j, :, cols]).astype(BF16)

        loop(D // TM, grad_qkv, D // TM)
        net.after_chunk(k, 2)
        for place, j in ((QB, 0), (VB, 2)):
            m.vec_grad[place : place + 1, cols] = jnp.sum(m.act[j, :, cols].astype(F32), axis=0, keepdims=True)
    net.ready_vec()
    for i in range(tiles):
        rows = slice(i * TM, (i + 1) * TM)
        g = m.total[rows, :]
        for j, w in enumerate((w_query, w_key, w_value)):
            g = g + mm_nt(m.act[j, rows, :], w[...])
        m.total[rows, :] = g
        net.during_finish(i)
    store_grad = copy(m.total, token_grad, 11)
    store_grad.start()
    net.end()
    store_grad.wait()


def local_kernel(bucket, length, tokens_in, out_grad_in, pool_grad, vec, w_attn, w_up, w_down,
                 layer_out, pools, token_grad, g_attn, g_up, g_down, g_vec, keep_qkv, keep_norm, *scratch):
    m = Memory(scratch)

    class Local(NoNetwork):
        def begin(self):
            m.vec[...] = vec[...]
            for src, dst in ((w_attn, m.attn), (w_up, m.up), (w_down, m.down)):
                c = pltpu.make_async_copy(src, dst, m.lsem.at[1])
                c.start()
                c.wait()

    layer_steps(m, Local(), bucket, length, tokens_in, out_grad_in, pool_grad, layer_out, pools, token_grad, keep_qkv, keep_norm)
    for src, dst in ((m.up, g_attn), (m.down, g_up), (m.spare, g_down)):
        c = pltpu.make_async_copy(src, dst, m.lsem.at[1])
        c.start()
        c.wait()
    g_vec[...] = m.vec_grad[...]


def layer_local(bucket, length, tokens, out_grad, pool_grad, vec, w_attn, w_up, w_down):
    count = tokens.shape[0]
    v, any_spec, smem = pl.BlockSpec(memory_space=pltpu.VMEM), pl.BlockSpec(memory_space=pl.ANY), pl.BlockSpec(memory_space=pltpu.SMEM)
    s = jax.ShapeDtypeStruct
    return pl.pallas_call(
        local_kernel,
        out_shape=[s((count, D), BF16), s(pool_grad.shape, F32), s((count, D), F32), s((4 * D, D), BF16), s((4 * D, D), BF16),
                   s((4 * D, D), BF16), s((16, D), F32), s((3, count, D), BF16), s((count, D), F32)],
        in_specs=[smem, smem, any_spec, any_spec, v, v, any_spec, any_spec, any_spec],
        out_specs=[any_spec, v, any_spec, any_spec, any_spec, any_spec, v, any_spec, any_spec],
        scratch_shapes=Memory.shapes(count),
        compiler_params=pltpu.CompilerParams(vmem_limit_bytes=63 * 2**20),
    )(bucket, length, tokens, out_grad, pool_grad, vec, w_attn, w_up, w_down)[:7]
def flip(x, d):
    bit = 1
    while bit <= d:
        if d & bit:
            x = x + bit - 2 * bit * lax.rem(x // bit, 2)
        bit *= 2
    return x


def near_first(n):
    return sorted(range(1, n), key=lambda d: (d == n // 2, d % 2 == 0, d))


class Place:
    def __init__(self, grid):
        self.grid = grid
        self.sizes = {"z": grid.nz, "hi": grid.side, "lo": grid.side}
        assert all(n & (n - 1) == 0 for n in self.sizes.values())

        self.on = {(name, d): flip(getattr(grid, name), d) for name, n in self.sizes.items() for d in range(n)}
        self.chips = {}
        for dz in range(grid.nz):
            for dh in range(grid.side):
                for dl in range(grid.side):
                    self.chips[dz, dh, dl] = grid.chip(self.on["z", dz], self.on["hi", dh], self.on["lo", dl])
        self.to = {key: self.device({key[0]: key[1]}) for key in self.on}
        self.sibling = grid.sib()

    def device(self, offsets):
        z, hi, lo = (self.on[name, offsets.get(name, 0)] for name in ("z", "hi", "lo"))
        return self.grid.dev(z, hi, lo, self.grid.core)

    def chip(self, offsets):
        return self.chips[tuple(offsets.get(name, 0) for name in ("z", "hi", "lo"))]

    def peer(self, name, d):
        return self.to[name, d]


class Spread:
    def __init__(self, place, sender, route, at, sem, unit, other):
        self.place, self.sender, self.route, self.at, self.sem = place, sender, route, at, sem
        self.unit, self.other = unit, other

    def send(self, offsets, device):
        p = self.place.chip(offsets)
        self.sender.start(self.at(self.unit, p), self.at(self.unit, p), self.sem(self.unit, p), device)

    def pass_on(self, offsets, axes):
        for name in axes:
            for d in near_first(self.place.sizes[name]):
                self.send(offsets, self.place.peer(name, d))

    def arrived(self, offsets):
        p = self.place.chip(offsets)
        self.sender.arrived(self.at(self.unit, p), self.sem(self.unit, p), self.place.grid)

    def to_sibling(self, offsets):
        self.send(offsets, self.place.sibling)

    def own(self, axes=None, sibling=True):
        self.pass_on({}, self.route if axes is None else axes)
        if sibling:
            self.to_sibling({})

    def first(self, d, axes=None, sibling=True):
        offsets = {self.route[0]: d}
        self.arrived(offsets)
        self.pass_on(offsets, self.route[1:])
        self.to_sibling(offsets)

    def second(self, a, d):
        offsets = {self.route[0]: a, self.route[1]: d}
        self.arrived(offsets)
        self.pass_on(offsets, self.route[2:])
        self.to_sibling(offsets)

    def third(self, a, b, d):
        offsets = {self.route[0]: a, self.route[1]: b, self.route[2]: d}
        self.arrived(offsets)
        self.to_sibling(offsets)

    def firsts(self):
        return [functools.partial(self.first, d) for d in near_first(self.place.sizes[self.route[0]])]

    def seconds(self):
        a_all = [0] + near_first(self.place.sizes[self.route[0]])
        return [functools.partial(self.second, a, d) for a in a_all for d in near_first(self.place.sizes[self.route[1]])]

    def thirds(self):
        a_all, b_all = ([0] + near_first(self.place.sizes[name]) for name in self.route[:2])
        return [functools.partial(self.third, a, b, d) for a in a_all for b in b_all for d in near_first(self.place.sizes[self.route[2]])]

    def from_sibling(self):
        offsets = [[0] + near_first(self.place.sizes[name]) for name in self.route]
        for a in offsets[0]:
            for b in offsets[1]:
                for c in offsets[2]:
                    p = self.place.chip({self.route[0]: a, self.route[1]: b, self.route[2]: c})
                    self.sender.arrived(self.at(self.other, p), self.sem(self.other, p), self.place.grid)

    @staticmethod
    def sends(grid):
        return 2 * grid.chips - 1


def mix(*lists):
    return [step for group in zip(*lists) for step in group]


class Stage:
    def __init__(self, place, sender, turn_over, z_early, source, held, second, third, last, sems):
        self.place, self.sender, self.source, self.z_early = place, sender, source, z_early
        self.held, self.from_second, self.from_third, self.from_z = held, second, third, last
        self.sem_sib, self.sem_second, self.sem_third, self.sem_z = sems
        g = place.grid
        self.grid = g
        self.which = lax.rem(g.core + turn_over, 2)
        s = g.side
        here = {n: [self.swap(place.on["hi", d], place.on["lo", d])[n] for d in range(s)] for n in range(2)}
        self.a_at, self.b_at = here[0], here[1]
        self.a, self.b = self.a_at[0], self.b_at[0]
        self.peers_a = [self.peer(self.a_at[k], self.b) for k in range(s)]
        self.peers_b = [self.peer(self.a, self.b_at[k]) for k in range(s)]
        self.blocks_a = [[self.block(self.a_at[k], b) for b in range(s)] for k in range(s)]
        self.blocks_b = [self.block(self.a, self.b_at[k]) for k in range(s)]

    def swap(self, x, y):
        return x * (1 - self.which) + y * self.which, y * (1 - self.which) + x * self.which

    def z(self, d):
        return self.place.on["z", d]

    def block(self, a, b):
        r, s = self.grid.rows, self.grid.side
        hi, lo = self.swap(a, b)
        index = hi * s + lo
        return pl.ds(pl.multiple_of(index * r, r), r)

    def peer(self, a, b):
        hi, lo = self.swap(a, b)
        return self.grid.dev(self.grid.z, hi, lo, self.grid.core)

    def to_sibling(self):
        for d in self.z_order():
            z = self.z(d)
            self.sender.start(self.source(1 - self.grid.core, z), self.held.at[z], self.sem_sib.at[z], self.place.sibling)

    def z_order(self):
        return near_first(self.grid.nz)[::-1] + [0]

    def add_sibling(self, d):
        s, r, z = self.grid.side, self.grid.rows, self.z(d)
        held, own = self.held.at[z], self.source(self.grid.core, z)
        self.sender.arrived(held, self.sem_sib.at[z], self.grid)

        def add(i):
            at = pl.ds(pl.multiple_of(i * r, r), r)
            held[at, :] = (held[at, :].astype(F32) + own[at, :].astype(F32)).astype(BF16)

        loop(s * s, add)
        for k in range(1, s):
            for b in range(s):
                self.sender.start(held.at[self.blocks_a[k][b]], self.from_second.at[k - 1, z, b * r : (b + 1) * r],
                                  self.sem_second.at[k - 1, z, b], self.peers_a[k])

    def add_second(self, d):
        s, r, z = self.grid.side, self.grid.rows, self.z(d)
        for k in range(s - 1):
            for b in range(s):
                self.sender.arrived(self.from_second.at[k, z, b * r : (b + 1) * r], self.sem_second.at[k, z, b], self.grid)
        for b in range(s):
            at = self.held.at[z, self.blocks_a[0][b]]
            total = at[...].astype(F32)
            for k in range(s - 1):
                total = total + self.from_second[k, z, b * r : (b + 1) * r].astype(F32)
            at[...] = total.astype(BF16)
        if self.z_early:
            if d:
                for k in range(s):
                    landing, sem = self.z_slot(d, k)
                    self.sender.start(self.held.at[z, self.blocks_b[k]], landing, sem, self.place.peer("z", d))
            return
        for k in range(1, s):
            self.sender.start(self.held.at[z, self.blocks_b[k]], self.from_third.at[k - 1, z],
                              self.sem_third.at[k - 1, z], self.peers_b[k])

    def z_slot(self, d, k):
        if k == 0:
            return self.from_z.at[d - 1], self.sem_z.at[d - 1]
        return self.from_third.at[k - 1, d], self.sem_third.at[k - 1, d]

    def z_total(self, k):
        total = self.held[self.grid.z, self.blocks_b[k]].astype(F32)
        for d in range(1, self.grid.nz):
            landing, sem = self.z_slot(d, k)
            self.sender.arrived(landing, sem, self.grid)
            total = total + landing[...].astype(F32)
        return total

    def own(self, z):
        s = self.grid.side
        for k in range(s - 1):
            self.sender.arrived(self.from_third.at[k, z], self.sem_third.at[k, z], self.grid)
        total = self.held[z, self.blocks_b[0]].astype(F32)
        for k in range(s - 1):
            total = total + self.from_third[k, z].astype(F32)
        return total

    def add_third(self, d):
        z = self.z(d)
        at = self.held.at[z, self.blocks_b[0]]
        at[...] = self.own(z).astype(BF16)
        self.sender.start(at, self.from_z.at[d - 1], self.sem_z.at[d - 1], self.place.peer("z", d))

    def result(self):
        if self.z_early:
            total = self.z_total(0)
            for k in range(1, self.grid.side):
                self.sender.arrived(self.from_third.at[k - 1, 0], self.sem_third.at[k - 1, 0], self.grid)
                total = total + self.from_third[k - 1, 0].astype(F32)
            return total
        total = self.own(self.grid.z)
        for k in range(self.grid.nz - 1):
            self.sender.arrived(self.from_z.at[k], self.sem_z.at[k], self.grid)
            total = total + self.from_z[k].astype(F32)
        return total

    def add_siblings(self):
        for d in self.z_order():
            self.add_sibling(d)

    def add_seconds(self):
        for d in self.z_order():
            self.add_second(d)

    def add_thirds(self):
        if self.z_early:
            for k in range(1, self.grid.side):
                at = self.held.at[self.grid.z, self.blocks_b[k]]
                at[...] = self.z_total(k).astype(BF16)
                self.sender.start(at, self.from_third.at[k - 1, 0], self.sem_third.at[k - 1, 0], self.peers_b[k])
            return
        for d in self.z_order()[:-1]:
            self.add_third(d)

    @staticmethod
    def sends(grid):
        n, s = grid.nz, grid.side
        return n + n * (s - 1) * s + n * (s - 1) + n - 1

    @staticmethod
    def scratch(grid, stages, width):
        n, s, r = grid.nz, grid.side, grid.rows
        return [
            pltpu.VMEM((stages, n, s * s * r, width), BF16),
            pltpu.VMEM((stages, s - 1, n, s * r, width), BF16),
            pltpu.VMEM((stages, s - 1, n, r, width), BF16),
            pltpu.VMEM((stages, n - 1, r, width), BF16),
            pltpu.SemaphoreType.DMA((stages, n)),
            pltpu.SemaphoreType.DMA((stages, s - 1, n, s)),
            pltpu.SemaphoreType.DMA((stages, s - 1, n)),
            pltpu.SemaphoreType.DMA((stages, n - 1)),
        ]


class SumAll:
    def __init__(self, place, sender, held, landing, sem):
        g = place.grid
        self.grid, self.sender, self.held, self.landing, self.sem = g, sender, held, landing, sem
        self.peers = [[g.sib()]] + [[place.peer(name, d) for d in range(1, place.sizes[name])] for name in ("lo", "hi", "z")]
        self.slots = [sum(len(p) for p in self.peers[:n]) for n in range(4)]

    def send(self, n):
        for k, peer in enumerate(self.peers[n]):
            slot = self.slots[n] + k
            self.sender.start(self.held.at[n], self.landing.at[slot], self.sem.at[slot], peer)

    def add(self, n):
        total = self.held[n]
        for k in range(len(self.peers[n])):
            slot = self.slots[n] + k
            self.sender.arrived(self.landing.at[slot], self.sem.at[slot], self.grid)
            total = total + self.landing[slot]
        self.held[n + 1] = total


def lane_places(grid, width):
    rank = grid.chip(grid.z, grid.hi, grid.lo) * 2 + grid.core
    first = lax.rem(rank * width, D)
    entry = lax.broadcasted_iota(jnp.int32, (128, D), 0)
    lane = lax.broadcasted_iota(jnp.int32, (128, D), 1)
    return jnp.where((lane == first + entry) & (entry < width), 1.0, 0.0).astype(BF16), rank * width // D


SHARES = (4, 2, 2, 4, 4, 10, 10, 12, 16, 12)


class Network:
    FFN, ATTN = 4, 4

    def __init__(self, grid, m, raws, outs, scratch):
        self.grid, self.m, self.raws, self.outs = grid, m, raws, outs
        (self.pre_out, self.pre_in, self.vec_out, self.vec_in, rsem, vsem, self.psem, ssem) = scratch[:8]
        ffn, attn = scratch[8:16], scratch[16:24]
        (self.swap_out, self.swap_in, self.wsem, self.swap_up_out, self.swap_up_in, self.wsem_up, sums, sums_in, sums_sem) = scratch[24:]
        self.sender = Sender(ssem)
        self.place = place = Place(grid)
        r, chips, c = grid.rows, grid.chips, grid.core

        def rows(ref, index):
            return ref.at[pl.ds(pl.multiple_of(index * r, r), r)]

        def spread(g, ref, jj, route, by_chip):
            def at(j, p):
                return rows(ref, p * 4 + j) if by_chip else rows(ref, j * chips + p)
            return Spread(place, self.sender, route, at, lambda j, p: rsem.at[g, j, p], c * 2 + jj, (1 - c) * 2 + jj)

        even, odd = ("z", "lo", "hi"), ("z", "hi", "lo")
        self.attn = [spread(0, m.attn, 0, even, False), spread(0, m.attn, 1, odd, False)]
        self.up = [spread(1, m.up, 0, even, False), spread(1, m.up, 1, odd, False)]
        self.down = [spread(2, m.down, 0, ("lo", "z", "hi"), True), spread(2, m.down, 1, ("hi", "z", "lo"), True)]
        self.vec = Spread(place, self.sender, even, self.vec_at, lambda j, p: vsem.at[j, p], c, 1 - c)

        z_rows = grid.side * grid.side * r

        def ffn_source(ref, quarter):
            def source(core, z):
                at = (quarter(core) * grid.nz + z) * z_rows
                return ref.at[pl.ds(pl.multiple_of(at, z_rows), z_rows)]
            return source

        def attn_source(t):
            def source(core, z):
                at = (t * grid.nz + z) * z_rows
                return m.up.at[pl.ds(pl.multiple_of(at, z_rows), z_rows), pl.ds(pl.multiple_of(core * (D // 2), D // 2), D // 2)]
            return source

        def stage(source, refs, slot, t, z_early=False):
            return Stage(place, self.sender, t, z_early, source, *(x.at[slot] for x in refs[:4]), tuple(x.at[slot] for x in refs[4:]))

        self.r_down = [stage(ffn_source(m.spare, lambda core, t=t: 2 * core + t), ffn, t, t, True) for t in range(2)]
        self.r_up = [stage(ffn_source(m.down, lambda core, t=t: 2 * t + core), ffn, 2 + t, t) for t in range(2)]
        self.r_attn = [stage(attn_source(t), attn, t, t) for t in range(4)]
        self.sums, self.sum_all = sums, SumAll(place, self.sender, sums, sums_in, sums_sem)


    def vec_at(self, j, p):
        base = self.m.x.shape[0]
        half_width = D // 2
        return self.m.spare.at[pl.ds(pl.multiple_of(base + p * 16, 16), 16), pl.ds(pl.multiple_of(j * half_width, half_width), half_width)]

    def mine(self, first, second):
        return jnp.where(self.grid.core == 0, first.astype(F32), second.astype(F32))

    def begin(self):
        grid, c = self.grid, self.grid.core
        greeting = pltpu.get_barrier_semaphore()
        peers = grid.peers()
        for peer in peers:
            pl.semaphore_signal(greeting, inc=1, device_id=peer, device_id_type=MESH)
        query, key, value, out, up, down, small = self.raws
        pairs = [[(query[...], value[...]), (key[...], out[...])],
                 [(up[:, j * D : (j + 1) * D], up[:, (2 + j) * D : (3 + j) * D]) for j in range(2)]]
        for g in range(2):
            for jj in range(2):
                first, second = pairs[g][jj]
                self.pre_out[g, jj] = self.mine(second, first).astype(BF16)
        matrix, _ = lane_places(grid, grid.dev_rows)
        matrix_up, row_up = lane_places(grid, 4 * grid.dev_rows)
        here = mm(small[...], matrix)
        up_row = mm(small[...], matrix_up)[8:9]
        sub = lax.broadcasted_iota(jnp.int32, (16, D), 0)
        placed = jnp.where(sub < 8, here, jnp.where(sub == UB + row_up, jnp.broadcast_to(up_row, (16, D)), 0.0))
        width = D // 2
        self.vec_out[...] = self.mine(placed[:, width:], placed[:, :width]).astype(BF16)
        pl.semaphore_wait(greeting, len(peers))
        for jj in range(2):
            self.sender.start(self.pre_out.at[0, jj], self.pre_in.at[0, jj], self.psem.at[0, jj], grid.sib())
        self.sender.start(self.vec_out, self.vec_in, self.psem.at[2, 0], grid.sib())
        for jj in range(2):
            self.sender.start(self.pre_out.at[1, jj], self.pre_in.at[1, jj], self.psem.at[1, jj], grid.sib())
        chip = self.place.chip({})
        for g, units in enumerate((self.attn, self.up)):
            for jj, unit in enumerate(units):
                self.sender.arrived(self.pre_in.at[g, jj], self.psem.at[g, jj], grid)
                own, other = self.mine(*pairs[g][jj]), self.pre_in[g, jj].astype(F32)
                both = jnp.concatenate([self.mine(own, other), self.mine(other, own)], axis=0)
                unit.at(unit.unit, chip)[...] = both.astype(BF16)
                if g == 0:
                    unit.own(("z",), sibling=False)
            if g == 0:
                self.sender.arrived(self.vec_in, self.psem.at[2, 0], grid)
                total = self.mine(placed[:, :width], placed[:, width:]) + self.vec_in[...].astype(F32)
                self.vec.at(self.vec.unit, chip)[...] = total.astype(BF16)
                self.vec.own()
                for unit in units:
                    unit.own(("lo", "hi"))
        for jj, unit in enumerate(self.down):
            r = grid.rows
            unit.at(unit.unit, chip)[...] = down[jj * r : (jj + 1) * r, :]
            unit.own(unit.route[:1])
        for unit in self.up:
            unit.own(("lo", "hi"))

    def run(self, steps):
        for step in steps:
            step()

    def need_attn(self):
        a, up = self.attn, self.up
        firsts = mix(a[0].firsts(), a[1].firsts(), self.vec.firsts())
        self.run(firsts[:6])
        for unit in up:
            unit.own(("z",), sibling=False)
        self.run(firsts[6:])
        self.run(mix(a[0].seconds(), a[1].seconds(), self.vec.seconds()))
        up_firsts, down_firsts = mix(up[0].firsts(), up[1].firsts()), mix(self.down[0].firsts(), self.down[1].firsts())
        up_seconds, up_thirds = mix(up[0].seconds(), up[1].seconds()), mix(up[0].thirds(), up[1].thirds())
        down_seconds, down_thirds = mix(self.down[0].seconds(), self.down[1].seconds()), mix(self.down[0].thirds(), self.down[1].thirds())
        early = 2 * len(up_firsts) // 3
        self.run(up_firsts[:early])
        for unit in self.down:
            unit.own(("z",), sibling=False)
        self.run(down_firsts)
        for unit in self.down:
            unit.own(unit.route[2:], sibling=False)
        self.run(mix(a[0].thirds(), a[1].thirds(), self.vec.thirds()))
        self.run(up_firsts[early:])
        for unit in a + [self.vec]:
            unit.from_sibling()
        base = self.m.x.shape[0]
        total = self.m.spare[base : base + 16, :].astype(F32)
        for p in range(1, self.grid.chips):
            total = total + self.m.spare[base + p * 16 : base + (p + 1) * 16, :].astype(F32)
        self.m.vec[...] = total
        self.plan = up_seconds + up_thirds + down_seconds + down_thirds
        total = len(self.plan)
        self.shares = [total * k // 100 for k in SHARES]

    def next(self):
        if self.shares:
            for _ in range(self.shares.pop(0)):
                if self.plan:
                    self.plan.pop(0)()

    def during_qkv(self, i):
        self.next()

    def during_attention(self, k):
        self.next()

    def need_up(self):
        while any(step.func.__self__ in self.up for step in self.plan):
            self.plan.pop(0)()
        for unit in self.up:
            unit.from_sibling()

    def during_up(self, j):
        self.next()

    def need_down(self):
        while self.plan:
            self.plan.pop(0)()
        for unit in self.down:
            unit.from_sibling()

    def gathered(self):
        self.sender.finish()
        self.sender.started = Started(len(self.sender.started))


    def ready_down(self):
        for stage in self.r_down:
            stage.to_sibling()

    def during_back(self, j):
        if j < 2:
            self.r_down[j].add_siblings()

    def during_up_grad(self, j):
        if j % 2 == 1:
            self.r_up[j // 2].to_sibling()
        if j == 2:
            self.r_down[0].add_seconds()
        if j == 3:
            self.r_up[0].add_siblings()

    def after_first_back(self):
        self.r_up[1].add_siblings()
        self.r_down[1].add_seconds()

    def after_out(self):
        self.r_attn[0].to_sibling()
        self.r_up[0].add_seconds()

    def after_chunk(self, k, middle):
        attn, up, down = self.r_attn, self.r_up, self.r_down
        if middle == 1:
            attn[k].add_siblings()
        if middle == 2:
            attn[1 + k].to_sibling()
        if (k, middle) == (0, 1):
            down[0].add_thirds()
        if (k, middle) == (1, 0):
            up[1].add_seconds()
            up[0].add_thirds()
        if (k, middle) == (1, 1):
            down[1].add_thirds()
            attn[0].add_seconds()
        if (k, middle) == (2, 0):
            up[1].add_thirds()
        if (k, middle) == (2, 1):
            attn[1].add_seconds()
            attn[0].add_thirds()

    def ready_vec(self):
        self.sums[0] = self.m.vec_grad[...]
        self.sum_all.send(0)

    def during_finish(self, i):
        attn = self.r_attn
        if i == 0:
            self.sum_all.add(0)
            self.sum_all.send(1)
        if i == 1:
            attn[3].add_siblings()
            attn[2].add_seconds()
        if i == 2:
            attn[1].add_thirds()
            self.down_result()
        if i == 3:
            self.sum_all.add(1)
            self.sum_all.send(2)

    def end(self):
        attn = self.r_attn
        attn[3].add_seconds()
        attn[2].add_thirds()
        self.up_result()
        self.sum_all.add(2)
        self.sum_all.send(3)
        self.attn_result(0)
        attn[3].add_thirds()
        self.attn_result(1)
        self.sum_all.add(3)
        self.small_result()
        self.attn_result(2)
        self.attn_result(3)
        self.finish_results()
        self.sender.finish()

    def down_result(self):
        r, down = self.grid.rows, self.outs[5]
        for t in range(2):
            down[t * r : (t + 1) * r, :] = self.r_down[t].result()

    def trade(self, total, out, landing, sem):
        c, dr = self.grid.core, self.grid.dev_rows
        top, bottom = total[:dr], total[dr:]
        out[...] = jnp.where(c == 0, bottom, top)
        self.sender.start(out, landing, sem, self.grid.sib())
        return jnp.where(c == 0, top, bottom)

    def by_core(self, put, own, landing=None):
        for core in range(2):
            @pl.when(self.grid.core == core)
            def _(core=core):
                put(core, own)

    def put_up(self, t):
        def put(core, value):
            at = (2 * t + core) * D
            self.outs[4][:, at : at + D] = value
        return put

    def put_attn(self, t):
        query, key, value, out = self.outs[:4]

        def put(core, v):
            if t == 0:
                out[:, core * (D // 2) : (core + 1) * (D // 2)] = v
                return
            at, wide = (t - 1) * (D // 3), D // 3
            if core == 0:
                query[:, at : at + wide] = v[:, :wide]
                key[:, at : at + wide // 2] = v[:, wide:]
            else:
                key[:, at + wide // 2 : at + wide] = v[:, : wide // 2]
                value[:, at : at + wide] = v[:, wide // 2 :]
        return put

    def up_result(self):
        for t in range(2):
            mine = self.trade(self.r_up[t].result(), self.swap_up_out.at[t], self.swap_up_in.at[t], self.wsem_up.at[t])
            self.by_core(self.put_up(t), mine)

    def attn_result(self, t):
        mine = self.trade(self.r_attn[t].result(), self.swap_out.at[t], self.swap_in.at[t], self.wsem.at[t])
        self.by_core(self.put_attn(t), mine)

    def finish_results(self):
        for n, put, landing, sems in ((2, self.put_up, self.swap_up_in, self.wsem_up), (4, self.put_attn, self.swap_in, self.wsem)):
            for t in range(n):
                self.sender.arrived(landing.at[t], sems.at[t], self.grid)
                for core in range(2):
                    @pl.when(self.grid.core == 1 - core)
                    def _(core=core):
                        put(t)(core, landing[t])

    def small_result(self):
        x = self.sums[4]
        high = x.astype(BF16)
        rest = x - high.astype(F32)
        middle = rest.astype(BF16)
        low = (rest - middle.astype(F32)).astype(BF16)
        matrix, _ = lane_places(self.grid, self.grid.dev_rows)
        matrix_up, row_up = lane_places(self.grid, 4 * self.grid.dev_rows)
        narrow, wide = (mm_nt(high, k) + mm_nt(middle, k) + mm_nt(low, k) for k in (matrix, matrix_up))
        sub = lax.broadcasted_iota(jnp.int32, (16, 128), 0)
        up = jnp.sum(jnp.where(sub == UB + row_up, wide, 0.0), axis=0, keepdims=True)
        self.outs[6][...] = jnp.where(sub < 8, narrow, jnp.broadcast_to(up, (16, 128)))

    @staticmethod
    def sends(grid):
        return 5 + 7 * Spread.sends(grid) + 8 * Stage.sends(grid) + 6 + peer_count(grid)

    @staticmethod
    def scratch(grid):
        chips, dr = grid.chips, grid.dev_rows
        dma = pltpu.SemaphoreType.DMA
        return [
            pltpu.VMEM((2, 2, dr, D), BF16),
            pltpu.VMEM((2, 2, dr, D), BF16),
            pltpu.VMEM((16, D // 2), BF16),
            pltpu.VMEM((16, D // 2), BF16),
            dma((3, 4, chips)),
            dma((2, chips)),
            dma((3, 2)),
            dma((Network.sends(grid),)),
        ] + Stage.scratch(grid, 4, D) + Stage.scratch(grid, 4, D // 2) + [
            pltpu.VMEM((4, dr, D // 2), F32),
            pltpu.VMEM((4, dr, D // 2), F32),
            dma((4,)),
            pltpu.VMEM((2, dr, D), F32),
            pltpu.VMEM((2, dr, D), F32),
            dma((2,)),
            pltpu.VMEM((5, 16, D), F32),
            pltpu.VMEM((peer_count(grid), 16, D), F32),
            dma((peer_count(grid),)),
        ]


class Started(list):
    def __init__(self, offset):
        super().__init__()
        self.offset = offset

    def __len__(self):
        return self.offset + super().__len__()


def fused_kernel(grid, memory, bucket, length, tokens_in, out_grad_in, pool_grad, *refs):
    raws, (layer_out, pools, token_grad), outs, (keep_qkv, keep_norm), scratch = refs[:7], refs[7:10], refs[10:17], refs[17:19], refs[19:]
    grid.place()
    m = Memory(scratch[:memory])
    net = Network(grid, m, raws, outs, scratch[memory:])
    layer_steps(m, net, bucket, length, tokens_in, out_grad_in, pool_grad, layer_out, pools, token_grad, keep_qkv, keep_norm, grid.rows)


def layer_fused(grid, bucket, length, tokens, out_grad, pool_grad, query, key, value, out, up, down, small):
    count, dr = tokens.shape[0], grid.dev_rows
    v, any_spec, smem = pl.BlockSpec(memory_space=pltpu.VMEM), pl.BlockSpec(memory_space=pl.ANY), pl.BlockSpec(memory_space=pltpu.SMEM)
    s = jax.ShapeDtypeStruct
    memory = Memory.shapes(count)
    return pl.pallas_call(
        functools.partial(fused_kernel, grid, len(memory)),
        out_shape=[s((count, D), BF16), s(pool_grad.shape, F32), s((count, D), F32)] + [s((dr, D), F32)] * 4
        + [s((dr, 4 * D), F32), s((4 * dr, D), F32), s((16, 128), F32), s((3, count, D), BF16), s((count, D), F32)],
        in_specs=[smem, smem, any_spec, any_spec] + [v] * 8,
        out_specs=[any_spec, v, any_spec] + [v] * 7 + [any_spec, any_spec],
        scratch_shapes=memory + Network.scratch(grid),
        compiler_params=pltpu.CompilerParams(collective_id=2, has_side_effects=True, vmem_limit_bytes=255 * 2**18),
    )(bucket, length, tokens, out_grad, pool_grad, query, key, value, out, up, down, small)[:10]
def hand_out_kernel(parts, *refs):
    count = len(parts)
    srcs, small, dsts, vectors = refs[:count], refs[count], refs[count + 1 : 2 * count + 1], refs[2 * count + 1 : 2 * count + 10]
    held, sem_in, sem_out = refs[2 * count + 10 : -2], refs[-2], refs[-1]
    loads, stores = [], []
    for src, dst, kept, n in zip(srcs, dsts, held, parts):
        rows = src.shape[0] // n
        for k in range(n):
            at = slice(k * rows, (k + 1) * rows)
            loads.append(pltpu.make_async_copy(src.at[at], kept.at[at], sem_in.at[len(loads)]))
            stores.append(pltpu.make_async_copy(kept.at[at], dst.at[at], sem_out.at[len(stores)]))
    for c in loads:
        c.start()
    for k, out in enumerate(vectors):
        out[...] = small[k, : out.shape[0]]
    for load, store in zip(loads, stores):
        load.wait()
        store.start()
    for c in stores:
        c.wait()


def hand_out(grid, results):
    arrays, small = results[:9], results[9]
    parts = [4 if x.shape[0] % 64 == 0 and x.shape[1] == D else 1 for x in arrays]
    dr = grid.dev_rows
    v, any_spec = pl.BlockSpec(memory_space=pltpu.VMEM), pl.BlockSpec(memory_space=pl.ANY)
    lengths = [dr] * 8 + [4 * dr]
    out = pl.pallas_call(
        functools.partial(hand_out_kernel, parts),
        out_shape=[jax.ShapeDtypeStruct(x.shape, x.dtype) for x in arrays] + [jax.ShapeDtypeStruct((k,), F32) for k in lengths],
        in_specs=[any_spec] * 9 + [v],
        out_specs=[any_spec] * 9 + [v] * 9,
        scratch_shapes=[pltpu.VMEM(x.shape, x.dtype) for x in arrays] + [pltpu.SemaphoreType.DMA((sum(parts),))] * 2,
        compiler_params=pltpu.CompilerParams(vmem_limit_bytes=60 * 2**20),
    )(*arrays, small)
    layer_out, pools, token_grad, g_query, g_key, g_value, g_out, g_up, g_down = out[:9]
    vec = out[9:]
    return (
        layer_out, pools, token_grad, g_query, vec[QB], g_key, g_value, vec[VB], g_out, vec[OB], vec[G1], vec[S1],
        g_up, vec[UB], g_down, vec[DB], vec[G2], vec[S2],
    )


def body(
    grid,
    tokens,
    block_bucket,
    lengths,
    query_weight,
    query_bias,
    key_weight,
    value_weight,
    value_bias,
    out_weight,
    out_bias,
    first_gain,
    first_shift,
    up_weight,
    up_bias,
    down_weight,
    down_bias,
    second_gain,
    second_shift,
    out_grad,
    pool_grad,
):
    rank = lax.axis_index("dp") * lax.axis_size("fsdp") + lax.axis_index("fsdp")
    dr, n, s, pad, r = grid.dev_rows, grid.nz, grid.side, grid.pad, grid.rows
    if pad == r:
        vectors = (query_bias, value_bias, out_bias, first_gain, first_shift, down_bias, second_gain, second_shift)
        small = jnp.concatenate([
            jnp.pad(jnp.stack(vectors), ((0, 0), (0, 128 - dr))),
            jnp.pad(up_bias[None], ((0, 7), (0, 128 - 4 * dr)))])
        results = layer_fused(
            grid, block_bucket, lengths, tokens, out_grad, pool_grad, query_weight, key_weight, value_weight, out_weight,
            up_weight, down_weight, small)
        return hand_out(grid, results)
    raw_attn = jnp.stack([query_weight, key_weight, value_weight, out_weight])
    raw_up = up_weight.reshape(dr, 4, D).transpose(1, 0, 2)
    raw_down = down_weight.reshape(4, dr, D)
    small = jnp.stack([query_bias, value_bias, out_bias, first_gain, first_shift, down_bias, second_gain, second_shift])
    small = lax.dynamic_update_slice(jnp.zeros((16, D), BF16), small, (0, rank * dr))
    wide = lax.dynamic_update_slice(jnp.zeros((16 * D,), BF16), up_bias, (rank * 4 * dr,)).reshape(16, D)
    raw_vec = jnp.stack([small, wide])
    w_attn, w_up, w_down, w_vec = gather_all(grid, raw_attn, raw_up, raw_down, raw_vec)
    w_attn, w_up, w_down = (w[:, :, :r].reshape(4 * D, D) for w in (w_attn, w_up, w_down))
    vec = jnp.sum(w_vec.astype(F32), axis=1)
    vec = jnp.concatenate([vec[0, :8], vec[1, :8]])
    layer_out, pools, token_grad, g_attn, g_up, g_down, g_vec = layer_local(
        block_bucket, lengths, tokens, out_grad, pool_grad, vec, w_attn, w_up, w_down)
    panels = g_attn[D:].reshape(3, D, 3, D // 3).transpose(2, 1, 0, 3).reshape(3 * D, D)
    g_attn = jnp.concatenate([panels, g_attn[:D]])

    def blocks(grad):
        return jnp.pad(grad.reshape(-1, r, D), ((0, 0), (0, pad - r), (0, 0)))

    g_attn, g_up = (blocks(g).reshape(4, n, s, s, pad, D) for g in (g_attn, g_up))
    g_down = blocks(g_down).reshape(n, s, s, 4, pad, D)
    o_attn, o_up, o_down, o_vec = reduce_all(grid, g_attn, g_up, g_down, g_vec)
    small = lax.dynamic_slice(o_vec, (0, rank * dr), (8, dr))
    wide = lax.dynamic_slice(o_vec[8:12].reshape(4 * D), (rank * 4 * dr,), (4 * dr,))
    return (
        layer_out,
        pools,
        token_grad,
        o_attn[0],
        small[QB],
        o_attn[1],
        o_attn[2],
        small[VB],
        o_attn[3],
        small[OB],
        small[G1],
        small[S1],
        o_up.transpose(1, 0, 2).reshape(dr, 4 * D),
        wide,
        o_down.reshape(4 * dr, D),
        small[DB],
        small[G2],
        small[S2],
    )


def solution(mesh):
    whole, line = P(("dp", "fsdp"), None), P(("dp", "fsdp"))
    grid = Grid(mesh.shape["dp"], mesh.shape["fsdp"])
    return jax.shard_map(
        functools.partial(body, grid),
        mesh=mesh,
        in_specs=(
            whole, line, line, whole, line, whole, whole, line, whole, line,
            line, line, whole, line, whole, line, line, line, whole, whole,
        ),
        out_specs=(
            whole, whole, whole, whole, line, whole, whole, line, whole, line,
            line, line, whole, line, whole, line, line, line,
        ),
        check_vma=False,
    )
```
